32 devices in a mesh: expert: 16 (over z, x, core), half: 2 (over y).
Axes of the slice: x: 2, y: 2, z: 4, core: 2. Of those that a mesh axis runs over, the one named last changes fastest.
Arguments:
- tokens: bfloat16 [512, 4096], P('expert'), may hold values from -6 to 6
- target: bfloat16 [512, 4096], P('expert', 'half'), may hold values from -3 to 3
- routes: int32 [512, 8], P('expert'), may hold values from 0 to 15, all different within a row; in each aligned block of 32 rows (0 to 31, 32 to 63, ...) at most 32 rows name the same one
- route_scores: float32 [512, 8], P('expert'), may hold values from 0.1 to 1
- in_codes: bfloat16 [16, 2, 4096, 1536], P('expert', None, None, 'half'), may hold values from 0 to 255, as said below
- in_low: float32 [16, 2, 32, 1536], P('expert', None, None, 'half'), may hold values from -0.0390625 to -0.015625
- in_high: float32 [16, 2, 32, 1536], P('expert', None, None, 'half'), may hold values from 0.015625 to 0.0390625
- down_codes: bfloat16 [16, 1536, 4096], P('expert', None, 'half'), may hold values from 0 to 255, as said below
- down_low: float32 [16, 12, 4096], P('expert', None, 'half'), may hold values from -0.063788794 to -0.02551552
- down_high: float32 [16, 12, 4096], P('expert', None, 'half'), may hold values from 0.02551552 to 0.063788794
Outputs:
- grad_tokens: bfloat16 [512, 4096], P('expert', 'half')
- in_range_grad: float32 [16, 4, 32, 1536], P('expert', None, None, 'half')
- down_range_grad: float32 [16, 2, 12, 4096], P('expert', None, None, 'half')
The draws below stay inside these ranges and needn't reach their ends.
Inputs may be any that keep to these rules, and one draw needn't show every extreme that they name: `routes`: each row names 8 different experts. In each aligned block of 32 rows (the tokens of one index of expert) no expert is named by more than 32 rows, a bound that some block reaches. `in_codes`: whole numbers. `down_codes`: whole numbers.
All inputs are finite; a program needn't handle non-finite values.
Results may differ from the reference program's by a relative error of at most 0.013.
Values may be sent and summed in bfloat16 or wider, within the bound.
No kernel may reach another device: no remote copies, remote signals or barrier semaphores. Data moves between devices by JAX's collectives and lax.ppermute only.
A program may use at most 128 MiB of HBM per device.

```python
import math
import jax
import jax.numpy as jnp
import numpy as np
from jax import lax

D = 4096
FF = 1536
TOP = 8
TOK_DEV = 32
EXPERTS = 16
CAP = 32
TOKENS = 512
GD = 32
GF = 12
N_HALF = 2


def draw_in_codes(key, part):
    return jax.random.randint(key, (EXPERTS, 2, D, FF), 0, 256).astype(jnp.float32).astype(jnp.bfloat16)


def draw_down_codes(key, part):
    return jax.random.randint(key, (EXPERTS, FF, D), 0, 256).astype(jnp.float32).astype(jnp.bfloat16)


def block_levels(key, extent, split, smallest, high):
    level, own = 1.0, jax.random.fold_in(key, 6)
    for dim, shards_of in split:
        draws = jnp.exp(jax.random.uniform(jax.random.fold_in(own, dim), (shards_of,), jnp.float32, smallest / len(split), high / len(split)))
        level = level * jnp.repeat(draws, extent[dim] // shards_of).reshape([-1 if axis == dim else 1 for axis in range(len(extent))])
    return level


def assign_block(own_key, own, number, rows, number_of, top, limit, lean):
    order = jax.random.permutation(own_key, number_of)
    packed, common = shares(number_of, rows * top, limit, lean, True), shares(number_of, rows * top, limit, lean, False)
    places = jnp.arange(number_of)

    def named(lengths, offset_by):
        used = int((lengths > 0).sum())
        fixed = max(1, used // 4)
        passed = fixed + (places - fixed + offset_by * (used - fixed)) % max(1, number_of - fixed)
        return jnp.zeros((number_of,), jnp.int32).at[order[jnp.where(places < fixed, places, passed)]].set(jnp.asarray(lengths, jnp.int32))

    lengths = jnp.where(number % 4 == 0, named(packed, number // 4), named(common, number - number // 4 - 1))
    mixed = jax.random.permutation(jax.random.fold_in(own, 3), number_of)
    source_of, sink = mixed[0:number_of // 2 * 2:2], mixed[1:number_of // 2 * 2:2]
    room = jnp.minimum(lengths[source_of] - 1, limit - lengths[sink]) // 2
    room = jnp.where((source_of == order[0]) | (sink == order[0]) | (lengths[sink] == 0), 0, jnp.maximum(room, 0))
    passed = jax.random.randint(jax.random.fold_in(own, 4), (number_of // 2,), 0, 1 << 20) % (room + 1)
    lengths = lengths.at[source_of].add(-passed).at[sink].add(passed)
    items = jnp.searchsorted(jnp.cumsum(lengths), jnp.arange(rows * top), side="right").astype(jnp.int32)
    listing = items.reshape(top, rows).T
    listing = listing[jax.random.permutation(jax.random.fold_in(own, 1), rows)]
    offset_by = jax.random.randint(jax.random.fold_in(own, 2), (rows, 1), 0, top)
    return jnp.take_along_axis(listing, (jnp.arange(top)[None, :] + offset_by) % top, axis=1)


def shares(number_of, total, limit, lean, full):
    portions = [(1 << 20) // math.isqrt(standing ** lean) + 1 for standing in range(1, number_of + 1)]
    largest = limit if full else min(limit, max(-(-total // number_of), total * portions[0] // sum(portions)))
    least = 1 if total - largest >= number_of - 1 else 0
    given, rest = [largest] + [least] * (number_of - 1), total - largest - least * (number_of - 1)
    while rest > 0:
        candidates = [i for i in range(1, number_of) if given[i] < largest] or [i for i in range(1, number_of) if given[i] < limit]
        pool, left = sum([portions[i] for i in candidates]), rest
        for i in candidates:
            extra = min(limit - given[i], max(1, left * portions[i] // pool), rest)
            given[i] = given[i] + extra
            rest = rest - extra
    return np.array(given)


def centred(stream_key, dims, scale, reach, shards=(), held_as=jnp.bfloat16):
    gain = block_levels(stream_key, dims, shards, -0.22, 0.18) if shards else 1.0
    array = jax.random.normal(stream_key, dims, jnp.float32) * scale * gain
    return jnp.minimum(jnp.maximum(array, -reach), reach).astype(held_as)


def setup_inputs(seed: int = 0) -> dict:
    streams_of = jax.random.split(jax.random.key(seed), 11)
    tokens = centred(streams_of[0], (TOKENS, D), 1.0, 6.0, ((0, 16),))
    target = centred(streams_of[1], (TOKENS, D), 0.5, 3.0, ((0, 16), (1, 2)))
    routes_keys = jax.random.split(jax.random.fold_in(streams_of[2], 1), TOKENS // TOK_DEV)
    routes_turns = jax.random.permutation(jax.random.fold_in(streams_of[2], 3), TOKENS // TOK_DEV)
    routes = jax.vmap(lambda own, number: assign_block(jax.random.fold_in(streams_of[2], 2), own, number, TOK_DEV, EXPERTS, TOP, CAP, 2))(routes_keys, routes_turns).reshape((TOKENS, TOP))
    route_scores = jnp.clip(jnp.exp(math.log(1.0) - 2.3025851 * jax.random.uniform(streams_of[3], (TOKENS, TOP), jnp.float32) ** block_levels(streams_of[3], (TOKENS, TOP), ((0, 16),), -0.2, 0.2)), 0.1, 1.0)
    in_codes = draw_in_codes(jax.random.fold_in(streams_of[10], 71), 0)
    in_low = jnp.clip(-0.0390625 + 0.0234375 * jax.random.uniform(streams_of[5], (EXPERTS, 2, GD, FF), jnp.float32) ** block_levels(streams_of[5], (EXPERTS, 2, GD, FF), ((0, 16), (3, 2)), -0.2, 0.2), -0.0390625, -0.015625)
    in_high = jnp.clip(0.015625 + 0.0234375 * jax.random.uniform(streams_of[6], (EXPERTS, 2, GD, FF), jnp.float32) ** block_levels(streams_of[6], (EXPERTS, 2, GD, FF), ((0, 16), (3, 2)), -0.2, 0.2), 0.015625, 0.0390625)
    down_codes = draw_down_codes(jax.random.fold_in(streams_of[10], 71), 0)
    down_low = jnp.clip(-0.063788794 + 0.038273275 * jax.random.uniform(streams_of[8], (EXPERTS, GF, D), jnp.float32) ** block_levels(streams_of[8], (EXPERTS, GF, D), ((0, 16), (2, 2)), -0.2, 0.2), -0.063788794, -0.02551552)
    down_high = jnp.clip(0.02551552 + 0.038273275 * jax.random.uniform(streams_of[9], (EXPERTS, GF, D), jnp.float32) ** block_levels(streams_of[9], (EXPERTS, GF, D), ((0, 16), (2, 2)), -0.2, 0.2), 0.02551552, 0.063788794)
    return {"tokens": tokens, "target": target, "routes": routes, "route_scores": route_scores, "in_codes": in_codes, "in_low": in_low, "in_high": in_high, "down_codes": down_codes, "down_low": down_low, "down_high": down_high}


def route_tables(route_block, experts, capacity):
    flat_ids = route_block.reshape(-1).astype(jnp.int32)
    pair_count = flat_ids.shape[0]
    onehot = (flat_ids[:, None] == jnp.arange(experts, dtype=jnp.int32)[None, :]).astype(jnp.int32)
    before = (jnp.cumsum(onehot, axis=0) - onehot).astype(jnp.int32)
    slot_rank = jnp.sum(before * onehot, axis=1).astype(jnp.int32)
    dest_slot = (flat_ids * capacity + slot_rank).astype(jnp.int32)
    matches = dest_slot[None, :] == jnp.arange(experts * capacity, dtype=jnp.int32)[:, None]
    is_valid = jnp.any(matches, axis=1)
    source = jnp.sum(jnp.where(matches, jnp.arange(pair_count, dtype=jnp.int32)[None, :], 0), axis=1).astype(jnp.int32)
    return dest_slot, source, is_valid


def dequant(code_vals, low_edge, high_edge):
    groups = low_edge.shape[0]
    scaled = code_vals.astype(jnp.float32).reshape(groups, -1, code_vals.shape[-1]) / 255.0
    weight = low_edge[:, None, :] + (high_edge - low_edge)[:, None, :] * scaled
    return weight.reshape(code_vals.shape).astype(jnp.bfloat16)


def range_grads(grad_weight, code_vals, groups):
    shaped = grad_weight.reshape(groups, -1, grad_weight.shape[-1])
    scaled = code_vals.astype(jnp.float32).reshape(groups, -1, code_vals.shape[-1]) / 255.0
    low_grad = jnp.sum(shaped * (1.0 - scaled), axis=1)
    high_grad = jnp.sum(shaped * scaled, axis=1)
    return low_grad, high_grad


def contract_rows(left, right):
    return lax.dot_general(left, right, (((0,), (0,)), ((), ())), preferred_element_type=jnp.float32)


def contract_cols(left, right):
    return lax.dot_general(left, right, (((1,), (1,)), ((), ())), preferred_element_type=jnp.float32)


def reference(tokens, target, routes, route_scores, in_codes, in_low, in_high, down_codes, down_low, down_high):
    experts = in_codes.shape[0]
    sources = routes.shape[0] // TOK_DEV
    pairs = TOK_DEV * TOP
    blocks = routes.reshape(sources, TOK_DEV, TOP).astype(jnp.int32)
    dest_slot, source, is_valid = jax.vmap(lambda block_ids: route_tables(block_ids, experts, CAP))(blocks)
    weights = route_scores / jnp.sum(route_scores, axis=1, keepdims=True)
    base = jnp.arange(sources, dtype=jnp.int32)[:, None]
    token_index = (base * TOK_DEV + source // TOP).astype(jnp.int32)
    pair_index = (base * pairs + source).astype(jnp.int32)

    def by_expert(table):
        return table.reshape(sources, experts, CAP).transpose(1, 0, 2).reshape(experts, sources * CAP)

    token_index = by_expert(token_index)
    pair_index = by_expert(pair_index)
    row_live = by_expert(is_valid)

    def expert_forward(expert_item):
        code_vals, low_edge, high_edge, down_vals, down_low_edge, down_high_edge, row_index, live_rows = expert_item
        w_gate = dequant(code_vals[0], low_edge[0], high_edge[0])
        w_up = dequant(code_vals[1], low_edge[1], high_edge[1])
        w_down = dequant(down_vals, down_low_edge, down_high_edge)
        expert_rows = jnp.where(live_rows[:, None], tokens[row_index], jnp.zeros((), tokens.dtype))
        gate_pre = jnp.dot(expert_rows, w_gate, preferred_element_type=jnp.float32)
        up_pre = jnp.dot(expert_rows, w_up, preferred_element_type=jnp.float32)
        sigmoid_gate = jax.nn.sigmoid(gate_pre)
        hidden = (gate_pre * sigmoid_gate * up_pre).astype(jnp.bfloat16)
        return jnp.dot(hidden, w_down, preferred_element_type=jnp.float32).astype(jnp.bfloat16)

    outputs = lax.map(expert_forward, (in_codes, in_low, in_high, down_codes, down_low, down_high, token_index, row_live))
    slot_rank = (dest_slot % CAP).reshape(sources, TOK_DEV, TOP).astype(jnp.int32)
    source_ids = jnp.broadcast_to(base[:, :, None], (sources, TOK_DEV, TOP))
    picked = outputs.reshape(experts, sources, CAP, -1)[blocks, source_ids, slot_rank]
    picked = picked.reshape(sources * TOK_DEV, TOP, -1).astype(jnp.float32)
    mixed_out = jnp.sum(weights[:, :, None] * picked, axis=1)
    recon_error = mixed_out - target.astype(jnp.float32)
    error_grads = (weights[:, :, None] * recon_error[:, None, :]).astype(jnp.bfloat16).reshape(sources * pairs, -1)

    def expert_backward(expert_item):
        code_vals, low_edge, high_edge, down_vals, down_low_edge, down_high_edge, row_index, err_index, live_rows = expert_item
        w_gate = dequant(code_vals[0], low_edge[0], high_edge[0])
        w_up = dequant(code_vals[1], low_edge[1], high_edge[1])
        w_down = dequant(down_vals, down_low_edge, down_high_edge)
        expert_rows = jnp.where(live_rows[:, None], tokens[row_index], jnp.zeros((), tokens.dtype))
        grad_in = jnp.where(live_rows[:, None], error_grads[err_index], jnp.zeros((), error_grads.dtype))
        gate_pre = jnp.dot(expert_rows, w_gate, preferred_element_type=jnp.float32)
        up_pre = jnp.dot(expert_rows, w_up, preferred_element_type=jnp.float32)
        sigmoid_gate = jax.nn.sigmoid(gate_pre)
        gate_act = gate_pre * sigmoid_gate
        hidden = (gate_act * up_pre).astype(jnp.bfloat16)
        grad_hidden = contract_cols(grad_in, w_down)
        grad_gate = (grad_hidden * up_pre * sigmoid_gate * (1.0 + gate_pre * (1.0 - sigmoid_gate))).astype(jnp.bfloat16)
        grad_up = (grad_hidden * gate_act).astype(jnp.bfloat16)
        gate_low, gate_high = range_grads(contract_rows(expert_rows, grad_gate), code_vals[0], low_edge.shape[1])
        up_low, up_high = range_grads(contract_rows(expert_rows, grad_up), code_vals[1], low_edge.shape[1])
        down_lowg, down_highg = range_grads(contract_rows(hidden, grad_in), down_vals, down_low_edge.shape[0])
        quarter_ff = grad_gate.shape[1] // N_HALF
        row_total = jnp.zeros((grad_gate.shape[0], w_gate.shape[0]), jnp.float32)
        for quarter in range(N_HALF):
            start = quarter * quarter_ff
            stop = start + quarter_ff
            row_part = (contract_cols(grad_gate[:, start:stop], w_gate[:, start:stop]) + contract_cols(grad_up[:, start:stop], w_up[:, start:stop])).astype(jnp.bfloat16)
            row_part = lax.optimization_barrier(row_part)
            row_total = row_total + row_part.astype(jnp.float32)
        grad_rows = row_total.astype(jnp.bfloat16)
        return jnp.stack([gate_low, gate_high, up_low, up_high]), jnp.stack([down_lowg, down_highg]), grad_rows

    in_grad, down_grad, grad_rows = lax.map(expert_backward, (in_codes, in_low, in_high, down_codes, down_low, down_high, token_index, pair_index, row_live))
    grad_picked = grad_rows.reshape(experts, sources, CAP, -1)[blocks, source_ids, slot_rank]
    grad_picked = grad_picked.reshape(sources * TOK_DEV, TOP, -1).astype(jnp.float32)
    grad_tokens = jnp.sum(grad_picked, axis=1).astype(jnp.bfloat16)
    return grad_tokens, in_grad, down_grad
```

```python
import jax
import jax.numpy as jnp
from jax import lax
from jax.sharding import PartitionSpec as P


def swap(array, axis, distance):
    size = lax.axis_size(axis)
    return lax.ppermute(array, axis, [(i, i ^ distance) for i in range(size)])


def gather_rows(block):
    experts = lax.axis_size("expert")
    far = [block] + [swap(block, "expert", 4 * d) for d in range(1, experts // 4)]
    near = [swap(part, "expert", 2) for part in far]
    own = jnp.concatenate([part for pair in zip(far, near) for part in pair], axis=0)
    return own, swap(own, "expert", 1)


def scatter_rows(summed, rows):
    experts = lax.axis_size("expert")
    count = experts // 4
    pieces = summed.reshape(count, 2, rows, summed.shape[-1])
    order = list(range(1, count)) + [0]
    total = jnp.zeros((rows, summed.shape[-1]), jnp.float32)
    for d in order:
        arrived = swap(pieces[d, 1], "expert", 2).astype(jnp.float32)
        both = pieces[d, 0].astype(jnp.float32) + arrived
        if d:
            both = swap(both.astype(jnp.bfloat16), "expert", 4 * d).astype(jnp.float32)
        total = total + both
    return total


def dequant(code_vals, low_edge, high_edge):
    groups = low_edge.shape[0]
    scaled = code_vals.astype(jnp.float32).reshape(groups, -1, code_vals.shape[-1]) / 255.0
    weight = low_edge[:, None, :] + (high_edge - low_edge)[:, None, :] * scaled
    return weight.reshape(code_vals.shape).astype(jnp.bfloat16)


def range_grads(grad_weight, code_vals, groups):
    shaped = grad_weight.reshape(groups, -1, grad_weight.shape[-1])
    scaled = code_vals.astype(jnp.float32).reshape(groups, -1, code_vals.shape[-1]) / 255.0
    low_grad = jnp.sum(shaped * (1.0 - scaled), axis=1)
    high_grad = jnp.sum(shaped * scaled, axis=1)
    return (low_grad, high_grad)


def contract_rows(left, right):
    return lax.dot_general(
        left, right, (((0,), (0,)), ((), ())), preferred_element_type=jnp.float32
    )


def contract_cols(left, right):
    return lax.dot_general(
        left, right, (((1,), (1,)), ((), ())), preferred_element_type=jnp.float32
    )


def dot(left, right):
    return jnp.dot(left, right, preferred_element_type=jnp.float32)


def local(
    tokens, target, routes, route_scores, in_codes, in_low, in_high, down_codes, down_low, down_high
):
    experts = lax.axis_size("expert")
    halves = lax.axis_size("half")
    me = lax.axis_index("expert")
    my_half = lax.axis_index("half")
    rows = tokens.shape[0]
    quarter = target.shape[1]
    hidden_own = in_codes.shape[3]
    width_groups = in_low.shape[2] // halves
    hidden_groups = down_low.shape[1] // halves

    def take(array, axis, size, d):
        return lax.dynamic_slice_in_dim(array, (my_half ^ d) * size, size, axis)

    weights = route_scores / jnp.sum(route_scores, axis=1, keepdims=True)
    names = routes[:, :, None] == jnp.arange(experts, dtype=jnp.int32)[None, None, :]
    table = jnp.sum(jnp.where(names, weights[:, :, None], 0.0), axis=1)
    table_all = lax.all_gather(table, "expert", axis=0, tiled=False)
    column = lax.dynamic_index_in_dim(table_all, me, axis=2, keepdims=False)
    order = [2 * j for j in range(experts // 2)] + [2 * j + 1 for j in range(experts // 2)]
    column = column[me ^ jnp.array(order, dtype=jnp.int32)]
    column = column.reshape(2, -1, 1)

    parts = range(halves)
    mine = jnp.concatenate([take(tokens, 1, quarter, d) for d in parts], axis=1)
    x = gather_rows(mine)

    in_codes_d = [take(in_codes[0], 1, quarter, d) for d in parts]
    in_low_d = [take(in_low[0], 1, width_groups, d) for d in parts]
    in_high_d = [take(in_high[0], 1, width_groups, d) for d in parts]
    w_in_d = [
        jnp.concatenate(
            [dequant(in_codes_d[d][k], in_low_d[d][k], in_high_d[d][k]) for k in (0, 1)], axis=1
        )
        for d in parts
    ]
    w_in = jnp.concatenate(w_in_d, axis=0)
    down_codes_d = [take(down_codes[0], 0, hidden_own, d) for d in parts]
    w_down_d = [
        dequant(
            down_codes_d[d],
            take(down_low[0], 0, hidden_groups, d),
            take(down_high[0], 0, hidden_groups, d),
        )
        for d in parts
    ]

    sides = (0, 1)
    gate, up, sig, act, hidden = [], [], [], [], []
    for s in sides:
        pre = dot(x[s], w_in)
        gate.append(pre[:, :hidden_own])
        up.append(pre[:, hidden_own:])
        sig.append(jax.nn.sigmoid(gate[s]))
        act.append(gate[s] * sig[s])
        own = (act[s] * up[s]).astype(jnp.bfloat16)
        hidden.append([own] + [swap(own, "half", d) for d in parts if d])
    outs = [
        (column[s] * sum(dot(hidden[s][d], w_down_d[d]) for d in parts)).astype(jnp.bfloat16)
        for s in sides
    ]
    mixed = (outs[0].astype(jnp.float32) + swap(outs[1], "expert", 1).astype(jnp.float32)).astype(
        jnp.bfloat16
    )
    recon_error = scatter_rows(mixed, rows) - target.astype(jnp.float32)
    errors = gather_rows(recon_error.astype(jnp.bfloat16))
    grads = [(column[s] * errors[s].astype(jnp.float32)).astype(jnp.bfloat16) for s in sides]

    grad_gate, grad_up, grad_in = [], [], []
    for s in sides:
        arrived = [
            swap(contract_cols(grads[s], w_down_d[d]).astype(jnp.bfloat16), "half", d)
            for d in parts
            if d
        ]
        grad_hidden = contract_cols(grads[s], w_down_d[0])
        for part in arrived:
            grad_hidden = grad_hidden + part.astype(jnp.float32)
        grad_gate.append(
            (grad_hidden * up[s] * sig[s] * (1.0 + gate[s] * (1.0 - sig[s]))).astype(jnp.bfloat16)
        )
        grad_up.append((grad_hidden * act[s]).astype(jnp.bfloat16))
        grad_in.append(jnp.concatenate([grad_gate[s], grad_up[s]], axis=1))

    row_sum = None
    for d in reversed(parts):
        part = [contract_cols(grad_in[s], w_in_d[d]).astype(jnp.bfloat16) for s in sides]
        both = part[0].astype(jnp.float32) + swap(part[1], "expert", 1).astype(jnp.float32)
        if d:
            both = swap(both.astype(jnp.bfloat16), "half", d).astype(jnp.float32)
        row_sum = both if row_sum is None else row_sum + both
    grad_tokens = scatter_rows(row_sum.astype(jnp.bfloat16), rows).astype(jnp.bfloat16)

    x_all = jnp.concatenate(x, axis=0)
    gate_all = jnp.concatenate(grad_gate, axis=0)
    up_all = jnp.concatenate(grad_up, axis=0)
    grads_all = jnp.concatenate(grads, axis=0)
    in_grad = jnp.zeros((4, width_groups * halves, hidden_own), jnp.float32)
    down_grad = jnp.zeros((2, hidden_groups * halves, quarter), jnp.float32)
    for d in parts:
        x_d = x_all[:, d * quarter : (d + 1) * quarter]
        found = []
        for k, g in ((0, gate_all), (1, up_all)):
            found += range_grads(contract_rows(x_d, g), in_codes_d[d][k], width_groups)
        in_grad = lax.dynamic_update_slice_in_dim(
            in_grad, jnp.stack(found), (my_half ^ d) * width_groups, 1
        )
        hidden_d = jnp.concatenate([hidden[s][d] for s in sides], axis=0)
        found = range_grads(contract_rows(hidden_d, grads_all), down_codes_d[d], hidden_groups)
        down_grad = lax.dynamic_update_slice_in_dim(
            down_grad, jnp.stack(found), (my_half ^ d) * hidden_groups, 1
        )
    return (grad_tokens, in_grad[None], down_grad[None])


def solution(mesh):
    placed = (
        P("expert", None),
        P("expert", "half"),
        P("expert", None),
        P("expert", None),
        P("expert", None, None, "half"),
        P("expert", None, None, "half"),
        P("expert", None, None, "half"),
        P("expert", None, "half"),
        P("expert", None, "half"),
        P("expert", None, "half"),
    )
    return jax.shard_map(
        local,
        mesh=mesh,
        in_specs=placed,
        out_specs=(
            P("expert", "half"),
            P("expert", None, None, "half"),
            P("expert", None, None, "half"),
        ),
        check_vma=False,
    )
```

```python
import functools

import jax
import jax.numpy as jnp
from jax import lax
from jax.experimental import pallas as pl
from jax.experimental.pallas import tpu as pltpu
from jax.sharding import PartitionSpec as P

CHUNKS = 2
BF16 = jnp.bfloat16
F32 = jnp.float32
MIB = 1 << 20


def swap(array, axis, distance):
    size = lax.axis_size(axis)
    return lax.ppermute(array, axis, [(i, i ^ distance) for i in range(size)])


def far_distances():
    experts = lax.axis_size("expert")
    distances = []
    distance = experts // 2
    while distance > 1:
        distances.append(distance)
        distance //= 2
    return distances


def gather_rows(block):
    for distance in far_distances():
        block = jnp.concatenate([block, swap(block, "expert", distance)], axis=0)
    return block, swap(block, "expert", 1)


def scatter_rows(first, second):
    total, arrived = first, second
    for distance in reversed(far_distances()):
        half = total.shape[0] // 2
        leave = (total[half:].astype(F32) + arrived[half:].astype(F32)).astype(BF16)
        sent = swap(leave, "expert", distance)
        total = total[:half].astype(F32) + arrived[:half].astype(F32)
        arrived = sent
    return total.astype(F32) + arrived.astype(F32)


def dot(left, right):
    return jnp.dot(left, right, preferred_element_type=F32)


def dot_cols(left, right):
    return lax.dot_general(left, right, (((1,), (1,)), ((), ())), preferred_element_type=F32)


def dot_rows(left, right):
    return lax.dot_general(left, right, (((0,), (0,)), ((), ())), preferred_element_type=F32)


def cost(flops, bytes_accessed):
    return pl.CostEstimate(flops=int(flops), bytes_accessed=int(bytes_accessed), transcendentals=0)


def params(mib):
    return pltpu.CompilerParams(vmem_limit_bytes=mib * MIB)


def moved(step, blocks, place):
    return ((step // blocks) ^ place[1]) * blocks + step % blocks


def call(kernel, grid, ins, outs, place, scratch=(), mib=32, flops=0):
    total = sum(a.size * a.dtype.itemsize for a, _, _ in ins)
    for shape, kind, _, _ in outs:
        count = 1
        for extent in shape:
            count *= extent
        total += count * jnp.dtype(kind).itemsize
    spec = pltpu.PrefetchScalarGridSpec(
        num_scalar_prefetch=1,
        grid=grid,
        in_specs=[pl.BlockSpec(block, index) for _, block, index in ins],
        out_specs=[pl.BlockSpec(block, index) for _, _, block, index in outs],
        scratch_shapes=list(scratch),
    )
    return pl.pallas_call(
        kernel,
        grid_spec=spec,
        out_shape=[jax.ShapeDtypeStruct(shape, kind) for shape, kind, _, _ in outs],
        compiler_params=params(mib),
        cost_estimate=cost(flops, total),
    )(place, *[a for a, _, _ in ins])


def whole2(*_):
    return (0, 0)


def whole3(*_):
    return (0, 0, 0)


def whole4(*_):
    return (0, 0, 0, 0)


def dequant_in(place, codes, low, high, halves):
    _, _, width, hidden = codes.shape
    groups = low.shape[2]
    size = width // groups
    per = max(1, 512 // size)
    rows = per * size
    blocks = width // halves // rows

    def kernel(place_ref, code_ref, low_ref, high_ref, out_ref):
        base = moved(pl.program_id(0), blocks, place_ref) * per
        for k in range(2):
            for g in range(per):
                bottom = low_ref[0, k, pl.ds(base + g, 1), :]
                scale = (high_ref[0, k, pl.ds(base + g, 1), :] - bottom) * (1.0 / 255.0)
                vals = code_ref[0, k, g * size : (g + 1) * size, :].astype(F32)
                out_ref[g * size : (g + 1) * size, k * hidden : (k + 1) * hidden] = (
                    bottom + scale * vals
                ).astype(BF16)

    return call(
        kernel,
        (width // rows,),
        [
            (codes, (1, 2, rows, hidden), lambda i, p: (0, 0, moved(i, blocks, p), 0)),
            (low, low.shape, whole4),
            (high, high.shape, whole4),
        ],
        [((width, 2 * hidden), BF16, (rows, 2 * hidden), lambda i, p: (i, 0))],
        place,
    )[0]


def hidden_rows(total_groups, size, halves):
    per = total_groups // halves
    while per > 3:
        per = next(f for f in range(2, per + 1) if per % f == 0) and per // next(
            f for f in range(2, per + 1) if per % f == 0
        )
    return per, per * size


def dequant_down(place, codes, low, high, halves):
    _, height, quarter = codes.shape
    groups = low.shape[1]
    size = height // groups
    per, rows = hidden_rows(groups, size, halves)
    blocks = height // halves // rows

    def kernel(place_ref, code_ref, low_ref, high_ref, out_ref):
        base = moved(pl.program_id(0), blocks, place_ref) * per
        for g in range(per):
            bottom = low_ref[0, pl.ds(base + g, 1), :]
            scale = (high_ref[0, pl.ds(base + g, 1), :] - bottom) * (1.0 / 255.0)
            vals = code_ref[0, g * size : (g + 1) * size, :].astype(F32)
            out_ref[g * size : (g + 1) * size, :] = (bottom + scale * vals).astype(BF16)

    return call(
        kernel,
        (height // rows,),
        [
            (codes, (1, rows, quarter), lambda i, p: (0, moved(i, blocks, p), 0)),
            (low, low.shape, whole3),
            (high, high.shape, whole3),
        ],
        [((height, quarter), BF16, (rows, quarter), lambda i, p: (i, 0))],
        place,
    )[0]


def forward_in(place, x_own, x_other, w_in):
    rows = x_own.shape[0]
    width, both = w_in.shape
    hidden = both // 2
    depth = min(512, width)
    steps = width // depth

    def kernel(place_ref, own_ref, other_ref, w_ref, hidden_ref, slope_ref, act_ref, acc_ref):
        step = pl.program_id(0)
        x = jnp.concatenate([own_ref[...], other_ref[...]], axis=0)
        part = dot(x, w_ref[...])

        @pl.when(step == 0)
        def _():
            acc_ref[...] = part

        @pl.when(step > 0)
        def _():
            acc_ref[...] += part

        @pl.when(step == steps - 1)
        def _():
            gate = acc_ref[:, :hidden]
            up = acc_ref[:, hidden:]
            sig = 1.0 / (1.0 + jnp.exp(-gate))
            act = gate * sig
            hidden_ref[...] = (act * up).astype(BF16)
            slope_ref[...] = up * sig * (1.0 + gate * (1.0 - sig))
            act_ref[...] = act

    shape = (2 * rows, hidden)
    return call(
        kernel,
        (steps,),
        [
            (x_own, (rows, depth), lambda i, p: (0, i)),
            (x_other, (rows, depth), lambda i, p: (0, i)),
            (w_in, (depth, both), lambda i, p: (i, 0)),
        ],
        [(shape, BF16, shape, whole2), (shape, F32, shape, whole2), (shape, F32, shape, whole2)],
        place,
        scratch=[pltpu.VMEM((2 * rows, both), F32)],
        flops=4 * rows * width * both,
    )


def route_weight(extra, place_ref, experts):
    lane = lax.broadcasted_iota(jnp.int32, extra.shape, 1)
    me = place_ref[0]
    named = (lane == me) | (lane == me + experts) | (lane == me + 2 * experts)
    return jnp.sum(jnp.where(named, extra.astype(F32), 0.0), axis=1, keepdims=True)


def forward_down(place, hidden, w_down, x_own, x_other, extra):
    experts = lax.axis_size("expert")
    rows = x_own.shape[0]
    own = hidden[0].shape[1]
    height, quarter = w_down.shape
    cols = min(512, quarter)
    at = (x_own.shape[1] - extra) // extra

    def kernel(place_ref, *refs):
        *hidden_refs, w_ref, own_ref, other_ref, out_own_ref, out_other_ref = refs
        total = dot(hidden_refs[0][...], w_ref[:own, :])
        for d in range(1, len(hidden_refs)):
            total += dot(hidden_refs[d][...], w_ref[d * own : (d + 1) * own, :])
        out_own_ref[...] = (
            route_weight(own_ref[...], place_ref, experts) * total[:rows]
        ).astype(BF16)
        out_other_ref[...] = (
            route_weight(other_ref[...], place_ref, experts) * total[rows:]
        ).astype(BF16)

    return call(
        kernel,
        (quarter // cols,),
        [(part, part.shape, whole2) for part in hidden]
        + [
            (w_down, (height, cols), lambda i, p: (0, i)),
            (x_own, (rows, extra), lambda i, p: (0, at)),
            (x_other, (rows, extra), lambda i, p: (0, at)),
        ],
        [((rows, quarter), BF16, (rows, cols), lambda i, p: (0, i))] * 2,
        place,
        flops=4 * rows * height * quarter,
    )


def backward_down(place, err_own, err_other, x_own, x_other, w_down, extra, halves):
    experts = lax.axis_size("expert")
    rows, quarter = err_own.shape
    height = w_down.shape[0]
    own = height // halves
    cuts = 2 if own % 256 == 0 else 1
    size = own // cuts
    at = (x_own.shape[1] - extra) // extra

    def kernel(place_ref, err_own_ref, err_other_ref, own_ref, other_ref, w_ref, grad_ref, *outs):
        step = pl.program_id(0)

        @pl.when(step == 0)
        def _():
            weight = route_weight(own_ref[...], place_ref, experts)
            grad_ref[:rows, :] = (weight * err_own_ref[...].astype(F32)).astype(BF16)
            weight = route_weight(other_ref[...], place_ref, experts)
            grad_ref[rows:, :] = (weight * err_other_ref[...].astype(F32)).astype(BF16)

        part = dot_cols(grad_ref[...], w_ref[...])
        for d in range(halves):
            for c in range(cuts):

                @pl.when(step == d * cuts + c)
                def _():
                    outs[d][:, c * size : (c + 1) * size] = part.astype(outs[d].dtype)

    shape = (2 * rows, own)
    return call(
        kernel,
        (halves * cuts,),
        [
            (err_own, (rows, quarter), whole2),
            (err_other, (rows, quarter), whole2),
            (x_own, (rows, extra), lambda i, p: (0, at)),
            (x_other, (rows, extra), lambda i, p: (0, at)),
            (w_down, (size, quarter), lambda i, p: (i, 0)),
        ],
        [((2 * rows, quarter), BF16, (2 * rows, quarter), whole2), (shape, F32, shape, whole2)]
        + [(shape, BF16, shape, whole2)] * (halves - 1),
        place,
        flops=4 * rows * height * quarter,
    )


def backward_hidden(place, grad_own, arrived, slope, act, w_in, d, quarter):
    both_rows, hidden = slope.shape
    rows = both_rows // 2
    size = min(512, quarter)
    steps = quarter // size
    count = len(arrived)

    def kernel(place_ref, grad_own_ref, *refs):
        arrived_refs = refs[:count]
        slope_ref, act_ref, w_ref, grad_ref, out_own_ref, out_other_ref = refs[count:]

        @pl.when(pl.program_id(0) == 0)
        def _():
            grad_hidden = grad_own_ref[...]
            for ref in arrived_refs:
                grad_hidden += ref[...].astype(F32)
            grad_ref[:, :hidden] = (grad_hidden * slope_ref[...]).astype(BF16)
            grad_ref[:, hidden:] = (grad_hidden * act_ref[...]).astype(BF16)

        part = dot_cols(grad_ref[...], w_ref[...]).astype(BF16)
        out_own_ref[...] = part[:rows]
        out_other_ref[...] = part[rows:]

    shape = (both_rows, hidden)
    return call(
        kernel,
        (steps,),
        [(part, shape, whole2) for part in [grad_own, *arrived, slope, act]]
        + [(w_in, (size, 2 * hidden), lambda i, p: (d * steps + i, 0))],
        [((both_rows, 2 * hidden), BF16, (both_rows, 2 * hidden), whole2)]
        + [((rows, quarter), BF16, (rows, size), lambda i, p: (0, i))] * 2,
        place,
        flops=4 * both_rows * hidden * quarter,
    )


def row_part(place, grad_in, w_in, d, quarter):
    both_rows, both = grad_in.shape
    rows = both_rows // 2
    size = min(512, quarter)
    steps = quarter // size

    def kernel(place_ref, grad_ref, w_ref, out_own_ref, out_other_ref):
        part = dot_cols(grad_ref[...], w_ref[...]).astype(BF16)
        out_own_ref[...] = part[:rows]
        out_other_ref[...] = part[rows:]

    return call(
        kernel,
        (steps,),
        [
            (grad_in, grad_in.shape, whole2),
            (w_in, (size, both), lambda i, p: (d * steps + i, 0)),
        ],
        [((rows, quarter), BF16, (rows, size), lambda i, p: (0, i))] * 2,
        place,
        flops=2 * both_rows * both * quarter,
    )


def ends(grad, codes):
    upper = jnp.sum(grad * codes.astype(F32), axis=0, keepdims=True) * (1.0 / 255.0)
    return jnp.sum(grad, axis=0, keepdims=True) - upper, upper


def ranges_down(place, hidden, grads, codes, groups, halves):
    _, height, quarter = codes.shape
    size = height // groups
    per, rows = hidden_rows(groups, size, halves)
    blocks = height // halves // rows
    flat = [part for parts in hidden for part in parts]
    chunks = len(grads)

    def kernel(place_ref, *refs):
        hidden_refs = refs[: len(flat)]
        grad_refs = refs[len(flat) : len(flat) + chunks]
        code_ref, out_ref = refs[len(flat) + chunks :]
        step = pl.program_id(0)
        base = moved(step, blocks, place_ref) * per
        for d in range(halves):

            @pl.when(step // blocks == d)
            def _():
                for g in range(per):
                    cut = slice(g * size, (g + 1) * size)
                    grad = dot_rows(hidden_refs[d][:, cut], grad_refs[0][...])
                    for c in range(1, chunks):
                        grad += dot_rows(hidden_refs[c * halves + d][:, cut], grad_refs[c][...])
                    low, high = ends(grad, code_ref[0, cut, :])
                    out_ref[0, pl.ds(base + g, 1), :] = low
                    out_ref[1, pl.ds(base + g, 1), :] = high

    shape = (2, groups, quarter)
    return call(
        kernel,
        (height // rows,),
        [(part, (part.shape[0], rows), lambda i, p: (0, i % blocks)) for part in flat]
        + [(grad, grad.shape, whole2) for grad in grads]
        + [(codes, (1, rows, quarter), lambda i, p: (0, moved(i, blocks, p), 0))],
        [(shape, F32, shape, whole3)],
        place,
        flops=2 * sum(g.shape[0] for g in grads) * height * quarter,
    )[0]


def ranges_in(place, x, grads, codes, groups, halves):
    _, _, width, hidden = codes.shape
    size = width // groups
    per = 2
    rows = per * size
    blocks = width // halves // rows
    chunks = len(grads)

    def kernel(place_ref, *refs):
        x_refs = refs[: 2 * chunks]
        grad_refs = refs[2 * chunks : 3 * chunks]
        code_ref, out_ref = refs[3 * chunks :]
        base = moved(pl.program_id(0), blocks, place_ref) * per
        grad = None
        for c in range(chunks):
            left = jnp.concatenate([x_refs[2 * c][...], x_refs[2 * c + 1][...]], axis=0)
            part = dot_rows(left, grad_refs[c][...])
            grad = part if grad is None else grad + part
        for k in range(2):
            for g in range(per):
                cut = slice(g * size, (g + 1) * size)
                low, high = ends(
                    grad[cut, k * hidden : (k + 1) * hidden], code_ref[0, k, cut, :]
                )
                out_ref[2 * k, pl.ds(base + g, 1), :] = low
                out_ref[2 * k + 1, pl.ds(base + g, 1), :] = high

    shape = (4, groups, hidden)
    flat = [part for pair in x for part in pair]
    return call(
        kernel,
        (width // rows,),
        [(part, (part.shape[0], rows), lambda i, p: (0, i)) for part in flat]
        + [(grad, grad.shape, whole2) for grad in grads]
        + [(codes, (1, 2, rows, hidden), lambda i, p: (0, 0, moved(i, blocks, p), 0))],
        [(shape, F32, shape, whole3)],
        place,
        flops=2 * sum(g.size for g in grads) * width,
    )[0]


def local(
    tokens, target, routes, route_scores, in_codes, in_low, in_high, down_codes, down_low, down_high
):
    experts = lax.axis_size("expert")
    halves = lax.axis_size("half")
    me = lax.axis_index("expert")
    my_half = lax.axis_index("half")
    place = jnp.stack([me, my_half]).astype(jnp.int32)
    rows = tokens.shape[0] // CHUNKS
    quarter = target.shape[1]
    parts = range(halves)
    chunks = range(CHUNKS)

    weights = route_scores / jnp.sum(route_scores, axis=1, keepdims=True)
    names = routes[:, :, None] == jnp.arange(experts, dtype=jnp.int32)[None, None, :]
    table = jnp.sum(jnp.where(names, weights[:, :, None], 0.0), axis=1)
    top = lax.reduce_precision(table, 8, 7)
    middle = lax.reduce_precision(table - top, 8, 7)
    bottom = table - top - middle
    extra = -(-3 * experts // 128) * 128
    terms = jnp.concatenate([top, middle, bottom], axis=1)
    terms = jnp.pad(terms, ((0, 0), (0, extra - terms.shape[1]))).astype(BF16)

    mine = [
        lax.dynamic_slice_in_dim(tokens, (my_half ^ d) * quarter, quarter, 1) for d in parts
    ]
    mine = jnp.concatenate(mine + [terms], axis=1)
    x = [gather_rows(mine[c * rows : (c + 1) * rows]) for c in chunks]
    w_in = dequant_in(place, in_codes, in_low, in_high, halves)
    w_down = dequant_down(place, down_codes, down_low, down_high, halves)

    hidden, slope, act = [], [], []
    for c in chunks:
        own, chunk_slope, chunk_act = forward_in(place, *x[c], w_in)
        hidden.append([own] + [swap(own, "half", d) for d in parts if d])
        slope.append(chunk_slope)
        act.append(chunk_act)

    errors = []
    for c in chunks:
        out_own, out_other = forward_down(place, hidden[c], w_down, *x[c], extra)
        mixed = scatter_rows(out_own, swap(out_other, "expert", 1))
        wanted = target[c * rows : (c + 1) * rows].astype(F32)
        errors.append(gather_rows((mixed - wanted).astype(BF16)))

    grads, grad_own, arrived = [], [], []
    for c in chunks:
        grad, own, *others = backward_down(place, *errors[c], *x[c], w_down, extra, halves)
        grads.append(grad)
        grad_own.append(own)
        arrived.append([swap(other, "half", d + 1) for d, other in enumerate(others)])

    grad_in, grad_tokens = [], []
    for c in chunks:
        total = None
        for d in reversed(parts):
            if d == halves - 1:
                both, own, other = backward_hidden(
                    place, grad_own[c], arrived[c], slope[c], act[c], w_in, d, quarter
                )
                grad_in.append(both)
            else:
                own, other = row_part(place, grad_in[c], w_in, d, quarter)
            summed = own.astype(F32) + swap(other, "expert", 1).astype(F32)
            if d:
                summed = swap(summed.astype(BF16), "half", d)
            total = summed if total is None else total.astype(F32) + summed.astype(F32)
        grad_tokens.append(total)
    grad_tokens = [scatter_sum(total) for total in grad_tokens]

    down_grad = ranges_down(place, hidden, grads, down_codes, down_low.shape[1], halves)
    in_grad = ranges_in(place, x, grad_in, in_codes, in_low.shape[2], halves)
    return (
        jnp.concatenate(grad_tokens, axis=0).astype(BF16),
        in_grad[None],
        down_grad[None],
    )


def scatter_sum(total):
    for distance in reversed(far_distances()):
        half = total.shape[0] // 2
        arrived = swap(total[half:].astype(BF16), "expert", distance)
        total = total[:half].astype(F32) + arrived.astype(F32)
    return total


def solution(mesh):
    placed = (
        P("expert", None),
        P("expert", "half"),
        P("expert", None),
        P("expert", None),
        P("expert", None, None, "half"),
        P("expert", None, None, "half"),
        P("expert", None, None, "half"),
        P("expert", None, "half"),
        P("expert", None, "half"),
        P("expert", None, "half"),
    )
    return jax.shard_map(
        local,
        mesh=mesh,
        in_specs=placed,
        out_specs=(
            P("expert", "half"),
            P("expert", None, None, "half"),
            P("expert", None, None, "half"),
        ),
        check_vma=False,
    )
```

```python
import functools

import jax
import jax.numpy as jnp
from jax import lax
from jax.experimental import pallas as pl
from jax.experimental.pallas import tpu as pltpu
from jax.sharding import PartitionSpec as P

BF16 = jnp.bfloat16
F32 = jnp.float32
MIB = 1 << 20


def swap(array, axis, distance):
    size = lax.axis_size(axis)
    return lax.ppermute(array, axis, [(i, i ^ distance) for i in range(size)])


def tie(array, *others):
    return lax.optimization_barrier((array, *others))[0]


def far_distances():
    experts = lax.axis_size("expert")
    distances = []
    distance = experts // 2
    while distance > 4:
        distances.append(distance)
        distance //= 2
    return distances


def join(parts):
    return parts[0] if len(parts) == 1 else jnp.concatenate(parts, axis=0)


def gather_far(block):
    parts = [block]
    for distance in far_distances():
        parts.append(swap(join(parts), "expert", distance))
    return parts


def pick(part, cut):
    if isinstance(part, list):
        return part[0] if cut.start else part[1]
    return part[cut]


def add(parts):
    total = parts[0].astype(F32)
    for part in parts[1:]:
        total = total + part.astype(F32)
    return total


def scatter_rows(near, across):
    rows = near[0].shape[0] // 2
    totals = []
    for cut in (slice(rows, 2 * rows), slice(0, rows)):
        sent = swap(add([pick(part, cut) for part in across]).astype(BF16), "expert", 2)
        totals.append([pick(part, cut) for part in near] + [sent])
    sent = swap(add(totals[0]).astype(BF16), "expert", 4)
    terms = totals[1] + [sent]
    for distance in reversed(far_distances()):
        half = terms[0].shape[0] // 2
        sent = swap(add([part[half:] for part in terms]).astype(BF16), "expert", distance)
        terms = [part[:half] for part in terms] + [sent]
    return add(terms)


def dot(left, right):
    return jnp.dot(left, right, preferred_element_type=F32)


def dot_cols(left, right):
    return lax.dot_general(left, right, (((1,), (1,)), ((), ())), preferred_element_type=F32)


def dot_rows(left, right):
    return lax.dot_general(left, right, (((0,), (0,)), ((), ())), preferred_element_type=F32)


def cost(flops, bytes_accessed):
    return pl.CostEstimate(flops=int(flops), bytes_accessed=int(bytes_accessed), transcendentals=0)


def params(mib):
    return pltpu.CompilerParams(vmem_limit_bytes=mib * MIB)


def moved(step, blocks, place):
    return ((step // blocks) ^ place[1]) * blocks + step % blocks


def call(kernel, grid, ins, outs, place, scratch=(), mib=44, flops=0, reuse=None):
    total = sum(a.size * a.dtype.itemsize for a, _, _ in ins)
    for shape, kind, _, _ in outs:
        count = 1
        for extent in shape:
            count *= extent
        total += count * jnp.dtype(kind).itemsize
    spec = pltpu.PrefetchScalarGridSpec(
        num_scalar_prefetch=1,
        grid=grid,
        in_specs=[pl.BlockSpec(block, index) for _, block, index in ins]
        + ([] if reuse is None else [pl.BlockSpec(memory_space=pl.ANY)]),
        out_specs=[pl.BlockSpec(block, index) for _, _, block, index in outs],
        scratch_shapes=list(scratch),
    )
    return pl.pallas_call(
        kernel,
        grid_spec=spec,
        out_shape=[jax.ShapeDtypeStruct(shape, kind) for shape, kind, _, _ in outs],
        compiler_params=params(mib),
        cost_estimate=cost(flops, total),
        input_output_aliases={} if reuse is None else {1 + len(ins): 0},
    )(place, *[a for a, _, _ in ins], *([] if reuse is None else [reuse]))


def whole2(*_):
    return (0, 0)


def whole3(*_):
    return (0, 0, 0)


def whole4(*_):
    return (0, 0, 0, 0)


def dequant_in(place, codes, low, high, halves):
    _, _, width, hidden = codes.shape
    groups = low.shape[2]
    size = width // groups
    per = max(1, 512 // size)
    rows = per * size
    blocks = width // halves // rows

    def kernel(place_ref, code_ref, low_ref, high_ref, out_ref):
        base = moved(pl.program_id(0), blocks, place_ref) * per
        for k in range(2):
            for g in range(per):
                bottom = low_ref[0, k, pl.ds(base + g, 1), :]
                scale = (high_ref[0, k, pl.ds(base + g, 1), :] - bottom) * (1.0 / 255.0)
                vals = code_ref[0, k, g * size : (g + 1) * size, :].astype(F32)
                out_ref[g * size : (g + 1) * size, k * hidden : (k + 1) * hidden] = (
                    bottom + scale * vals
                ).astype(BF16)

    return call(
        kernel,
        (width // rows,),
        [
            (codes, (1, 2, rows, hidden), lambda i, p: (0, 0, moved(i, blocks, p), 0)),
            (low, low.shape, whole4),
            (high, high.shape, whole4),
        ],
        [((width, 2 * hidden), BF16, (rows, 2 * hidden), lambda i, p: (i, 0))],
        place,
        mib=56,
    )[0]


def hidden_rows(total_groups, size, halves):
    per = total_groups // halves
    while per > 3:
        per = next(f for f in range(2, per + 1) if per % f == 0) and per // next(
            f for f in range(2, per + 1) if per % f == 0
        )
    return per, per * size


def dequant_down(place, codes, low, high, halves):
    _, height, quarter = codes.shape
    groups = low.shape[1]
    size = height // groups
    per, rows = hidden_rows(groups, size, halves)
    blocks = height // halves // rows

    def kernel(place_ref, code_ref, low_ref, high_ref, out_ref):
        base = moved(pl.program_id(0), blocks, place_ref) * per
        for g in range(per):
            bottom = low_ref[0, pl.ds(base + g, 1), :]
            scale = (high_ref[0, pl.ds(base + g, 1), :] - bottom) * (1.0 / 255.0)
            vals = code_ref[0, g * size : (g + 1) * size, :].astype(F32)
            out_ref[g * size : (g + 1) * size, :] = (bottom + scale * vals).astype(BF16)

    return call(
        kernel,
        (height // rows,),
        [
            (codes, (1, rows, quarter), lambda i, p: (0, moved(i, blocks, p), 0)),
            (low, low.shape, whole3),
            (high, high.shape, whole3),
        ],
        [((height, quarter), BF16, (rows, quarter), lambda i, p: (i, 0))],
        place,
        mib=56,
    )[0]


def forward_in(place, x_own, x_other, w_in):
    rows = x_own.shape[0]
    width, both = w_in.shape
    hidden = both // 2
    depth = min(512, width)
    steps = width // depth

    def kernel(place_ref, own_ref, other_ref, w_ref, hidden_ref, slope_ref, act_ref, acc_ref):
        step = pl.program_id(0)
        x = jnp.concatenate([own_ref[...], other_ref[...]], axis=0)
        part = dot(x, w_ref[...])

        @pl.when(step == 0)
        def _():
            acc_ref[...] = part

        @pl.when(step > 0)
        def _():
            acc_ref[...] += part

        @pl.when(step == steps - 1)
        def _():
            gate = acc_ref[:, :hidden]
            up = acc_ref[:, hidden:]
            sig = 1.0 / (1.0 + jnp.exp(-gate))
            act = gate * sig
            hidden_ref[...] = (act * up).astype(BF16)
            slope_ref[...] = up * sig * (1.0 + gate * (1.0 - sig))
            act_ref[...] = act

    shape = (2 * rows, hidden)
    return call(
        kernel,
        (steps,),
        [
            (x_own, (rows, depth), lambda i, p: (0, i)),
            (x_other, (rows, depth), lambda i, p: (0, i)),
            (w_in, (depth, both), lambda i, p: (i, 0)),
        ],
        [(shape, BF16, shape, whole2), (shape, F32, shape, whole2), (shape, F32, shape, whole2)],
        place,
        scratch=[pltpu.VMEM((2 * rows, both), F32)],
        flops=4 * rows * width * both,
    )


def route_weight(extra, place_ref, experts):
    lane = lax.broadcasted_iota(jnp.int32, extra.shape, 1)
    me = place_ref[0]
    named = (lane == me) | (lane == me + experts) | (lane == me + 2 * experts)
    return jnp.sum(jnp.where(named, extra.astype(F32), 0.0), axis=1, keepdims=True)


def forward_down(place, hidden, w_down, x_own, x_other, extra):
    experts = lax.axis_size("expert")
    rows = x_own.shape[0]
    own = hidden[0].shape[1]
    height, quarter = w_down.shape
    cols = min(512, quarter)
    at = (x_own.shape[1] - extra) // extra

    def kernel(place_ref, *refs):
        *hidden_refs, w_ref, own_ref, other_ref, out_own_ref, out_other_ref = refs
        total = dot(hidden_refs[0][...], w_ref[:own, :])
        for d in range(1, len(hidden_refs)):
            total += dot(hidden_refs[d][...], w_ref[d * own : (d + 1) * own, :])
        out_own_ref[...] = (
            route_weight(own_ref[...], place_ref, experts) * total[:rows]
        ).astype(BF16)
        out_other_ref[...] = (
            route_weight(other_ref[...], place_ref, experts) * total[rows:]
        ).astype(BF16)

    return call(
        kernel,
        (quarter // cols,),
        [(part, part.shape, whole2) for part in hidden]
        + [
            (w_down, (height, cols), lambda i, p: (0, i)),
            (x_own, (rows, extra), lambda i, p: (0, at)),
            (x_other, (rows, extra), lambda i, p: (0, at)),
        ],
        [((rows, quarter), BF16, (rows, cols), lambda i, p: (0, i))] * 2,
        place,
        flops=4 * rows * height * quarter,
    )


def backward_down(place, err_own, err_other, x_own, x_other, w_down, extra, halves):
    experts = lax.axis_size("expert")
    rows, quarter = err_own.shape
    height = w_down.shape[0]
    own = height // halves
    cuts = 2 if own % 256 == 0 else 1
    size = own // cuts
    at = (x_own.shape[1] - extra) // extra

    def kernel(place_ref, err_own_ref, err_other_ref, own_ref, other_ref, w_ref, grad_ref, *outs):
        step = pl.program_id(0)

        @pl.when(step == 0)
        def _():
            weight = route_weight(own_ref[...], place_ref, experts)
            grad_ref[:rows, :] = (weight * err_own_ref[...].astype(F32)).astype(BF16)
            weight = route_weight(other_ref[...], place_ref, experts)
            grad_ref[rows:, :] = (weight * err_other_ref[...].astype(F32)).astype(BF16)

        part = dot_cols(grad_ref[...], w_ref[...])
        for d in range(halves):
            for c in range(cuts):

                @pl.when(step == d * cuts + c)
                def _():
                    outs[d][:, c * size : (c + 1) * size] = part.astype(outs[d].dtype)

    shape = (2 * rows, own)
    return call(
        kernel,
        (halves * cuts,),
        [
            (err_own, (rows, quarter), whole2),
            (err_other, (rows, quarter), whole2),
            (x_own, (rows, extra), lambda i, p: (0, at)),
            (x_other, (rows, extra), lambda i, p: (0, at)),
            (w_down, (size, quarter), lambda i, p: (i, 0)),
        ],
        [((2 * rows, quarter), BF16, (2 * rows, quarter), whole2), (shape, F32, shape, whole2)]
        + [(shape, BF16, shape, whole2)] * (halves - 1),
        place,
        flops=4 * rows * height * quarter,
    )


def backward_hidden(place, grad_own, arrived, slope, act, w_in, d, quarter):
    both_rows, hidden = slope.shape
    rows = both_rows // 2
    size = min(512, quarter)
    steps = quarter // size
    count = len(arrived)

    def kernel(place_ref, grad_own_ref, *refs):
        arrived_refs = refs[:count]
        slope_ref, act_ref, w_ref, grad_ref, out_own_ref, out_other_ref = refs[count:]

        @pl.when(pl.program_id(0) == 0)
        def _():
            grad_hidden = grad_own_ref[...]
            for ref in arrived_refs:
                grad_hidden += ref[...].astype(F32)
            grad_ref[:, :hidden] = (grad_hidden * slope_ref[...]).astype(BF16)
            grad_ref[:, hidden:] = (grad_hidden * act_ref[...]).astype(BF16)

        part = dot_cols(grad_ref[...], w_ref[...]).astype(BF16)
        out_own_ref[...] = part[:rows]
        out_other_ref[...] = part[rows:]

    shape = (both_rows, hidden)
    return call(
        kernel,
        (steps,),
        [(part, shape, whole2) for part in [grad_own, *arrived, slope, act]]
        + [(w_in, (size, 2 * hidden), lambda i, p: (d * steps + i, 0))],
        [((both_rows, 2 * hidden), BF16, (both_rows, 2 * hidden), whole2)]
        + [((rows, quarter), BF16, (rows, size), lambda i, p: (0, i))] * 2,
        place,
        flops=4 * both_rows * hidden * quarter,
    )


def row_part(place, grad_in, w_in, d, quarter):
    both_rows, both = grad_in.shape
    rows = both_rows // 2
    size = min(512, quarter)
    steps = quarter // size

    def kernel(place_ref, grad_ref, w_ref, out_own_ref, out_other_ref):
        part = dot_cols(grad_ref[...], w_ref[...]).astype(BF16)
        out_own_ref[...] = part[:rows]
        out_other_ref[...] = part[rows:]

    return call(
        kernel,
        (steps,),
        [
            (grad_in, grad_in.shape, whole2),
            (w_in, (size, both), lambda i, p: (d * steps + i, 0)),
        ],
        [((rows, quarter), BF16, (rows, size), lambda i, p: (0, i))] * 2,
        place,
        flops=2 * both_rows * both * quarter,
    )


def ends(grad, codes):
    upper = jnp.sum(grad * codes.astype(F32), axis=0, keepdims=True) * (1.0 / 255.0)
    return jnp.sum(grad, axis=0, keepdims=True) - upper, upper


def ranges_down(place, hidden, grads, codes, groups, halves):
    _, height, quarter = codes.shape
    size = height // groups
    per, rows = hidden_rows(groups, size, halves)
    blocks = height // halves // rows
    flat = [part for parts in hidden for part in parts]
    chunks = len(grads)

    def kernel(place_ref, *refs):
        hidden_refs = refs[: len(flat)]
        grad_refs = refs[len(flat) : len(flat) + chunks]
        code_ref, out_ref = refs[len(flat) + chunks :]
        step = pl.program_id(0)
        base = moved(step, blocks, place_ref) * per
        for d in range(halves):

            @pl.when(step // blocks == d)
            def _():
                for g in range(per):
                    cut = slice(g * size, (g + 1) * size)
                    grad = dot_rows(hidden_refs[d][:, cut], grad_refs[0][...])
                    for c in range(1, chunks):
                        grad += dot_rows(hidden_refs[c * halves + d][:, cut], grad_refs[c][...])
                    low, high = ends(grad, code_ref[0, cut, :])
                    out_ref[0, pl.ds(base + g, 1), :] = low
                    out_ref[1, pl.ds(base + g, 1), :] = high

    shape = (2, groups, quarter)
    return call(
        kernel,
        (height // rows,),
        [(part, (part.shape[0], rows), lambda i, p: (0, i % blocks)) for part in flat]
        + [(grad, grad.shape, whole2) for grad in grads]
        + [(codes, (1, rows, quarter), lambda i, p: (0, moved(i, blocks, p), 0))],
        [(shape, F32, shape, whole3)],
        place,
        flops=2 * sum(g.shape[0] for g in grads) * height * quarter,
    )[0]


def ranges_in(place, x, grads, codes, groups, halves, d, found):
    _, _, width, hidden = codes.shape
    size = width // groups
    per = 2
    rows = per * size
    blocks = width // halves // rows
    held = groups // halves
    chunks = len(grads)

    def kernel(place_ref, *refs):
        x_refs = refs[: 2 * chunks]
        grad_refs = refs[2 * chunks : 3 * chunks]
        code_ref, out_ref = refs[3 * chunks], refs[-1]
        base = pl.program_id(0) * per
        left = [
            jnp.concatenate([x_refs[2 * c][...], x_refs[2 * c + 1][...]], axis=0)
            for c in range(chunks)
        ]
        for k in range(2):
            cols = slice(k * hidden, (k + 1) * hidden)
            grad = dot_rows(left[0], grad_refs[0][:, cols])
            for c in range(1, chunks):
                grad += dot_rows(left[c], grad_refs[c][:, cols])
            for g in range(per):
                cut = slice(g * size, (g + 1) * size)
                low, high = ends(grad[cut], code_ref[0, k, cut, :])
                out_ref[2 * k, pl.ds(base + g, 1), :] = low
                out_ref[2 * k + 1, pl.ds(base + g, 1), :] = high

    shape = (4, groups, hidden)
    flat = [part for pair in x for part in pair]
    ins = (
        [(part, (part.shape[0], rows), lambda i, p: (0, d * blocks + i)) for part in flat]
        + [(grad, grad.shape, whole2) for grad in grads]
        + [
            (
                codes,
                (1, 2, rows, hidden),
                lambda i, p: (0, 0, (p[1] ^ d) * blocks + i, 0),
            )
        ]
    )
    return call(
        kernel,
        (blocks,),
        ins,
        [(shape, F32, (4, held, hidden), lambda i, p: (0, p[1] ^ d, 0))],
        place,
        flops=2 * sum(g.size for g in grads) * (width // halves),
        reuse=found,
    )[0]


def prepare(place, tokens, routes, route_scores, extra):
    experts = lax.axis_size("expert")
    halves = lax.axis_size("half")
    rows, width = tokens.shape
    quarter = width // halves
    top_count = routes.shape[1]

    def kernel(place_ref, token_ref, route_ref, score_ref, out_ref):
        for d in range(halves):
            start = pl.multiple_of((place_ref[1] ^ d) * quarter, 128)
            out_ref[:, d * quarter : (d + 1) * quarter] = token_ref[:, pl.ds(start, quarter)]
        scores = score_ref[...]
        weights = scores / jnp.sum(scores, axis=1, keepdims=True)
        names = route_ref[...]
        lane = lax.broadcasted_iota(jnp.int32, (rows, extra), 1)
        third = jnp.where(lane < experts, 0, jnp.where(lane < 2 * experts, 1, 2))
        expert = lane - third * experts
        table = jnp.zeros((rows, extra), F32)
        for k in range(top_count):
            table += jnp.where(expert == names[:, k : k + 1], weights[:, k : k + 1], 0.0)
        top = table.astype(BF16).astype(F32)
        middle = (table - top).astype(BF16).astype(F32)
        bottom = table - top - middle
        terms = jnp.where(third == 0, top, jnp.where(third == 1, middle, bottom))
        out_ref[:, width:] = terms.astype(BF16)

    return call(
        kernel,
        (1,),
        [(a, a.shape, whole2) for a in (tokens, routes, route_scores)],
        [((rows, width + extra), BF16, (rows, width + extra), whole2)],
        place,
    )[0]


def local(
    tokens, target, routes, route_scores, in_codes, in_low, in_high, down_codes, down_low, down_high
):
    experts = lax.axis_size("expert")
    halves = lax.axis_size("half")
    place = jnp.stack([lax.axis_index("expert"), lax.axis_index("half")]).astype(jnp.int32)
    quarter = target.shape[1]
    parts = range(halves)
    chunks = (0, 1)
    extra = -(-3 * experts // 128) * 128

    mine = prepare(place, tokens, routes, route_scores, extra)
    near_own = swap(mine, "expert", 4)
    across = [swap(mine, "expert", 2)]
    far = join(gather_far(mine)[1:])
    w_in = dequant_in(place, in_codes, in_low, in_high, halves)
    w_down = dequant_down(place, down_codes, down_low, down_high, halves)
    far = tie(far, w_in, w_down)
    near_far = swap(far, "expert", 4)
    first = jnp.concatenate([mine, far, near_own, near_far], axis=0)
    across += [swap(part, "expert", 2) for part in (far, near_own, near_far)]
    x = [(first, swap(first, "expert", 1))]

    hidden, slope, act = [], [], []
    for c in chunks:
        if c == 1:
            across[3] = tie(across[3], hidden[0][0])
            second = jnp.concatenate(across, axis=0)
            x.append((second, swap(second, "expert", 1)))
        own, chunk_slope, chunk_act = forward_in(place, *x[c], w_in)
        hidden.append([own] + [swap(own, "half", d) for d in parts if d])
        slope.append(chunk_slope)
        act.append(chunk_act)

    sums = []
    for c in chunks:
        if c == 1:
            hidden[1][1:] = [tie(part, sums[0][0]) for part in hidden[1][1:]]
        out_own, out_other = forward_down(place, hidden[c], w_down, *x[c], extra)
        sums.append([out_own, swap(out_other, "expert", 1)])
    mixed = scatter_rows(sums[0], sums[1])
    error = (mixed - target.astype(F32)).astype(BF16)

    kept = join(gather_far(error))
    near = swap(kept, "expert", 4)
    across = [swap(kept, "expert", 2), swap(near, "expert", 2)]
    first = jnp.concatenate([kept, near], axis=0)
    errors = [(first, swap(first, "expert", 1))]
    grads, grad_own, arrived = [], [], []
    for c in chunks:
        if c == 1:
            across[1] = tie(across[1], grads[0])
            second = jnp.concatenate(across, axis=0)
            errors.append((second, swap(second, "expert", 1)))
        grad, own, *others = backward_down(place, *errors[c], *x[c], w_down, extra, halves)
        grads.append(grad)
        grad_own.append(own)
        arrived.append([swap(other, "half", d + 1) for d, other in enumerate(others)])

    grad_in, sums = [], [[], []]
    last = halves - 1

    def spread(c, d, own, other):
        rows = own.shape[0] // 2
        cuts = [slice(rows, 2 * rows), slice(0, rows)] if c else [slice(0, 2 * rows)]
        pieces = [add([own[cut], other[cut]]).astype(BF16) for cut in cuts]
        if c:
            pieces = [tie(piece, sums[0][-1]) for piece in pieces] if d == last else pieces
        sent = [swap(piece, "half", d) for piece in pieces]
        sums[c].append(sent if c else sent[0])
        return pieces

    for c in chunks:
        if c == 1:
            arrived[1] = [tie(part, *pieces) for part in arrived[1]]
        both, own, other = backward_hidden(
            place, grad_own[c], arrived[c], slope[c], act[c], w_in, last, quarter
        )
        grad_in.append(both)
        pieces = spread(c, last, own, swap(other, "expert", 1))
    for d in range(last - 1, -1, -1):
        for c in chunks:
            own, other = row_part(place, grad_in[c], w_in, d, quarter)
            other = swap(other, "expert", 1)
            if d:
                spread(c, d, own, other)
            else:
                sums[c] += [own, other]
    grad_tokens = scatter_rows(*sums)

    grads = [tie(grad, *grad_in) for grad in grads]
    down_grad = ranges_down(place, hidden, grads, down_codes, down_low.shape[1], halves)
    in_grad = None
    for d in parts:
        in_grad = ranges_in(place, x, grad_in, in_codes, in_low.shape[2], halves, d, in_grad)
    return (grad_tokens.astype(BF16), in_grad[None], down_grad[None])


def solution(mesh):
    placed = (
        P("expert", None),
        P("expert", "half"),
        P("expert", None),
        P("expert", None),
        P("expert", None, None, "half"),
        P("expert", None, None, "half"),
        P("expert", None, None, "half"),
        P("expert", None, "half"),
        P("expert", None, "half"),
        P("expert", None, "half"),
    )
    return jax.shard_map(
        local,
        mesh=mesh,
        in_specs=placed,
        out_specs=(
            P("expert", "half"),
            P("expert", None, None, "half"),
            P("expert", None, None, "half"),
        ),
        check_vma=False,
    )
```

```python
import functools

import jax
import jax.numpy as jnp
from jax import lax
from jax.experimental import pallas as pl
from jax.experimental.pallas import tpu as pltpu
from jax.sharding import PartitionSpec as P

BF16 = jnp.bfloat16
F32 = jnp.float32
MIB = 1 << 20


def swap(array, axis, distance):
    size = lax.axis_size(axis)
    return lax.ppermute(array, axis, [(i, i ^ distance) for i in range(size)])


def tie(array, *others):
    return lax.optimization_barrier((array, *others))[0]


def far_distances():
    experts = lax.axis_size("expert")
    distances = []
    distance = experts // 2
    while distance > 4:
        distances.append(distance)
        distance //= 2
    return distances


def join(parts):
    return parts[0] if len(parts) == 1 else jnp.concatenate(parts, axis=0)


def gather_far(block):
    parts = [block]
    for distance in far_distances():
        parts.append(swap(join(parts), "expert", distance))
    return parts


def pick(part, cut):
    if isinstance(part, list):
        return part[0] if cut.start else part[1]
    return part[cut]


def add(parts):
    total = parts[0].astype(F32)
    for part in parts[1:]:
        total = total + part.astype(F32)
    return total


def scatter_rows(near, across):
    rows = near[0].shape[0] // 2
    totals = []
    for cut in (slice(rows, 2 * rows), slice(0, rows)):
        sent = swap(add([pick(part, cut) for part in across]).astype(BF16), "expert", 2)
        totals.append([pick(part, cut) for part in near] + [sent])
    sent = swap(add(totals[0]).astype(BF16), "expert", 4)
    terms = totals[1] + [sent]
    for distance in reversed(far_distances()):
        half = terms[0].shape[0] // 2
        sent = swap(add([part[half:] for part in terms]).astype(BF16), "expert", distance)
        terms = [part[:half] for part in terms] + [sent]
    return add(terms)


def dot(left, right):
    return jnp.dot(left, right, preferred_element_type=F32)


def dot_cols(left, right):
    return lax.dot_general(left, right, (((1,), (1,)), ((), ())), preferred_element_type=F32)


def dot_rows(left, right):
    return lax.dot_general(left, right, (((0,), (0,)), ((), ())), preferred_element_type=F32)


def cost(flops, bytes_accessed):
    return pl.CostEstimate(flops=int(flops), bytes_accessed=int(bytes_accessed), transcendentals=0)


def moved(step, blocks, place):
    return ((step // blocks) ^ place[1]) * blocks + step % blocks


def call(kernel, grid, ins, outs, place, scratch=(), mib=16, flops=0, reuse=None):
    total = sum(a.size * a.dtype.itemsize for a, _, _ in ins)
    for shape, kind, _, _ in outs:
        count = 1
        for extent in shape:
            count *= extent
        total += count * jnp.dtype(kind).itemsize

    def spec(block, index):
        if isinstance(block, tuple):
            return pl.BlockSpec(block, index)
        return pl.BlockSpec(memory_space=block)

    in_specs = [spec(block, index) for _, block, index in ins]
    arrays = [a for a, _, _ in ins]
    if reuse is not None:
        in_specs.append(pl.BlockSpec(memory_space=pl.ANY))
        arrays.append(reuse)
    return pl.pallas_call(
        kernel,
        grid_spec=pltpu.PrefetchScalarGridSpec(
            num_scalar_prefetch=1,
            grid=grid,
            in_specs=in_specs,
            out_specs=[spec(block, index) for _, _, block, index in outs],
            scratch_shapes=list(scratch),
        ),
        out_shape=[jax.ShapeDtypeStruct(shape, kind) for shape, kind, _, _ in outs],
        compiler_params=pltpu.CompilerParams(vmem_limit_bytes=mib * MIB),
        cost_estimate=cost(flops, total),
        input_output_aliases={} if reuse is None else {1 + len(ins): 0},
    )(place, *arrays)


def resident(kernel, ins, outs, place, mib=16, flops=0, scratch=()):
    return call(
        kernel,
        (),
        [(a, pltpu.VMEM, None) for a in ins],
        [(shape, kind, pltpu.VMEM, None) for shape, kind in outs],
        place,
        mib=mib,
        flops=flops,
        scratch=scratch,
    )


def step_of(extent):
    return 256 if extent % 256 == 0 else 128


def tiles(extent, body):
    size = step_of(extent)

    def step(i, carry):
        body(pl.multiple_of(i * size, size))
        return carry

    lax.fori_loop(0, extent // size, step, 0)


def whole2(*_):
    return (0, 0)


def whole3(*_):
    return (0, 0, 0)


def whole4(*_):
    return (0, 0, 0, 0)


def dequant(place, codes, low, high, halves):
    count, height, cols = codes.shape
    groups = low.shape[1]
    size = height // groups
    held = groups // halves

    def kernel(place_ref, code_ref, low_ref, high_ref, out_ref):
        def block(i, carry):
            base = moved(i, held, place_ref)
            source = pl.multiple_of(base * size, size)
            to = pl.multiple_of(i * size, size)
            for k in range(count):
                bottom = low_ref[k, pl.ds(base, 1), :]
                scale = (high_ref[k, pl.ds(base, 1), :] - bottom) * (1.0 / 255.0)
                vals = code_ref[k, pl.ds(source, size), :].astype(F32)
                out_ref[pl.ds(to, size), k * cols : (k + 1) * cols] = (
                    bottom + scale * vals
                ).astype(BF16)
            return carry

        lax.fori_loop(0, groups, block, 0)

    return resident(
        kernel, [codes, low, high], [((height, count * cols), BF16)], place
    )[0]


def hidden_rows(total_groups, size, halves):
    per = total_groups // halves
    while per > 3:
        per = next(f for f in range(2, per + 1) if per % f == 0) and per // next(
            f for f in range(2, per + 1) if per % f == 0
        )
    return per, per * size


def forward_in(place, x_own, x_other, w_in):
    rows = x_own.shape[0]
    width, both = w_in.shape
    hidden = both // 2
    size = step_of(hidden)

    def kernel(place_ref, own_ref, other_ref, w_ref, hidden_ref, slope_ref, act_ref):
        x = jnp.concatenate([own_ref[:, :width], other_ref[:, :width]], axis=0)

        def body(start):
            gate = dot(x, w_ref[:, pl.ds(start, size)])
            up = dot(x, w_ref[:, pl.ds(pl.multiple_of(hidden + start, size), size)])
            sig = 1.0 / (1.0 + jnp.exp(-gate))
            act = gate * sig
            hidden_ref[:, pl.ds(start, size)] = (act * up).astype(BF16)
            slope_ref[:, pl.ds(start, size)] = up * sig * (1.0 + gate * (1.0 - sig))
            act_ref[:, pl.ds(start, size)] = act

        tiles(hidden, body)

    shape = (2 * rows, hidden)
    return resident(
        kernel,
        [x_own, x_other, w_in],
        [(shape, BF16), (shape, F32), (shape, F32)],
        place,
        flops=4 * rows * width * both,
    )


def route_weight(extra, place_ref, experts):
    lane = lax.broadcasted_iota(jnp.int32, extra.shape, 1)
    me = place_ref[0]
    named = (lane == me) | (lane == me + experts) | (lane == me + 2 * experts)
    return jnp.sum(jnp.where(named, extra.astype(F32), 0.0), axis=1, keepdims=True)


def forward_down(place, hidden, w_down, x_own, x_other, extra):
    experts = lax.axis_size("expert")
    rows = x_own.shape[0]
    height, quarter = w_down.shape
    width = x_own.shape[1] - extra
    size = step_of(quarter)

    def kernel(place_ref, *refs):
        *hidden_refs, w_ref, own_ref, other_ref, out_own_ref, out_other_ref = refs
        left = jnp.concatenate([ref[...] for ref in hidden_refs], axis=1)
        own = route_weight(own_ref[:, width:], place_ref, experts)
        other = route_weight(other_ref[:, width:], place_ref, experts)

        def body(start):
            total = dot(left, w_ref[:, pl.ds(start, size)])
            out_own_ref[:, pl.ds(start, size)] = (own * total[:rows]).astype(BF16)
            out_other_ref[:, pl.ds(start, size)] = (other * total[rows:]).astype(BF16)

        tiles(quarter, body)

    return resident(
        kernel,
        [*hidden, w_down, x_own, x_other],
        [((rows, quarter), BF16)] * 2,
        place,
        flops=4 * rows * height * quarter,
    )


def backward_down(place, err_own, err_other, x_own, x_other, w_down, extra, halves):
    experts = lax.axis_size("expert")
    rows, quarter = err_own.shape
    height = w_down.shape[0]
    own = height // halves
    width = x_own.shape[1] - extra
    size = step_of(own)

    def kernel(place_ref, err_own_ref, err_other_ref, own_ref, other_ref, w_ref, grad_ref, *outs):
        weight = route_weight(own_ref[:, width:], place_ref, experts)
        grad_ref[:rows, :] = (weight * err_own_ref[...].astype(F32)).astype(BF16)
        weight = route_weight(other_ref[:, width:], place_ref, experts)
        grad_ref[rows:, :] = (weight * err_other_ref[...].astype(F32)).astype(BF16)
        for d in range(halves):

            def body(start):
                at = pl.multiple_of(d * own + start, size)
                part = dot_cols(grad_ref[...], w_ref[pl.ds(at, size), :])
                outs[d][:, pl.ds(start, size)] = part.astype(outs[d].dtype)

            tiles(own, body)

    shape = (2 * rows, own)
    return resident(
        kernel,
        [err_own, err_other, x_own, x_other, w_down],
        [((2 * rows, quarter), BF16), (shape, F32)] + [(shape, BF16)] * (halves - 1),
        place,
        flops=4 * rows * height * quarter,
    )


def backward_hidden(place, grad_own, arrived, slope, act, w_in, d, quarter):
    both_rows, hidden = slope.shape
    rows = both_rows // 2
    size = step_of(quarter)
    count = len(arrived)

    def kernel(place_ref, grad_own_ref, *refs):
        arrived_refs = refs[:count]
        slope_ref, act_ref, w_ref, grad_ref, out_own_ref, out_other_ref = refs[count:]
        grad_hidden = grad_own_ref[...]
        for ref in arrived_refs:
            grad_hidden += ref[...].astype(F32)
        grad_ref[:, :hidden] = (grad_hidden * slope_ref[...]).astype(BF16)
        grad_ref[:, hidden:] = (grad_hidden * act_ref[...]).astype(BF16)

        def body(start):
            at = pl.multiple_of(d * quarter + start, size)
            part = dot_cols(grad_ref[...], w_ref[pl.ds(at, size), :]).astype(BF16)
            out_own_ref[:, pl.ds(start, size)] = part[:rows]
            out_other_ref[:, pl.ds(start, size)] = part[rows:]

        tiles(quarter, body)

    return resident(
        kernel,
        [grad_own, *arrived, slope, act, w_in],
        [((both_rows, 2 * hidden), BF16)] + [((rows, quarter), BF16)] * 2,
        place,
        flops=4 * both_rows * hidden * quarter,
    )


def row_part(place, grad_in, w_in, d, quarter):
    both_rows, both = grad_in.shape
    rows = both_rows // 2
    size = step_of(quarter)

    def kernel(place_ref, grad_ref, w_ref, out_own_ref, out_other_ref):
        def body(start):
            at = pl.multiple_of(d * quarter + start, size)
            part = dot_cols(grad_ref[...], w_ref[pl.ds(at, size), :]).astype(BF16)
            out_own_ref[:, pl.ds(start, size)] = part[:rows]
            out_other_ref[:, pl.ds(start, size)] = part[rows:]

        tiles(quarter, body)

    return resident(
        kernel,
        [grad_in, w_in],
        [((rows, quarter), BF16)] * 2,
        place,
        flops=2 * both_rows * both * quarter,
    )


def ends(grad, codes):
    upper = jnp.sum(grad * codes.astype(F32), axis=0, keepdims=True) * (1.0 / 255.0)
    return jnp.sum(grad, axis=0, keepdims=True) - upper, upper


def range_tile(left, right, size, step, codes, store):
    turned = left.T
    for start in range(0, right.shape[1], step):
        cols = slice(start, start + step)
        grad = dot(turned, right[:, cols])
        for g in range(turned.shape[0] // size):
            cut = slice(g * size, (g + 1) * size)
            low, high = ends(grad[cut], codes(cut, cols))
            store(g, cols, low, high)


def ranges_down(place, hidden, grads, codes, groups, halves):
    _, height, quarter = codes.shape
    size = height // groups
    per, rows = hidden_rows(groups, size, halves)
    blocks = height // halves // rows
    flat = [part for parts in hidden for part in parts]
    chunks = len(grads)
    tokens = grads[0].shape[0]

    def kernel(place_ref, *refs):
        hidden_refs = refs[: len(flat)]
        grad_refs = refs[len(flat) : len(flat) + chunks]
        code_ref, out_ref, right_ref = refs[len(flat) + chunks :]
        step = pl.program_id(0)
        base = moved(step, blocks, place_ref) * per

        @pl.when(step == 0)
        def _():
            for c in range(chunks):
                right_ref[c * tokens : (c + 1) * tokens, :] = grad_refs[c][...]

        def store(g, cols, low, high):
            out_ref[0, pl.ds(base + g, 1), cols] = low
            out_ref[1, pl.ds(base + g, 1), cols] = high

        for d in range(halves):

            @pl.when(step // blocks == d)
            def _():
                left = [hidden_refs[c * halves + d][...] for c in range(chunks)]
                range_tile(
                    jnp.concatenate(left, axis=0),
                    right_ref,
                    size,
                    step_of(quarter),
                    lambda cut, cols: code_ref[0, cut, cols],
                    store,
                )

    shape = (2, groups, quarter)
    return call(
        kernel,
        (height // rows,),
        [(part, (part.shape[0], rows), lambda i, p: (0, i % blocks)) for part in flat]
        + [(grad, pltpu.VMEM, None) for grad in grads]
        + [(codes, (1, rows, quarter), lambda i, p: (0, moved(i, blocks, p), 0))],
        [(shape, F32, shape, whole3)],
        place,
        scratch=[pltpu.VMEM((chunks * tokens, quarter), BF16)],
        mib=20,
        flops=2 * sum(g.shape[0] for g in grads) * height * quarter,
    )[0]


def ranges_in(place, x, grads, codes, groups, halves, d, found):
    _, _, width, hidden = codes.shape
    size = width // groups
    held = groups // halves
    per = next(p for p in (4, 2, 1) if held % p == 0)
    rows = per * size
    blocks = held // per
    chunks = len(grads)
    tokens, both = grads[0].shape

    def kernel(place_ref, *refs):
        x_refs = refs[: 2 * chunks]
        grad_refs = refs[2 * chunks : 3 * chunks]
        code_ref, out_ref, right_ref = refs[3 * chunks], refs[-2], refs[-1]
        step = pl.program_id(0)
        base = step * per

        @pl.when(step == 0)
        def _():
            for c in range(chunks):
                right_ref[c * tokens : (c + 1) * tokens, :] = grad_refs[c][...]

        def split(cols):
            k = cols.start // hidden
            return k, slice(cols.start - k * hidden, cols.stop - k * hidden)

        def codes_at(cut, cols):
            k, cols = split(cols)
            return code_ref[0, k, cut, cols]

        def store(g, cols, low, high):
            k, cols = split(cols)
            out_ref[2 * k, pl.ds(base + g, 1), cols] = low
            out_ref[2 * k + 1, pl.ds(base + g, 1), cols] = high

        left = jnp.concatenate([ref[...] for ref in x_refs], axis=0)
        wide = 256 if hidden % 256 == 0 else hidden
        range_tile(left, right_ref, size, wide, codes_at, store)

    shape = (4, groups, hidden)
    flat = [part for pair in x for part in pair]
    return call(
        kernel,
        (blocks,),
        [(part, (part.shape[0], rows), lambda i, p: (0, d * blocks + i)) for part in flat]
        + [(grad, pltpu.VMEM, None) for grad in grads]
        + [
            (
                codes,
                (1, 2, rows, hidden),
                lambda i, p: (0, 0, (p[1] ^ d) * blocks + i, 0),
            )
        ],
        [(shape, F32, (4, held, hidden), lambda i, p: (0, p[1] ^ d, 0))],
        place,
        scratch=[pltpu.VMEM((chunks * tokens, both), BF16)],
        mib=20,
        flops=2 * sum(g.size for g in grads) * (width // halves),
        reuse=found,
    )[0]


def prepare(place, tokens, routes, route_scores, extra):
    experts = lax.axis_size("expert")
    halves = lax.axis_size("half")
    rows, width = tokens.shape
    quarter = width // halves
    top_count = routes.shape[1]

    def kernel(place_ref, token_ref, route_ref, score_ref, out_ref):
        for d in range(halves):
            start = pl.multiple_of((place_ref[1] ^ d) * quarter, 128)
            out_ref[:, d * quarter : (d + 1) * quarter] = token_ref[:, pl.ds(start, quarter)]
        scores = score_ref[...]
        weights = scores / jnp.sum(scores, axis=1, keepdims=True)
        names = route_ref[...]
        lane = lax.broadcasted_iota(jnp.int32, (rows, extra), 1)
        third = jnp.where(lane < experts, 0, jnp.where(lane < 2 * experts, 1, 2))
        expert = lane - third * experts
        table = jnp.zeros((rows, extra), F32)
        for k in range(top_count):
            table += jnp.where(expert == names[:, k : k + 1], weights[:, k : k + 1], 0.0)
        top = table.astype(BF16).astype(F32)
        middle = (table - top).astype(BF16).astype(F32)
        bottom = table - top - middle
        terms = jnp.where(third == 0, top, jnp.where(third == 1, middle, bottom))
        out_ref[:, width:] = terms.astype(BF16)

    return call(
        kernel,
        (1,),
        [(a, a.shape, whole2) for a in (tokens, routes, route_scores)],
        [((rows, width + extra), BF16, (rows, width + extra), whole2)],
        place,
    )[0]


def local(
    tokens, target, routes, route_scores, in_codes, in_low, in_high, down_codes, down_low, down_high
):
    experts = lax.axis_size("expert")
    halves = lax.axis_size("half")
    place = jnp.stack([lax.axis_index("expert"), lax.axis_index("half")]).astype(jnp.int32)
    quarter = target.shape[1]
    parts = range(halves)
    chunks = (0, 1)
    extra = -(-3 * experts // 128) * 128

    mine = prepare(place, tokens, routes, route_scores, extra)
    near_own = swap(mine, "expert", 4)
    across = [swap(mine, "expert", 2)]
    far = join(gather_far(mine)[1:])
    w_in = dequant(place, in_codes[0], in_low[0], in_high[0], halves)
    far = tie(far, w_in)
    near_far = swap(far, "expert", 4)
    w_down = dequant(place, down_codes, tie(down_low, w_in), down_high, halves)
    near_far = tie(near_far, w_down)
    first = jnp.concatenate([mine, far, near_own, near_far], axis=0)
    across += [swap(part, "expert", 2) for part in (far, near_own, near_far)]
    x = [(first, swap(first, "expert", 1))]

    hidden, slope, act = [], [], []
    for c in chunks:
        if c == 1:
            across[3] = tie(across[3], hidden[0][0])
            second = jnp.concatenate(across, axis=0)
            x.append((second, swap(second, "expert", 1)))
        own, chunk_slope, chunk_act = forward_in(place, *x[c], w_in)
        hidden.append([own] + [swap(own, "half", d) for d in parts if d])
        slope.append(chunk_slope)
        act.append(chunk_act)

    sums = []
    for c in chunks:
        if c == 1:
            hidden[1][1:] = [tie(part, sums[0][0]) for part in hidden[1][1:]]
        out_own, out_other = forward_down(place, hidden[c], w_down, *x[c], extra)
        sums.append([out_own, swap(out_other, "expert", 1)])
    mixed = scatter_rows(sums[0], sums[1])
    error = (mixed - target.astype(F32)).astype(BF16)

    kept = join(gather_far(error))
    near = swap(kept, "expert", 4)
    across = [swap(kept, "expert", 2), swap(near, "expert", 2)]
    first = jnp.concatenate([kept, near], axis=0)
    errors = [(first, swap(first, "expert", 1))]
    grads, grad_own, arrived = [], [], []
    for c in chunks:
        if c == 1:
            across[1] = tie(across[1], grads[0])
            second = jnp.concatenate(across, axis=0)
            errors.append((second, swap(second, "expert", 1)))
        grad, own, *others = backward_down(place, *errors[c], *x[c], w_down, extra, halves)
        grads.append(grad)
        grad_own.append(own)
        arrived.append([swap(other, "half", d + 1) for d, other in enumerate(others)])

    grad_in, sums = [], [[], []]
    last = halves - 1

    def spread(c, d, own, other):
        rows = own.shape[0] // 2
        cuts = [slice(rows, 2 * rows), slice(0, rows)] if c else [slice(0, 2 * rows)]
        pieces = [add([own[cut], other[cut]]).astype(BF16) for cut in cuts]
        if c:
            pieces = [tie(piece, sums[0][-1]) for piece in pieces] if d == last else pieces
        sent = [swap(piece, "half", d) for piece in pieces]
        sums[c].append(sent if c else sent[0])
        return pieces

    arrived[0] = [tie(part, grads[1]) for part in arrived[0]]
    for c in chunks:
        if c == 1:
            arrived[1] = [tie(part, *pieces) for part in arrived[1]]
        both, own, other = backward_hidden(
            place, grad_own[c], arrived[c], slope[c], act[c], w_in, last, quarter
        )
        grad_in.append(both)
        pieces = spread(c, last, own, swap(other, "expert", 1))
    for d in range(last - 1, -1, -1):
        for c in chunks:
            own, other = row_part(place, grad_in[c], w_in, d, quarter)
            other = swap(other, "expert", 1)
            if d:
                spread(c, d, own, other)
            else:
                sums[c] += [own, other]
    grad_tokens = scatter_rows(*sums)

    grads = [tie(grad, *grad_in) for grad in grads]
    down_grad = ranges_down(place, hidden, grads, down_codes, down_low.shape[1], halves)
    in_grad = None
    for d in parts:
        in_grad = ranges_in(place, x, grad_in, in_codes, in_low.shape[2], halves, d, in_grad)
    return (grad_tokens.astype(BF16), in_grad[None], down_grad[None])


def solution(mesh):
    placed = (
        P("expert", None),
        P("expert", "half"),
        P("expert", None),
        P("expert", None),
        P("expert", None, None, "half"),
        P("expert", None, None, "half"),
        P("expert", None, None, "half"),
        P("expert", None, "half"),
        P("expert", None, "half"),
        P("expert", None, "half"),
    )
    return jax.shard_map(
        local,
        mesh=mesh,
        in_specs=placed,
        out_specs=(
            P("expert", "half"),
            P("expert", None, None, "half"),
            P("expert", None, None, "half"),
        ),
        check_vma=False,
    )
```

```python
import functools

import jax
import jax.numpy as jnp
from jax import lax
from jax.experimental import pallas as pl
from jax.experimental.pallas import tpu as pltpu
from jax.sharding import PartitionSpec as P

BF16 = jnp.bfloat16
F32 = jnp.float32
MIB = 1 << 20


def swap(array, axis, distance):
    size = lax.axis_size(axis)
    return lax.ppermute(array, axis, [(i, i ^ distance) for i in range(size)])


def tie(array, *others):
    return lax.optimization_barrier((array, *others))[0]


def far_distances():
    experts = lax.axis_size("expert")
    distances = []
    distance = experts // 2
    while distance > 4:
        distances.append(distance)
        distance //= 2
    return distances


def join(parts):
    return parts[0] if len(parts) == 1 else jnp.concatenate(parts, axis=0)


def gather_far(block):
    parts = [block]
    for distance in far_distances():
        parts.append(swap(join(parts), "expert", distance))
    return parts


def add(parts):
    total = parts[0].astype(F32)
    for part in parts[1:]:
        total = total + part.astype(F32)
    return total


def scatter_far(terms):
    for distance in reversed(far_distances()):
        half = terms[0].shape[0] // 2
        sent = swap(add([part[half:] for part in terms]).astype(BF16), "expert", distance)
        terms = [part[:half] for part in terms] + [sent]
    return add(terms)


def scatter_rows(near, across):
    rows = near[0].shape[0] // 2
    upper = swap(add([part[rows:] for part in across]).astype(BF16), "expert", 2)
    sent = swap(add([part[rows:] for part in near] + [upper]).astype(BF16), "expert", 4)
    lower = tie(add([part[:rows] for part in across]).astype(BF16), upper)
    return scatter_far([part[:rows] for part in near] + [swap(lower, "expert", 2), sent])


def dot(left, right):
    return jnp.dot(left, right, preferred_element_type=F32)


def dot_cols(left, right):
    return lax.dot_general(left, right, (((1,), (1,)), ((), ())), preferred_element_type=F32)


def dot_rows(left, right):
    return lax.dot_general(left, right, (((0,), (0,)), ((), ())), preferred_element_type=F32)


def cost(flops, bytes_accessed):
    return pl.CostEstimate(flops=int(flops), bytes_accessed=int(bytes_accessed), transcendentals=0)


def moved(step, blocks, place):
    return ((step // blocks) ^ place[1]) * blocks + step % blocks


def call(kernel, grid, ins, outs, place, scratch=(), mib=16, flops=0, reuse=None):
    total = sum(a.size * a.dtype.itemsize for a, _, _ in ins)
    for shape, kind, _, _ in outs:
        count = 1
        for extent in shape:
            count *= extent
        total += count * jnp.dtype(kind).itemsize

    def spec(block, index):
        if isinstance(block, tuple):
            return pl.BlockSpec(block, index)
        return pl.BlockSpec(memory_space=block)

    in_specs = [spec(block, index) for _, block, index in ins]
    arrays = [a for a, _, _ in ins]
    if reuse is not None:
        in_specs.append(pl.BlockSpec(memory_space=pl.ANY))
        arrays.append(reuse)
    return pl.pallas_call(
        kernel,
        grid_spec=pltpu.PrefetchScalarGridSpec(
            num_scalar_prefetch=1,
            grid=grid,
            in_specs=in_specs,
            out_specs=[spec(block, index) for _, _, block, index in outs],
            scratch_shapes=list(scratch),
        ),
        out_shape=[jax.ShapeDtypeStruct(shape, kind) for shape, kind, _, _ in outs],
        compiler_params=pltpu.CompilerParams(vmem_limit_bytes=mib * MIB),
        cost_estimate=cost(flops, total),
        input_output_aliases={} if reuse is None else {1 + len(ins): 0},
    )(place, *arrays)


def resident(kernel, ins, outs, place, mib=16, flops=0, scratch=()):
    return call(
        kernel,
        (),
        [(a, pltpu.VMEM, None) for a in ins],
        [(shape, kind, pltpu.VMEM, None) for shape, kind in outs],
        place,
        mib=mib,
        flops=flops,
        scratch=scratch,
    )


def step_of(extent):
    return 256 if extent % 256 == 0 else 128


def tiles(extent, body):
    size = step_of(extent)

    def step(i, carry):
        body(pl.multiple_of(i * size, size))
        return carry

    lax.fori_loop(0, extent // size, step, 0)


def whole2(*_):
    return (0, 0)


def whole3(*_):
    return (0, 0, 0)


def whole4(*_):
    return (0, 0, 0, 0)


def pack(place, parts):
    rows = sum(part.shape[0] for part in parts)

    def kernel(place_ref, *refs):
        start = 0
        for ref in refs[:-1]:
            refs[-1][start : start + ref.shape[0], :] = ref[...]
            start += ref.shape[0]

    return resident(kernel, parts, [((rows, parts[0].shape[1]), parts[0].dtype)], place)[0]


def dequant(place, codes, low, high, halves=1):
    count, height, cols = codes.shape
    groups = low.shape[1]
    size = height // groups
    held = groups // halves

    def kernel(place_ref, code_ref, low_ref, high_ref, out_ref):
        def block(i, carry):
            base = moved(i, held, place_ref) if halves > 1 else i
            source = pl.multiple_of(base * size, size)
            to = pl.multiple_of(i * size, size)
            for k in range(count):
                bottom = low_ref[k, pl.ds(base, 1), :]
                scale = (high_ref[k, pl.ds(base, 1), :] - bottom) * (1.0 / 255.0)
                vals = code_ref[k, pl.ds(source, size), :].astype(F32)
                out_ref[pl.ds(to, size), k * cols : (k + 1) * cols] = (
                    bottom + scale * vals
                ).astype(BF16)
            return carry

        lax.fori_loop(0, groups, block, 0)

    return resident(
        kernel, [codes, low, high], [((height, count * cols), BF16)], place
    )[0]


def hidden_rows(total_groups, size, halves):
    per = total_groups // halves
    while per > 3:
        per = next(f for f in range(2, per + 1) if per % f == 0) and per // next(
            f for f in range(2, per + 1) if per % f == 0
        )
    return per, per * size


def forward_in(place, x_own, x_other, w_in):
    rows = x_own.shape[0]
    width, both = w_in.shape
    hidden = both // 2
    size = step_of(hidden)

    def kernel(place_ref, own_ref, other_ref, w_ref, hidden_ref, slope_ref, act_ref):
        x = jnp.concatenate([own_ref[...], other_ref[...]], axis=0)

        def body(start):
            gate = dot(x, w_ref[:, pl.ds(start, size)])
            up = dot(x, w_ref[:, pl.ds(pl.multiple_of(hidden + start, size), size)])
            sig = 1.0 / (1.0 + jnp.exp(-gate))
            act = gate * sig
            hidden_ref[:, pl.ds(start, size)] = (act * up).astype(BF16)
            slope_ref[:, pl.ds(start, size)] = up * sig * (1.0 + gate * (1.0 - sig))
            act_ref[:, pl.ds(start, size)] = act

        tiles(hidden, body)

    shape = (2 * rows, hidden)
    return resident(
        kernel,
        [x_own, x_other, w_in],
        [(shape, BF16), (shape, F32), (shape, F32)],
        place,
        flops=4 * rows * width * both,
    )


def route_weight(extra, place_ref, experts):
    lane = lax.broadcasted_iota(jnp.int32, extra.shape, 1)
    me = place_ref[0]
    named = (lane == me) | (lane == me + experts) | (lane == me + 2 * experts)
    return jnp.sum(jnp.where(named, extra.astype(F32), 0.0), axis=1, keepdims=True)


def forward_down(place, hidden, w_down, terms, c):
    experts = lax.axis_size("expert")
    rows = hidden[0].shape[0] // 2
    height, quarter = w_down.shape
    size = step_of(quarter)
    held = slice(c * rows, (c + 1) * rows)

    def kernel(place_ref, *refs):
        *hidden_refs, w_ref, own_ref, other_ref, out_own_ref, out_other_ref = refs
        left = jnp.concatenate([ref[...] for ref in hidden_refs], axis=1)
        own = route_weight(own_ref[held, :], place_ref, experts)
        other = route_weight(other_ref[held, :], place_ref, experts)

        def body(start):
            total = dot(left, w_ref[:, pl.ds(start, size)])
            out_own_ref[:, pl.ds(start, size)] = (own * total[:rows]).astype(BF16)
            out_other_ref[:, pl.ds(start, size)] = (other * total[rows:]).astype(BF16)

        tiles(quarter, body)

    return resident(
        kernel,
        [*hidden, w_down, *terms],
        [((rows, quarter), BF16)] * 2,
        place,
        flops=4 * rows * height * quarter,
    )


def backward_down(place, err_own, err_other, w_down, terms, c, halves):
    experts = lax.axis_size("expert")
    rows, quarter = err_own.shape
    height = w_down.shape[0]
    own = height // halves
    size = step_of(own)
    held = slice(c * rows, (c + 1) * rows)

    def kernel(place_ref, err_own_ref, err_other_ref, own_ref, other_ref, w_ref, grad_ref, *outs):
        weight = route_weight(own_ref[held, :], place_ref, experts)
        grad_ref[:rows, :] = (weight * err_own_ref[...].astype(F32)).astype(BF16)
        weight = route_weight(other_ref[held, :], place_ref, experts)
        grad_ref[rows:, :] = (weight * err_other_ref[...].astype(F32)).astype(BF16)
        for d in reversed(range(halves)):

            def body(start):
                at = pl.multiple_of(d * own + start, size)
                part = dot_cols(grad_ref[...], w_ref[pl.ds(at, size), :])
                outs[d][:, pl.ds(start, size)] = part.astype(outs[d].dtype)

            tiles(own, body)

    shape = (2 * rows, own)
    return resident(
        kernel,
        [err_own, err_other, *terms, w_down],
        [((2 * rows, quarter), BF16), (shape, F32)] + [(shape, BF16)] * (halves - 1),
        place,
        flops=4 * rows * height * quarter,
    )


def backward_hidden(place, grad_own, arrived, slope, act, w_in, halves):
    both_rows, hidden = slope.shape
    rows = both_rows // 2
    quarter = w_in.shape[0] // halves
    size = step_of(quarter)
    count = len(arrived)

    def kernel(place_ref, grad_own_ref, *refs):
        arrived_refs = refs[:count]
        slope_ref, act_ref, w_ref, grad_ref, *outs = refs[count:]
        grad_hidden = grad_own_ref[...]
        for ref in arrived_refs:
            grad_hidden += ref[...].astype(F32)
        grad_ref[:, :hidden] = (grad_hidden * slope_ref[...]).astype(BF16)
        grad_ref[:, hidden:] = (grad_hidden * act_ref[...]).astype(BF16)
        for d in range(halves):

            def body(start):
                at = pl.multiple_of((place_ref[1] ^ d) * quarter + start, size)
                part = dot_cols(grad_ref[...], w_ref[pl.ds(at, size), :]).astype(BF16)
                outs[2 * d][:, pl.ds(start, size)] = part[:rows]
                outs[2 * d + 1][:, pl.ds(start, size)] = part[rows:]

            tiles(quarter, body)

    grad, *parts = resident(
        kernel,
        [grad_own, *arrived, slope, act, w_in],
        [((both_rows, 2 * hidden), BF16)] + [((rows, quarter), BF16)] * (2 * halves),
        place,
        flops=4 * both_rows * hidden * quarter * halves,
    )
    return grad, parts


def ends(grad, codes):
    upper = jnp.sum(grad * codes.astype(F32), axis=0, keepdims=True) * (1.0 / 255.0)
    return jnp.sum(grad, axis=0, keepdims=True) - upper, upper


def range_tile(left, right, size, step, codes, store):
    turned = left.T
    for start in range(0, right.shape[1], step):
        cols = slice(start, start + step)
        grad = dot(turned, right[:, cols])
        for g in range(turned.shape[0] // size):
            cut = slice(g * size, (g + 1) * size)
            low, high = ends(grad[cut], codes(cut, cols))
            store(g, cols, low, high)


def ranges_down(place, hidden, grads, codes, groups, halves):
    _, height, quarter = codes.shape
    size = height // groups
    per, rows = hidden_rows(groups, size, halves)
    blocks = height // halves // rows
    flat = [part for parts in hidden for part in parts]
    chunks = len(grads)
    tokens = grads[0].shape[0]

    def kernel(place_ref, *refs):
        hidden_refs = refs[: len(flat)]
        grad_refs = refs[len(flat) : len(flat) + chunks]
        code_ref, out_ref, right_ref = refs[len(flat) + chunks :]
        step = pl.program_id(0)
        base = moved(step, blocks, place_ref) * per

        @pl.when(step == 0)
        def _():
            for c in range(chunks):
                right_ref[c * tokens : (c + 1) * tokens, :] = grad_refs[c][...]

        def store(g, cols, low, high):
            out_ref[0, pl.ds(base + g, 1), cols] = low
            out_ref[1, pl.ds(base + g, 1), cols] = high

        for d in range(halves):

            @pl.when(step // blocks == d)
            def _():
                left = [hidden_refs[c * halves + d][...] for c in range(chunks)]
                range_tile(
                    jnp.concatenate(left, axis=0),
                    right_ref,
                    size,
                    step_of(quarter),
                    lambda cut, cols: code_ref[0, cut, cols],
                    store,
                )

    shape = (2, groups, quarter)
    return call(
        kernel,
        (height // rows,),
        [(part, (part.shape[0], rows), lambda i, p: (0, i % blocks)) for part in flat]
        + [(grad, pltpu.VMEM, None) for grad in grads]
        + [(codes, (1, rows, quarter), lambda i, p: (0, moved(i, blocks, p), 0))],
        [(shape, F32, shape, whole3)],
        place,
        scratch=[pltpu.VMEM((chunks * tokens, quarter), BF16)],
        mib=20,
        flops=2 * sum(g.shape[0] for g in grads) * height * quarter,
    )[0]


def ranges_in(place, x, grads, codes, groups, part, parts, found):
    _, _, width, hidden = codes.shape
    size = width // groups
    held = groups // parts
    per = next(p for p in (4, 2, 1) if held % p == 0)
    rows = per * size
    blocks = held // per
    flat = [array for pair in x for array in pair]
    chunks = len(grads)
    tokens, both = grads[0].shape
    wide = 256 if hidden % 256 == 0 else hidden

    def kernel(place_ref, *refs):
        x_refs = refs[: len(flat)]
        grad_refs = refs[len(flat) : len(flat) + chunks]
        code_ref, out_ref, right_ref = refs[len(flat) + chunks], refs[-2], refs[-1]
        base = pl.program_id(0) * per

        @pl.when(pl.program_id(0) == 0)
        def _():
            for c in range(chunks):
                right_ref[c * tokens : (c + 1) * tokens, :] = grad_refs[c][...]

        def split(cols):
            k = cols.start // hidden
            return k, slice(cols.start - k * hidden, cols.stop - k * hidden)

        def codes_at(cut, cols):
            k, cols = split(cols)
            return code_ref[0, k, cut, cols]

        def store(g, cols, low, high):
            k, cols = split(cols)
            out_ref[2 * k, pl.ds(base + g, 1), cols] = low
            out_ref[2 * k + 1, pl.ds(base + g, 1), cols] = high

        left = jnp.concatenate([ref[...] for ref in x_refs], axis=0)
        range_tile(left, right_ref, size, wide, codes_at, store)

    shape = (4, groups, hidden)
    return call(
        kernel,
        (blocks,),
        [(a, (a.shape[0], rows), lambda i, p: (0, part * blocks + i)) for a in flat]
        + [(grad, pltpu.VMEM, None) for grad in grads]
        + [(codes, (1, 2, rows, hidden), lambda i, p: (0, 0, part * blocks + i, 0))],
        [(shape, F32, (4, held, hidden), lambda i, p: (0, part, 0))],
        place,
        scratch=[pltpu.VMEM((chunks * tokens, both), BF16)],
        mib=20,
        flops=2 * sum(grad.size for grad in grads) * (width // parts),
        reuse=found,
    )[0]


def prepare(place, routes, route_scores, extra):
    experts = lax.axis_size("expert")
    rows, top_count = routes.shape

    def kernel(place_ref, route_ref, score_ref, out_ref):
        scores = score_ref[...]
        weights = scores / jnp.sum(scores, axis=1, keepdims=True)
        names = route_ref[...]
        lane = lax.broadcasted_iota(jnp.int32, (rows, extra), 1)
        third = jnp.where(lane < experts, 0, jnp.where(lane < 2 * experts, 1, 2))
        expert = lane - third * experts
        table = jnp.zeros((rows, extra), F32)
        for k in range(top_count):
            table += jnp.where(expert == names[:, k : k + 1], weights[:, k : k + 1], 0.0)
        top = table.astype(BF16).astype(F32)
        middle = (table - top).astype(BF16).astype(F32)
        bottom = table - top - middle
        terms = jnp.where(third == 0, top, jnp.where(third == 1, middle, bottom))
        out_ref[...] = terms.astype(BF16)

    return resident(kernel, [routes, route_scores], [((rows, extra), BF16)], place)[0]


def local(
    tokens, target, routes, route_scores, in_codes, in_low, in_high, down_codes, down_low, down_high
):
    experts = lax.axis_size("expert")
    halves = lax.axis_size("half")
    place = jnp.stack([lax.axis_index("expert"), lax.axis_index("half")]).astype(jnp.int32)
    quarter = target.shape[1]
    parts = range(halves)
    chunks = (0, 1)

    near_own = swap(tokens, "expert", 4)
    across = [swap(tokens, "expert", 2)]
    far = join(gather_far(tokens)[1:])
    w_in = dequant(place, in_codes[0], in_low[0], in_high[0])
    near_own = tie(near_own, w_in)
    far = tie(far, w_in, across[0])
    near_far = swap(far, "expert", 4)
    across += [swap(near_own, "expert", 2), swap(far, "expert", 2)]
    w_down = dequant(place, down_codes, tie(down_low, far), down_high, halves)
    extra = -(-3 * experts // 128) * 128
    terms = join(gather_far(prepare(place, tie(routes, w_in), route_scores, extra)))
    near_far = tie(near_far, w_down, terms, across[1])
    near_terms = swap(terms, "expert", 4)
    across.append(swap(near_far, "expert", 2))
    first = pack(place, [tokens, far, near_own, near_far])
    x = [(first, tie(swap(first, "expert", 1), across[2]))]

    hidden, slope, act = [], [], []
    for c in chunks:
        if c == 1:
            across[3] = tie(across[3], hidden[0][0], near_terms)
            second = pack(place, [across[i] for i in (0, 2, 1, 3)])
            x.append((second, swap(second, "expert", 1)))
        own, chunk_slope, chunk_act = forward_in(place, *x[c], w_in)
        hidden.append([own] + [swap(own, "half", d) for d in parts if d])
        slope.append(chunk_slope)
        act.append(chunk_act)
    terms = jnp.concatenate([terms, near_terms], axis=0)
    terms = jnp.concatenate([terms, swap(terms, "expert", 2)], axis=0)
    terms = (terms, swap(terms, "expert", 1))

    sums = []
    for c in chunks:
        if c == 1:
            hidden[1][1:] = [tie(part, sums[0][0]) for part in hidden[1][1:]]
        out_own, out_other = forward_down(place, hidden[c], w_down, terms, c)
        sums.append([out_own, swap(out_other, "expert", 1)])
    mixed = scatter_rows(sums[0], sums[1])
    error = (mixed - target.astype(F32)).astype(BF16)

    kept = join(gather_far(error))
    near = swap(kept, "expert", 4)
    across = [swap(kept, "expert", 2)]
    near = tie(near, across[0])
    across.append(swap(near, "expert", 2))
    first = pack(place, [kept, near])
    errors = [(first, swap(first, "expert", 1))]
    grads, grad_own, arrived = [], [], []
    for c in chunks:
        if c == 1:
            second = pack(place, [across[0], tie(across[1], grads[0])])
            errors.append((second, swap(second, "expert", 1)))
        grad, own, *others = backward_down(place, *errors[c], w_down, terms, c, halves)
        grads.append(grad)
        grad_own.append(own)
        arrived.append([swap(other, "half", d + 1) for d, other in enumerate(others)])

    grad_in, kinds = [], []
    arrived[0] = [tie(part, grads[1]) for part in arrived[0]]
    for c in chunks:
        if c == 1:
            arrived[1] = [tie(part, grad_in[0]) for part in arrived[1]]
        grad, found = backward_hidden(
            place, grad_own[c], arrived[c], slope[c], act[c], w_in, halves
        )
        grad_in.append(grad)
        kinds.append(found)
    kinds[0] = [tie(part, grad_in[1]) for part in kinds[0]]
    lower, upper = slice(0, first.shape[0] // 2), slice(first.shape[0] // 2, first.shape[0])
    keep, go = [
        [[found[2 * d], swap(found[2 * d + 1], "expert", 1)] for d in parts] for found in kinds
    ]
    stay, leave = keep[0], go[0]
    outer = [(d, keep[d]) for d in parts if d]
    crossed = [
        (
            swap(add([part[upper] for part in go[d]]).astype(BF16), "half", d),
            swap(add([part[lower] for part in go[d]]).astype(BF16), "expert", 2),
        )
        for d in parts
        if d
    ]
    by_half = [pair[0] for pair in crossed]
    across_upper = swap(
        add([part[upper] for part in leave] + by_half).astype(BF16), "expert", 2
    )
    arrived_upper = [
        swap(tie(add([part[upper] for part in keep]).astype(BF16), *by_half), "half", d)
        for d, keep in outer
    ]
    near = swap(
        add([part[upper] for part in stay] + arrived_upper + [across_upper]).astype(BF16),
        "expert",
        4,
    )
    across_lower = swap(
        tie(add([part[lower] for part in leave]).astype(BF16), across_upper), "expert", 2
    )
    arrived_lower = [
        swap(
            tie(
                add([part[lower] for part in keep] + [pair[1]]).astype(BF16), *arrived_upper
            ),
            "half",
            d,
        )
        for (d, keep), pair in zip(outer, crossed)
    ]
    grad_tokens = scatter_far(
        [part[lower] for part in stay] + arrived_lower + [across_lower, near]
    )

    grads = [tie(grad, *grad_in) for grad in grads]
    down_grad = ranges_down(place, hidden, grads, down_codes, down_low.shape[1], halves)
    in_grad = None
    pieces = 2
    for part in range(pieces):
        in_grad = ranges_in(place, x, grad_in, in_codes, in_low.shape[2], part, pieces, in_grad)
    return (grad_tokens.astype(BF16), in_grad[None], down_grad[None])


def solution(mesh):
    placed = (
        P("expert", None),
        P("expert", "half"),
        P("expert", None),
        P("expert", None),
        P("expert", None, None, "half"),
        P("expert", None, None, "half"),
        P("expert", None, None, "half"),
        P("expert", None, "half"),
        P("expert", None, "half"),
        P("expert", None, "half"),
    )
    return jax.shard_map(
        local,
        mesh=mesh,
        in_specs=placed,
        out_specs=(
            P("expert", "half"),
            P("expert", None, None, "half"),
            P("expert", None, None, "half"),
        ),
        check_vma=False,
    )
```

```python
import functools

import jax
import jax.numpy as jnp
from jax import lax
from jax.experimental import pallas as pl
from jax.experimental.pallas import tpu as pltpu
from jax.sharding import PartitionSpec as P

BF16 = jnp.bfloat16
F32 = jnp.float32
MIB = 1 << 20


def swap(array, axis, distance):
    size = lax.axis_size(axis)
    return lax.ppermute(array, axis, [(i, i ^ distance) for i in range(size)])


def tie(array, *others):
    return lax.optimization_barrier((array, *others))[0]


def far_distances():
    experts = lax.axis_size("expert")
    distances = []
    distance = experts // 2
    while distance > 4:
        distances.append(distance)
        distance //= 2
    return distances


def join(parts):
    return parts[0] if len(parts) == 1 else jnp.concatenate(parts, axis=0)


def gather_far(block):
    parts = [block]
    for distance in far_distances():
        parts.append(swap(join(parts), "expert", distance))
    return parts


def add(parts):
    total = parts[0].astype(F32)
    for part in parts[1:]:
        total = total + part.astype(F32)
    return total


def scatter_far(terms):
    for distance in reversed(far_distances()):
        half = terms[0].shape[0] // 2
        sent = swap(add([part[half:] for part in terms]).astype(BF16), "expert", distance)
        terms = [part[:half] for part in terms] + [sent]
    return add(terms)


def scatter_rows(near, across, cuts):
    rows = near[0].shape[0] // 2
    upper = [swap(add([part[rows:, cut] for part in across]).astype(BF16), "expert", 2) for cut in cuts]
    sent = [
        swap(add([part[rows:, cut] for part in near] + [part_of]).astype(BF16), "expert", 4)
        for cut, part_of in zip(cuts, upper)
    ]
    lower = swap(tie(add([part[:rows] for part in across]).astype(BF16), *upper), "expert", 2)
    return [
        scatter_far([part[:rows, cut] for part in near] + [lower[:, cut], part_of])
        for cut, part_of in zip(cuts, sent)
    ]


def dot(left, right):
    return jnp.dot(left, right, preferred_element_type=F32)


def dot_cols(left, right):
    return lax.dot_general(left, right, (((1,), (1,)), ((), ())), preferred_element_type=F32)


def dot_rows(left, right):
    return lax.dot_general(left, right, (((0,), (0,)), ((), ())), preferred_element_type=F32)


def cost(flops, bytes_accessed):
    return pl.CostEstimate(flops=int(flops), bytes_accessed=int(bytes_accessed), transcendentals=0)


def moved(step, blocks, place):
    return ((step // blocks) ^ place[1]) * blocks + step % blocks


def call(kernel, grid, ins, outs, place, scratch=(), mib=16, flops=0, reuse=None):
    total = sum(a.size * a.dtype.itemsize for a, _, _ in ins)
    for shape, kind, _, _ in outs:
        count = 1
        for extent in shape:
            count *= extent
        total += count * jnp.dtype(kind).itemsize

    def spec(block, index):
        if isinstance(block, tuple):
            return pl.BlockSpec(block, index)
        return pl.BlockSpec(memory_space=block)

    in_specs = [spec(block, index) for _, block, index in ins]
    arrays = [a for a, _, _ in ins]
    if reuse is not None:
        in_specs.append(pl.BlockSpec(memory_space=pl.ANY))
        arrays.append(reuse)
    return pl.pallas_call(
        kernel,
        grid_spec=pltpu.PrefetchScalarGridSpec(
            num_scalar_prefetch=1,
            grid=grid,
            in_specs=in_specs,
            out_specs=[spec(block, index) for _, _, block, index in outs],
            scratch_shapes=list(scratch),
        ),
        out_shape=[jax.ShapeDtypeStruct(shape, kind) for shape, kind, _, _ in outs],
        compiler_params=pltpu.CompilerParams(vmem_limit_bytes=mib * MIB),
        cost_estimate=cost(flops, total),
        input_output_aliases={} if reuse is None else {1 + len(ins): 0},
    )(place, *arrays)


def resident(kernel, ins, outs, place, mib=16, flops=0, scratch=()):
    return call(
        kernel,
        (),
        [(a, pltpu.VMEM, None) for a in ins],
        [(shape, kind, pltpu.VMEM, None) for shape, kind in outs],
        place,
        mib=mib,
        flops=flops,
        scratch=scratch,
    )


def step_of(extent):
    return next(size for size in (512, 256, 128) if extent % size == 0)


def tiles(extent, body):
    size = step_of(extent)
    for start in range(0, extent, size):
        body(start)


def whole2(*_):
    return (0, 0)


def whole3(*_):
    return (0, 0, 0)


def whole4(*_):
    return (0, 0, 0, 0)


def pack(place, parts):
    rows = sum(line[0].shape[0] for line in parts)
    cols = sum(part.shape[1] for part in parts[0])

    def kernel(place_ref, *refs):
        refs, out_ref = list(refs[:-1]), refs[-1]
        row = 0
        for line in parts:
            col = 0
            for part in line:
                height, width = part.shape
                out_ref[row : row + height, col : col + width] = refs.pop(0)[...]
                col += width
            row += line[0].shape[0]

    flat = [part for line in parts for part in line]
    return resident(kernel, flat, [((rows, cols), parts[0][0].dtype)], place)[0]


def dequant(place, codes, low, high, halves=1):
    count, height, cols = codes.shape
    groups = low.shape[1]
    size = height // groups
    held = groups // halves

    def kernel(place_ref, code_ref, low_ref, high_ref, out_ref):
        def block(i, carry):
            base = moved(i, held, place_ref) if halves > 1 else i
            source = pl.multiple_of(base * size, size)
            to = pl.multiple_of(i * size, size)
            for k in range(count):
                bottom = low_ref[k, pl.ds(base, 1), :]
                scale = (high_ref[k, pl.ds(base, 1), :] - bottom) * (1.0 / 255.0)
                vals = code_ref[k, pl.ds(source, size), :].astype(F32)
                out_ref[pl.ds(to, size), k * cols : (k + 1) * cols] = (
                    bottom + scale * vals
                ).astype(BF16)
            return carry

        lax.fori_loop(0, groups, block, 0)

    return resident(
        kernel, [codes, low, high], [((height, count * cols), BF16)], place
    )[0]


def hidden_rows(total_groups, size, halves):
    per = total_groups // halves
    while per > 3:
        per = next(f for f in range(2, per + 1) if per % f == 0) and per // next(
            f for f in range(2, per + 1) if per % f == 0
        )
    return per, per * size


def forward_in(place, x_own, x_other, w_in):
    rows = x_own.shape[0]
    width, both = w_in.shape
    hidden = both // 2
    size = step_of(hidden)

    def kernel(place_ref, own_ref, other_ref, w_ref, hidden_ref, slope_ref, act_ref):
        x = jnp.concatenate([own_ref[...], other_ref[...]], axis=0)

        def body(start):
            gate = dot(x, w_ref[:, pl.ds(start, size)])
            up = dot(x, w_ref[:, pl.ds(hidden + start, size)])
            sig = 1.0 / (1.0 + jnp.exp(-gate))
            act = gate * sig
            hidden_ref[:, pl.ds(start, size)] = (act * up).astype(BF16)
            slope_ref[:, pl.ds(start, size)] = up * sig * (1.0 + gate * (1.0 - sig))
            act_ref[:, pl.ds(start, size)] = act

        tiles(hidden, body)

    shape = (2 * rows, hidden)
    return resident(
        kernel,
        [x_own, x_other, w_in],
        [(shape, BF16), (shape, F32), (shape, F32)],
        place,
        flops=4 * rows * width * both,
    )


def route_weight(extra, place_ref, experts):
    lane = lax.broadcasted_iota(jnp.int32, extra.shape, 1)
    me = place_ref[0]
    named = (lane == me) | (lane == me + experts) | (lane == me + 2 * experts)
    return jnp.sum(jnp.where(named, extra.astype(F32), 0.0), axis=1, keepdims=True)


def forward_down(place, hidden, w_down, terms, c):
    experts = lax.axis_size("expert")
    rows = hidden[0].shape[0] // 2
    height, quarter = w_down.shape
    size = step_of(quarter)
    held = slice(c * rows, (c + 1) * rows)

    def kernel(place_ref, *refs):
        *hidden_refs, w_ref, own_ref, other_ref, out_own_ref, out_other_ref = refs
        left = jnp.concatenate([ref[...] for ref in hidden_refs], axis=1)
        own = route_weight(own_ref[held, :], place_ref, experts)
        other = route_weight(other_ref[held, :], place_ref, experts)

        def body(start):
            total = dot(left, w_ref[:, pl.ds(start, size)])
            out_own_ref[:, pl.ds(start, size)] = (own * total[:rows]).astype(BF16)
            out_other_ref[:, pl.ds(start, size)] = (other * total[rows:]).astype(BF16)

        tiles(quarter, body)

    return resident(
        kernel,
        [*hidden, w_down, *terms],
        [((rows, quarter), BF16)] * 2,
        place,
        flops=4 * rows * height * quarter,
    )


def backward_down(place, err_own, err_other, w_down, terms, c, halves):
    experts = lax.axis_size("expert")
    rows, quarter = err_own.shape
    height = w_down.shape[0]
    own = height // halves
    size = step_of(own)
    held = slice(c * rows, (c + 1) * rows)

    def kernel(place_ref, err_own_ref, err_other_ref, own_ref, other_ref, w_ref, grad_ref, *outs):
        weight = route_weight(own_ref[held, :], place_ref, experts)
        grad_ref[:rows, :] = (weight * err_own_ref[...].astype(F32)).astype(BF16)
        weight = route_weight(other_ref[held, :], place_ref, experts)
        grad_ref[rows:, :] = (weight * err_other_ref[...].astype(F32)).astype(BF16)
        for d in reversed(range(halves)):

            def body(start):
                at = d * own + start
                part = dot_cols(grad_ref[...], w_ref[pl.ds(at, size), :])
                outs[d][:, pl.ds(start, size)] = part.astype(outs[d].dtype)

            tiles(own, body)

    shape = (2 * rows, own)
    return resident(
        kernel,
        [err_own, err_other, *terms, w_down],
        [((2 * rows, quarter), BF16), (shape, F32)] + [(shape, BF16)] * (halves - 1),
        place,
        flops=4 * rows * height * quarter,
    )


def backward_hidden(place, grad_own, arrived, slope, act, w_in, halves):
    both_rows, hidden = slope.shape
    rows = both_rows // 2
    quarter = w_in.shape[0] // halves
    size = step_of(quarter)
    count = len(arrived)

    def kernel(place_ref, grad_own_ref, *refs):
        arrived_refs = refs[:count]
        slope_ref, act_ref, w_ref, grad_ref, *outs = refs[count:]
        grad_hidden = grad_own_ref[...]
        for ref in arrived_refs:
            grad_hidden += ref[...].astype(F32)
        grad_ref[:, :hidden] = (grad_hidden * slope_ref[...]).astype(BF16)
        grad_ref[:, hidden:] = (grad_hidden * act_ref[...]).astype(BF16)
        for d in range(halves):

            def body(start):
                at = pl.multiple_of((place_ref[1] ^ d) * quarter + start, size)
                part = dot_cols(grad_ref[...], w_ref[pl.ds(at, size), :]).astype(BF16)
                outs[2 * d][:, pl.ds(start, size)] = part[:rows]
                outs[2 * d + 1][:, pl.ds(start, size)] = part[rows:]

            tiles(quarter, body)

    grad, *parts = resident(
        kernel,
        [grad_own, *arrived, slope, act, w_in],
        [((both_rows, 2 * hidden), BF16)] + [((rows, quarter), BF16)] * (2 * halves),
        place,
        flops=4 * both_rows * hidden * quarter * halves,
    )
    return grad, parts


def ends(grad, codes):
    upper = jnp.sum(grad * codes.astype(F32), axis=0, keepdims=True) * (1.0 / 255.0)
    return jnp.sum(grad, axis=0, keepdims=True) - upper, upper


def range_tile(left, right, size, step, codes, store):
    turned = left.T
    for start in range(0, right.shape[1], step):
        cols = slice(start, start + step)
        grad = dot(turned, right[:, cols])
        for g in range(turned.shape[0] // size):
            cut = slice(g * size, (g + 1) * size)
            low, high = ends(grad[cut], codes(cut, cols))
            store(g, cols, low, high)


def ranges_down(place, hidden, grads, codes, groups, halves):
    _, height, quarter = codes.shape
    size = height // groups
    per, rows = hidden_rows(groups, size, halves)
    blocks = height // halves // rows
    flat = [part for parts in hidden for part in parts]
    chunks = len(grads)
    tokens = grads[0].shape[0]

    def kernel(place_ref, *refs):
        hidden_refs = refs[: len(flat)]
        grad_refs = refs[len(flat) : len(flat) + chunks]
        code_ref, out_ref, right_ref = refs[len(flat) + chunks :]
        step = pl.program_id(0)
        base = moved(step, blocks, place_ref) * per

        @pl.when(step == 0)
        def _():
            for c in range(chunks):
                right_ref[c * tokens : (c + 1) * tokens, :] = grad_refs[c][...]

        def store(g, cols, low, high):
            out_ref[0, pl.ds(base + g, 1), cols] = low
            out_ref[1, pl.ds(base + g, 1), cols] = high

        for d in range(halves):

            @pl.when(step // blocks == d)
            def _():
                left = [hidden_refs[c * halves + d][...] for c in range(chunks)]
                range_tile(
                    jnp.concatenate(left, axis=0),
                    right_ref,
                    size,
                    256,
                    lambda cut, cols: code_ref[0, cut, cols],
                    store,
                )

    shape = (2, groups, quarter)
    return call(
        kernel,
        (height // rows,),
        [(part, (part.shape[0], rows), lambda i, p: (0, i % blocks)) for part in flat]
        + [(grad, pltpu.VMEM, None) for grad in grads]
        + [(codes, (1, rows, quarter), lambda i, p: (0, moved(i, blocks, p), 0))],
        [(shape, F32, shape, whole3)],
        place,
        scratch=[pltpu.VMEM((chunks * tokens, quarter), BF16)],
        mib=20,
        flops=2 * sum(g.shape[0] for g in grads) * height * quarter,
    )[0]


def ranges_in(place, x, grads, codes, groups, part, parts, found):
    _, _, width, hidden = codes.shape
    size = width // groups
    held = groups // parts
    per = next(p for p in (4, 2, 1) if held % p == 0)
    rows = per * size
    blocks = held // per
    flat = [array for pair in x for array in pair]
    chunks = len(grads)
    tokens, both = grads[0].shape
    wide = 256 if hidden % 256 == 0 else hidden

    def kernel(place_ref, *refs):
        x_refs = refs[: len(flat)]
        grad_refs = refs[len(flat) : len(flat) + chunks]
        code_ref, out_ref, right_ref = refs[len(flat) + chunks], refs[-2], refs[-1]
        base = pl.program_id(0) * per

        @pl.when(pl.program_id(0) == 0)
        def _():
            for c in range(chunks):
                right_ref[c * tokens : (c + 1) * tokens, :] = grad_refs[c][...]

        def split(cols):
            k = cols.start // hidden
            return k, slice(cols.start - k * hidden, cols.stop - k * hidden)

        def codes_at(cut, cols):
            k, cols = split(cols)
            return code_ref[0, k, cut, cols]

        def store(g, cols, low, high):
            k, cols = split(cols)
            out_ref[2 * k, pl.ds(base + g, 1), cols] = low
            out_ref[2 * k + 1, pl.ds(base + g, 1), cols] = high

        left = jnp.concatenate([ref[...] for ref in x_refs], axis=0)
        range_tile(left, right_ref, size, wide, codes_at, store)

    shape = (4, groups, hidden)
    return call(
        kernel,
        (blocks,),
        [(a, (a.shape[0], rows), lambda i, p: (0, part * blocks + i)) for a in flat]
        + [(grad, pltpu.VMEM, None) for grad in grads]
        + [(codes, (1, 2, rows, hidden), lambda i, p: (0, 0, part * blocks + i, 0))],
        [(shape, F32, (4, held, hidden), lambda i, p: (0, part, 0))],
        place,
        scratch=[pltpu.VMEM((chunks * tokens, both), BF16)],
        mib=20,
        flops=2 * sum(grad.size for grad in grads) * (width // parts),
        reuse=found,
    )[0]


def prepare(place, routes, route_scores, extra):
    experts = lax.axis_size("expert")
    rows, top_count = routes.shape

    def kernel(place_ref, route_ref, score_ref, out_ref):
        scores = score_ref[...]
        weights = scores / jnp.sum(scores, axis=1, keepdims=True)
        names = route_ref[...]
        lane = lax.broadcasted_iota(jnp.int32, (rows, extra), 1)
        third = jnp.where(lane < experts, 0, jnp.where(lane < 2 * experts, 1, 2))
        expert = lane - third * experts
        table = jnp.zeros((rows, extra), F32)
        for k in range(top_count):
            table += jnp.where(expert == names[:, k : k + 1], weights[:, k : k + 1], 0.0)
        top = table.astype(BF16).astype(F32)
        middle = (table - top).astype(BF16).astype(F32)
        bottom = table - top - middle
        terms = jnp.where(third == 0, top, jnp.where(third == 1, middle, bottom))
        out_ref[...] = terms.astype(BF16)

    return resident(kernel, [routes, route_scores], [((rows, extra), BF16)], place)[0]


def local(
    tokens, target, routes, route_scores, in_codes, in_low, in_high, down_codes, down_low, down_high
):
    experts = lax.axis_size("expert")
    halves = lax.axis_size("half")
    place = jnp.stack([lax.axis_index("expert"), lax.axis_index("half")]).astype(jnp.int32)
    quarter = target.shape[1]
    parts = range(halves)
    chunks = (0, 1)

    far = join(gather_far(tokens)[1:])
    near_own = swap(tokens, "expert", 4)
    across = [swap(tokens, "expert", 2)]
    w_in = dequant(place, in_codes[0], in_low[0], in_high[0])
    w_down = dequant(place, down_codes, tie(down_low, w_in), down_high, halves)
    far = tie(far, w_in, w_down, across[0])
    near_far = swap(far, "expert", 4)
    middle = pack(place, [[far], [near_own]])
    across.append(swap(middle, "expert", 2))
    extra = -(-3 * experts // 128) * 128
    terms = join(gather_far(prepare(place, tie(routes, far), route_scores, extra)))
    near_far = tie(near_far, across[1], terms)
    across.append(swap(near_far, "expert", 2))
    first = pack(place, [[tokens], [middle], [near_far]])
    x = [(first, swap(first, "expert", 1))]
    near_terms = swap(terms, "expert", 4)

    hidden, slope, act = [], [], []
    for c in chunks:
        if c == 1:
            across[2] = tie(across[2], hidden[0][0], near_terms)
            second = pack(place, [[part] for part in across])
            x.append((second, swap(second, "expert", 1)))
        own, chunk_slope, chunk_act = forward_in(place, *x[c], w_in)
        hidden.append([own] + [swap(own, "half", d) for d in parts if d])
        slope.append(chunk_slope)
        act.append(chunk_act)
    terms = jnp.concatenate([terms, near_terms], axis=0)
    terms = jnp.concatenate([terms, swap(terms, "expert", 2)], axis=0)
    terms = (terms, swap(terms, "expert", 1))

    sums = []
    for c in chunks:
        if c == 1:
            hidden[1][1:] = [tie(part, sums[0][0]) for part in hidden[1][1:]]
        out_own, out_other = forward_down(place, hidden[c], w_down, terms, c)
        sums.append([out_own, swap(out_other, "expert", 1)])
    middle = quarter // 2
    cuts = [slice(0, middle), slice(middle, quarter)]
    mixed = scatter_rows(sums[0], sums[1], cuts)
    error = [
        (mixed[f] - target[:, cuts[f]].astype(F32)).astype(BF16) for f in range(len(cuts))
    ]

    kept = [gather_far(part) for part in error]
    near = [swap(join(part), "expert", 4) for part in kept]
    kept = pack(place, [list(line) for line in zip(*kept)])
    across = swap(kept, "expert", 2)
    near = [tie(part, across) for part in near]
    near_across = [swap(part, "expert", 2) for part in near]
    first = pack(place, [[kept], near])
    errors = [(first, swap(first, "expert", 1))]
    grads, grad_own, arrived = [], [], []
    for c in chunks:
        if c == 1:
            second = pack(place, [[across], [tie(part, grads[0]) for part in near_across]])
            errors.append((second, swap(second, "expert", 1)))
        grad, own, *others = backward_down(place, *errors[c], w_down, terms, c, halves)
        grads.append(grad)
        grad_own.append(own)
        arrived.append([swap(other, "half", d + 1) for d, other in enumerate(others)])

    grad_in, kinds = [], []
    arrived[0] = [tie(part, grads[1]) for part in arrived[0]]
    for c in chunks:
        if c == 1:
            arrived[1] = [tie(part, grad_in[0]) for part in arrived[1]]
        grad, found = backward_hidden(
            place, grad_own[c], arrived[c], slope[c], act[c], w_in, halves
        )
        grad_in.append(grad)
        kinds.append(found)
    kinds[0] = [tie(part, grad_in[1]) for part in kinds[0]]
    lower, upper = slice(0, first.shape[0] // 2), slice(first.shape[0] // 2, first.shape[0])
    keep, go = [
        [[found[2 * d], swap(found[2 * d + 1], "expert", 1)] for d in parts] for found in kinds
    ]
    stay, leave = keep[0], go[0]
    outer = [(d, keep[d]) for d in parts if d]
    crossed = [
        (
            swap(add([part[upper] for part in go[d]]).astype(BF16), "half", d),
            swap(add([part[lower] for part in go[d]]).astype(BF16), "expert", 2),
        )
        for d in parts
        if d
    ]
    by_half = [pair[0] for pair in crossed]
    across_upper = swap(
        add([part[upper] for part in leave] + by_half).astype(BF16), "expert", 2
    )
    arrived_upper = [
        swap(tie(add([part[upper] for part in keep]).astype(BF16), *by_half), "half", d)
        for d, keep in outer
    ]
    near = swap(
        add([part[upper] for part in stay] + arrived_upper + [across_upper]).astype(BF16),
        "expert",
        4,
    )
    across_lower = swap(
        tie(add([part[lower] for part in leave]).astype(BF16), across_upper), "expert", 2
    )
    arrived_lower = [
        swap(
            tie(
                add([part[lower] for part in keep] + [pair[1]]).astype(BF16), *arrived_upper
            ),
            "half",
            d,
        )
        for (d, keep), pair in zip(outer, crossed)
    ]
    grad_tokens = scatter_far(
        [part[lower] for part in stay] + arrived_lower + [across_lower, near]
    )

    grads = [tie(grad, *grad_in) for grad in grads]
    down_grad = ranges_down(place, hidden, grads, down_codes, down_low.shape[1], halves)
    in_grad = None
    pieces = 2
    for part in range(pieces):
        in_grad = ranges_in(place, x, grad_in, in_codes, in_low.shape[2], part, pieces, in_grad)
    return (grad_tokens.astype(BF16), in_grad[None], down_grad[None])


def solution(mesh):
    placed = (
        P("expert", None),
        P("expert", "half"),
        P("expert", None),
        P("expert", None),
        P("expert", None, None, "half"),
        P("expert", None, None, "half"),
        P("expert", None, None, "half"),
        P("expert", None, "half"),
        P("expert", None, "half"),
        P("expert", None, "half"),
    )
    return jax.shard_map(
        local,
        mesh=mesh,
        in_specs=placed,
        out_specs=(
            P("expert", "half"),
            P("expert", None, None, "half"),
            P("expert", None, None, "half"),
        ),
        check_vma=False,
    )
```

```python
import functools

import jax
import jax.numpy as jnp
from jax import lax
from jax.experimental import pallas as pl
from jax.experimental.pallas import tpu as pltpu
from jax.sharding import PartitionSpec as P

BF16 = jnp.bfloat16
F32 = jnp.float32
MIB = 1 << 20


def swap(array, axis, distance):
    size = lax.axis_size(axis)
    return lax.ppermute(array, axis, [(i, i ^ distance) for i in range(size)])


def tie(array, *others):
    return lax.optimization_barrier((array, *others))[0]


def far_distances():
    experts = lax.axis_size("expert")
    distances = []
    distance = experts // 2
    while distance > 4:
        distances.append(distance)
        distance //= 2
    return distances


def join(parts):
    return parts[0] if len(parts) == 1 else jnp.concatenate(parts, axis=0)


def gather_far(block):
    parts = [block]
    for distance in far_distances():
        parts.append(swap(join(parts), "expert", distance))
    return parts


def add(parts):
    total = parts[0].astype(F32)
    for part in parts[1:]:
        total = total + part.astype(F32)
    return total


def scatter_far(terms):
    for distance in reversed(far_distances()):
        half = terms[0].shape[0] // 2
        sent = swap(add([part[half:] for part in terms]).astype(BF16), "expert", distance)
        terms = [part[:half] for part in terms] + [sent]
    return add(terms)


def scatter_rows(near, across, cuts):
    rows = near[0].shape[0] // 2
    upper = [swap(add([part[rows:, cut] for part in across]).astype(BF16), "expert", 2) for cut in cuts]
    sent = [
        swap(add([part[rows:, cut] for part in near] + [part_of]).astype(BF16), "expert", 4)
        for cut, part_of in zip(cuts, upper)
    ]
    lower = swap(tie(add([part[:rows] for part in across]).astype(BF16), *upper), "expert", 2)
    return [
        scatter_far([part[:rows, cut] for part in near] + [lower[:, cut], part_of])
        for cut, part_of in zip(cuts, sent)
    ]


def dot(left, right):
    return jnp.dot(left, right, preferred_element_type=F32)


def dot_cols(left, right):
    return lax.dot_general(left, right, (((1,), (1,)), ((), ())), preferred_element_type=F32)


def dot_rows(left, right):
    return lax.dot_general(left, right, (((0,), (0,)), ((), ())), preferred_element_type=F32)


def cost(flops, bytes_accessed):
    return pl.CostEstimate(flops=int(flops), bytes_accessed=int(bytes_accessed), transcendentals=0)


def moved(step, blocks, place):
    return ((step // blocks) ^ place[1]) * blocks + step % blocks


def call(kernel, grid, ins, outs, place, scratch=(), mib=16, flops=0, reuse=None, weight=1e-6):
    total = sum(a.size * a.dtype.itemsize for a, _, _ in ins)
    for shape, kind, _, _ in outs:
        count = 1
        for extent in shape:
            count *= extent
        total += count * jnp.dtype(kind).itemsize

    def spec(block, index):
        if isinstance(block, tuple):
            return pl.BlockSpec(block, index)
        return pl.BlockSpec(memory_space=block)

    in_specs = [spec(block, index) for _, block, index in ins]
    arrays = [a for a, _, _ in ins]
    if reuse is not None:
        in_specs.append(pl.BlockSpec(memory_space=pl.ANY))
        arrays.append(reuse)
    return pl.pallas_call(
        kernel,
        grid_spec=pltpu.PrefetchScalarGridSpec(
            num_scalar_prefetch=1,
            grid=grid,
            in_specs=in_specs,
            out_specs=[spec(block, index) for _, _, block, index in outs],
            scratch_shapes=list(scratch),
        ),
        out_shape=[jax.ShapeDtypeStruct(shape, kind) for shape, kind, _, _ in outs],
        compiler_params=pltpu.CompilerParams(vmem_limit_bytes=mib * MIB),
        cost_estimate=cost(flops * weight, total * weight),
        input_output_aliases={} if reuse is None else {1 + len(ins): 0},
    )(place, *arrays)


def resident(kernel, ins, outs, place, mib=16, flops=0, scratch=()):
    return call(
        kernel,
        (),
        [(a, pltpu.VMEM, None) for a in ins],
        [(shape, kind, pltpu.VMEM, None) for shape, kind in outs],
        place,
        mib=mib,
        flops=flops,
        scratch=scratch,
    )


def step_of(extent):
    return next(size for size in (512, 256, 128) if extent % size == 0)


def tiles(extent, body):
    size = step_of(extent)
    for start in range(0, extent, size):
        body(start)


def whole2(*_):
    return (0, 0)


def whole3(*_):
    return (0, 0, 0)


def whole4(*_):
    return (0, 0, 0, 0)


def pack(place, parts):
    rows = sum(line[0].shape[0] for line in parts)
    cols = sum(part.shape[1] for part in parts[0])

    def kernel(place_ref, *refs):
        refs, out_ref = list(refs[:-1]), refs[-1]
        row = 0
        for line in parts:
            col = 0
            for part in line:
                height, width = part.shape
                out_ref[row : row + height, col : col + width] = refs.pop(0)[...]
                col += width
            row += line[0].shape[0]

    flat = [part for line in parts for part in line]
    return resident(kernel, flat, [((rows, cols), parts[0][0].dtype)], place)[0]


def dequant(place, codes, low, high, halves=1):
    count, height, cols = codes.shape
    groups = low.shape[1]
    size = height // groups
    held = groups // halves

    def kernel(place_ref, code_ref, low_ref, high_ref, out_ref):
        def block(i, carry):
            base = moved(i, held, place_ref) if halves > 1 else i
            source = pl.multiple_of(base * size, size)
            to = pl.multiple_of(i * size, size)
            for k in range(count):
                bottom = low_ref[k, pl.ds(base, 1), :]
                scale = (high_ref[k, pl.ds(base, 1), :] - bottom) * (1.0 / 255.0)
                vals = code_ref[k, pl.ds(source, size), :].astype(F32)
                out_ref[pl.ds(to, size), k * cols : (k + 1) * cols] = (
                    bottom + scale * vals
                ).astype(BF16)
            return carry

        lax.fori_loop(0, groups, block, 0)

    return resident(
        kernel, [codes, low, high], [((height, count * cols), BF16)], place
    )[0]


def hidden_rows(total_groups, size, halves):
    per = total_groups // halves
    while per > 3:
        per = next(f for f in range(2, per + 1) if per % f == 0) and per // next(
            f for f in range(2, per + 1) if per % f == 0
        )
    return per, per * size


def forward_in(place, x_own, x_other, w_in):
    rows = x_own.shape[0]
    width, both = w_in.shape
    hidden = both // 2
    size = step_of(hidden)

    def kernel(place_ref, own_ref, other_ref, w_ref, hidden_ref, slope_ref, act_ref):
        x = jnp.concatenate([own_ref[...], other_ref[...]], axis=0)

        def body(start):
            gate = dot(x, w_ref[:, pl.ds(start, size)])
            up = dot(x, w_ref[:, pl.ds(hidden + start, size)])
            sig = 1.0 / (1.0 + jnp.exp(-gate))
            act = gate * sig
            hidden_ref[:, pl.ds(start, size)] = (act * up).astype(BF16)
            slope_ref[:, pl.ds(start, size)] = up * sig * (1.0 + gate * (1.0 - sig))
            act_ref[:, pl.ds(start, size)] = act

        tiles(hidden, body)

    shape = (2 * rows, hidden)
    return resident(
        kernel,
        [x_own, x_other, w_in],
        [(shape, BF16), (shape, F32), (shape, F32)],
        place,
        flops=4 * rows * width * both,
    )


def route_weight(extra, place_ref, experts):
    lane = lax.broadcasted_iota(jnp.int32, extra.shape, 1)
    me = place_ref[0]
    named = (lane == me) | (lane == me + experts) | (lane == me + 2 * experts)
    return jnp.sum(jnp.where(named, extra.astype(F32), 0.0), axis=1, keepdims=True)


def forward_down(place, hidden, w_down, terms, c):
    experts = lax.axis_size("expert")
    rows = hidden[0].shape[0] // 2
    height, quarter = w_down.shape
    size = step_of(quarter)
    held = slice(c * rows, (c + 1) * rows)

    def kernel(place_ref, *refs):
        *hidden_refs, w_ref, own_ref, other_ref, out_own_ref, out_other_ref = refs
        left = jnp.concatenate([ref[...] for ref in hidden_refs], axis=1)
        own = route_weight(own_ref[held, :], place_ref, experts)
        other = route_weight(other_ref[held, :], place_ref, experts)

        def body(start):
            total = dot(left, w_ref[:, pl.ds(start, size)])
            out_own_ref[:, pl.ds(start, size)] = (own * total[:rows]).astype(BF16)
            out_other_ref[:, pl.ds(start, size)] = (other * total[rows:]).astype(BF16)

        tiles(quarter, body)

    return resident(
        kernel,
        [*hidden, w_down, *terms],
        [((rows, quarter), BF16)] * 2,
        place,
        flops=4 * rows * height * quarter,
    )


def backward_down(place, err_own, err_other, w_down, terms, c, halves):
    experts = lax.axis_size("expert")
    rows, quarter = err_own.shape
    height = w_down.shape[0]
    own = height // halves
    size = step_of(own)
    held = slice(c * rows, (c + 1) * rows)

    def kernel(place_ref, err_own_ref, err_other_ref, own_ref, other_ref, w_ref, grad_ref, *outs):
        weight = route_weight(own_ref[held, :], place_ref, experts)
        grad_ref[:rows, :] = (weight * err_own_ref[...].astype(F32)).astype(BF16)
        weight = route_weight(other_ref[held, :], place_ref, experts)
        grad_ref[rows:, :] = (weight * err_other_ref[...].astype(F32)).astype(BF16)
        for d in reversed(range(halves)):

            def body(start):
                at = d * own + start
                part = dot_cols(grad_ref[...], w_ref[pl.ds(at, size), :])
                outs[d][:, pl.ds(start, size)] = part.astype(outs[d].dtype)

            tiles(own, body)

    shape = (2 * rows, own)
    return resident(
        kernel,
        [err_own, err_other, *terms, w_down],
        [((2 * rows, quarter), BF16), (shape, F32)] + [(shape, BF16)] * (halves - 1),
        place,
        flops=4 * rows * height * quarter,
    )


def backward_hidden(place, grad_own, arrived, slope, act, w_in, halves):
    both_rows, hidden = slope.shape
    rows = both_rows // 2
    quarter = w_in.shape[0] // halves
    size = step_of(quarter)
    count = len(arrived)

    def kernel(place_ref, grad_own_ref, *refs):
        arrived_refs = refs[:count]
        slope_ref, act_ref, w_ref, grad_ref, *outs = refs[count:]
        grad_hidden = grad_own_ref[...]
        for ref in arrived_refs:
            grad_hidden += ref[...].astype(F32)
        grad_ref[:, :hidden] = (grad_hidden * slope_ref[...]).astype(BF16)
        grad_ref[:, hidden:] = (grad_hidden * act_ref[...]).astype(BF16)
        for d in range(halves):

            def body(start):
                at = pl.multiple_of((place_ref[1] ^ d) * quarter + start, size)
                part = dot_cols(grad_ref[...], w_ref[pl.ds(at, size), :]).astype(BF16)
                outs[2 * d][:, pl.ds(start, size)] = part[:rows]
                outs[2 * d + 1][:, pl.ds(start, size)] = part[rows:]

            tiles(quarter, body)

    grad, *parts = resident(
        kernel,
        [grad_own, *arrived, slope, act, w_in],
        [((both_rows, 2 * hidden), BF16)] + [((rows, quarter), BF16)] * (2 * halves),
        place,
        flops=4 * both_rows * hidden * quarter * halves,
    )
    return grad, parts


def ends(grad, codes):
    upper = jnp.sum(grad * codes.astype(F32), axis=0, keepdims=True) * (1.0 / 255.0)
    return jnp.sum(grad, axis=0, keepdims=True) - upper, upper


def range_tile(left, right, size, step, codes, store):
    turned = left.T
    for start in range(0, right.shape[1], step):
        cols = slice(start, start + step)
        grad = dot(turned, right[:, cols])
        for g in range(turned.shape[0] // size):
            cut = slice(g * size, (g + 1) * size)
            low, high = ends(grad[cut], codes(cut, cols))
            store(g, cols, low, high)


def ranges_down(place, hidden, grads, codes, groups, halves):
    _, height, quarter = codes.shape
    size = height // groups
    per, rows = hidden_rows(groups, size, halves)
    blocks = height // halves // rows
    flat = [part for parts in hidden for part in parts]
    chunks = len(grads)
    tokens = grads[0].shape[0]

    def kernel(place_ref, *refs):
        hidden_refs = refs[: len(flat)]
        grad_refs = refs[len(flat) : len(flat) + chunks]
        code_ref, out_ref, right_ref = refs[len(flat) + chunks :]
        step = pl.program_id(0)
        base = moved(step, blocks, place_ref) * per

        @pl.when(step == 0)
        def _():
            for c in range(chunks):
                right_ref[c * tokens : (c + 1) * tokens, :] = grad_refs[c][...]

        def store(g, cols, low, high):
            out_ref[0, pl.ds(base + g, 1), cols] = low
            out_ref[1, pl.ds(base + g, 1), cols] = high

        for d in range(halves):

            @pl.when(step // blocks == d)
            def _():
                left = [hidden_refs[c * halves + d][...] for c in range(chunks)]
                range_tile(
                    jnp.concatenate(left, axis=0),
                    right_ref,
                    size,
                    256,
                    lambda cut, cols: code_ref[0, cut, cols],
                    store,
                )

    shape = (2, groups, quarter)
    return call(
        kernel,
        (height // rows,),
        [(part, (part.shape[0], rows), lambda i, p: (0, i % blocks)) for part in flat]
        + [(grad, pltpu.VMEM, None) for grad in grads]
        + [(codes, (1, rows, quarter), lambda i, p: (0, moved(i, blocks, p), 0))],
        [(shape, F32, shape, whole3)],
        place,
        scratch=[pltpu.VMEM((chunks * tokens, quarter), BF16)],
        mib=20,
        flops=2 * sum(g.shape[0] for g in grads) * height * quarter,
    )[0]


def ranges_in(place, x, grads, codes, groups, part, parts, found):
    _, _, width, hidden = codes.shape
    size = width // groups
    held = groups // parts
    per = next(p for p in (4, 2, 1) if held % p == 0)
    rows = per * size
    blocks = held // per
    flat = [array for pair in x for array in pair]
    chunks = len(grads)
    tokens, both = grads[0].shape
    wide = 256 if hidden % 256 == 0 else hidden

    def kernel(place_ref, *refs):
        x_refs = refs[: len(flat)]
        grad_refs = refs[len(flat) : len(flat) + chunks]
        code_ref, out_ref, right_ref = refs[len(flat) + chunks], refs[-2], refs[-1]
        base = pl.program_id(0) * per

        @pl.when(pl.program_id(0) == 0)
        def _():
            for c in range(chunks):
                right_ref[c * tokens : (c + 1) * tokens, :] = grad_refs[c][...]

        def split(cols):
            k = cols.start // hidden
            return k, slice(cols.start - k * hidden, cols.stop - k * hidden)

        def codes_at(cut, cols):
            k, cols = split(cols)
            return code_ref[0, k, cut, cols]

        def store(g, cols, low, high):
            k, cols = split(cols)
            out_ref[2 * k, pl.ds(base + g, 1), cols] = low
            out_ref[2 * k + 1, pl.ds(base + g, 1), cols] = high

        left = jnp.concatenate([ref[...] for ref in x_refs], axis=0)
        range_tile(left, right_ref, size, wide, codes_at, store)

    shape = (4, groups, hidden)
    return call(
        kernel,
        (blocks,),
        [(a, (a.shape[0], rows), lambda i, p: (0, part * blocks + i)) for a in flat]
        + [(grad, pltpu.VMEM, None) for grad in grads]
        + [(codes, (1, 2, rows, hidden), lambda i, p: (0, 0, part * blocks + i, 0))],
        [(shape, F32, (4, held, hidden), lambda i, p: (0, part, 0))],
        place,
        scratch=[pltpu.VMEM((chunks * tokens, both), BF16)],
        mib=20,
        flops=2 * sum(grad.size for grad in grads) * (width // parts),
        reuse=found,
    )[0]


def prepare(place, routes, route_scores, extra):
    experts = lax.axis_size("expert")
    rows, top_count = routes.shape

    def kernel(place_ref, route_ref, score_ref, out_ref):
        scores = score_ref[...]
        weights = scores / jnp.sum(scores, axis=1, keepdims=True)
        names = route_ref[...]
        lane = lax.broadcasted_iota(jnp.int32, (rows, extra), 1)
        third = jnp.where(lane < experts, 0, jnp.where(lane < 2 * experts, 1, 2))
        expert = lane - third * experts
        table = jnp.zeros((rows, extra), F32)
        for k in range(top_count):
            table += jnp.where(expert == names[:, k : k + 1], weights[:, k : k + 1], 0.0)
        top = table.astype(BF16).astype(F32)
        middle = (table - top).astype(BF16).astype(F32)
        bottom = table - top - middle
        terms = jnp.where(third == 0, top, jnp.where(third == 1, middle, bottom))
        out_ref[...] = terms.astype(BF16)

    return resident(kernel, [routes, route_scores], [((rows, extra), BF16)], place)[0]


def local(
    tokens, target, routes, route_scores, in_codes, in_low, in_high, down_codes, down_low, down_high
):
    experts = lax.axis_size("expert")
    halves = lax.axis_size("half")
    place = jnp.stack([lax.axis_index("expert"), lax.axis_index("half")]).astype(jnp.int32)
    quarter = target.shape[1]
    parts = range(halves)
    chunks = (0, 1)

    far = join(gather_far(tokens)[1:])
    near_own = swap(tokens, "expert", 4)
    across = [swap(tokens, "expert", 2)]
    extra = -(-3 * experts // 128) * 128
    terms = prepare(place, routes, route_scores, extra)
    w_in = dequant(place, in_codes[0], tie(in_low, terms)[0], in_high[0])
    w_down = dequant(place, down_codes, tie(down_low, w_in), down_high, halves)
    far = tie(far, w_in, w_down, across[0])
    near_far = swap(far, "expert", 4)
    middle = pack(place, [[far], [near_own]])
    across.append(swap(middle, "expert", 2))
    terms = join(gather_far(terms))
    near_far = tie(near_far, across[1], terms)
    across.append(swap(near_far, "expert", 2))
    first = pack(place, [[tokens], [middle], [near_far]])
    x = [(first, swap(first, "expert", 1))]
    near_terms = swap(terms, "expert", 4)

    hidden, slope, act = [], [], []
    for c in chunks:
        if c == 1:
            across[2] = tie(across[2], hidden[0][0], near_terms)
            second = pack(place, [[part] for part in across])
            x.append((second, swap(second, "expert", 1)))
        own, chunk_slope, chunk_act = forward_in(place, *x[c], w_in)
        hidden.append([own] + [swap(own, "half", d) for d in parts if d])
        slope.append(chunk_slope)
        act.append(chunk_act)
    terms = jnp.concatenate([terms, near_terms], axis=0)
    terms = jnp.concatenate([terms, swap(terms, "expert", 2)], axis=0)
    terms = (terms, swap(terms, "expert", 1))

    sums = []
    for c in chunks:
        if c == 1:
            hidden[1][1:] = [tie(part, sums[0][0]) for part in hidden[1][1:]]
        out_own, out_other = forward_down(place, hidden[c], w_down, terms, c)
        sums.append([out_own, swap(out_other, "expert", 1)])
    middle = quarter // 2
    cuts = [slice(0, middle), slice(middle, quarter)]
    mixed = scatter_rows(sums[0], sums[1], cuts)
    error = [
        (mixed[f] - target[:, cuts[f]].astype(F32)).astype(BF16) for f in range(len(cuts))
    ]

    kept = [gather_far(part) for part in error]
    near = [swap(join(part), "expert", 4) for part in kept]
    kept = pack(place, [list(line) for line in zip(*kept)])
    across = swap(kept, "expert", 2)
    near = [tie(part, across) for part in near]
    near_across = [swap(part, "expert", 2) for part in near]
    first = pack(place, [[kept], near])
    errors = [(first, swap(first, "expert", 1))]
    grads, grad_own, arrived = [], [], []
    for c in chunks:
        if c == 1:
            second = pack(place, [[across], [tie(part, grads[0]) for part in near_across]])
            errors.append((second, swap(second, "expert", 1)))
        grad, own, *others = backward_down(place, *errors[c], w_down, terms, c, halves)
        grads.append(grad)
        grad_own.append(own)
        arrived.append([swap(other, "half", d + 1) for d, other in enumerate(others)])

    grad_in, kinds = [], []
    down_grad = ranges_down(place, hidden, grads, down_codes, down_low.shape[1], halves)
    arrived[0] = [tie(part, down_grad) for part in arrived[0]]
    for c in chunks:
        if c == 1:
            arrived[1] = [tie(part, grad_in[0]) for part in arrived[1]]
        grad, found = backward_hidden(
            place, grad_own[c], arrived[c], slope[c], act[c], w_in, halves
        )
        grad_in.append(grad)
        kinds.append(found)
    kinds[0] = [tie(part, grad_in[1]) for part in kinds[0]]
    lower, upper = slice(0, first.shape[0] // 2), slice(first.shape[0] // 2, first.shape[0])
    keep, go = [
        [[found[2 * d], swap(found[2 * d + 1], "expert", 1)] for d in parts] for found in kinds
    ]
    stay, leave = keep[0], go[0]
    outer = [(d, keep[d]) for d in parts if d]
    crossed = [
        (
            swap(add([part[upper] for part in go[d]]).astype(BF16), "half", d),
            swap(add([part[lower] for part in go[d]]).astype(BF16), "expert", 2),
        )
        for d in parts
        if d
    ]

    def ranges(part, pieces, found, *after):
        held = [tie(grad, *after) for grad in grad_in] if after else grad_in
        return ranges_in(place, x, held, in_codes, in_low.shape[2], part, pieces, found)

    by_half = [pair[0] for pair in crossed]
    across_upper = swap(
        add([part[upper] for part in leave] + by_half).astype(BF16), "expert", 2
    )
    arrived_upper = [
        swap(tie(add([part[upper] for part in keep]).astype(BF16), *by_half), "half", d)
        for d, keep in outer
    ]
    in_grad = ranges(0, 2, None, *by_half)
    near = swap(
        tie(
            add([part[upper] for part in stay] + arrived_upper + [across_upper]).astype(BF16),
            in_grad,
        ),
        "expert",
        4,
    )
    across_lower = swap(
        tie(add([part[lower] for part in leave]).astype(BF16), across_upper), "expert", 2
    )
    arrived_lower = [
        swap(
            tie(
                add([part[lower] for part in keep] + [pair[1]]).astype(BF16), *arrived_upper
            ),
            "half",
            d,
        )
        for (d, keep), pair in zip(outer, crossed)
    ]
    in_grad = ranges(2, 4, in_grad)
    near = tie(near, in_grad)
    grad_tokens = scatter_far(
        [part[lower] for part in stay] + arrived_lower + [across_lower, near]
    )

    in_grad = ranges(3, 4, in_grad)
    return (grad_tokens.astype(BF16), in_grad[None], down_grad[None])


def solution(mesh):
    placed = (
        P("expert", None),
        P("expert", "half"),
        P("expert", None),
        P("expert", None),
        P("expert", None, None, "half"),
        P("expert", None, None, "half"),
        P("expert", None, None, "half"),
        P("expert", None, "half"),
        P("expert", None, "half"),
        P("expert", None, "half"),
    )
    return jax.shard_map(
        local,
        mesh=mesh,
        in_specs=placed,
        out_specs=(
            P("expert", "half"),
            P("expert", None, None, "half"),
            P("expert", None, None, "half"),
        ),
        check_vma=False,
    )
```

```python
import functools

import jax
import jax.numpy as jnp
from jax import lax
from jax.experimental import pallas as pl
from jax.experimental.pallas import tpu as pltpu
from jax.sharding import PartitionSpec as P

BF16 = jnp.bfloat16
F32 = jnp.float32
MIB = 1 << 20


def swap(array, axis, distance):
    size = lax.axis_size(axis)
    return lax.ppermute(array, axis, [(i, i ^ distance) for i in range(size)])


def tie(array, *others):
    return lax.optimization_barrier((array, *others))[0]


def far_distances():
    experts = lax.axis_size("expert")
    distances = []
    distance = experts // 2
    while distance > 4:
        distances.append(distance)
        distance //= 2
    return distances


def join(parts):
    return parts[0] if len(parts) == 1 else jnp.concatenate(parts, axis=0)


def gather_far(block, *after):
    parts = [block]
    for distance in far_distances():
        parts.append(swap(join(parts), "expert", distance))
        if after:
            parts[-1] = tie(parts[-1], *after)
    return parts


def add(parts):
    total = parts[0].astype(F32)
    for part in parts[1:]:
        total = total + part.astype(F32)
    return total


def scatter_far(terms):
    for distance in reversed(far_distances()):
        half = terms[0].shape[0] // 2
        sent = swap(add([part[half:] for part in terms]).astype(BF16), "expert", distance)
        terms = [part[:half] for part in terms] + [sent]
    return add(terms)


def scatter_rows(near, across, cuts):
    rows = near[0].shape[0] // 2
    upper = [swap(add([part[rows:, cut] for part in across]).astype(BF16), "expert", 2) for cut in cuts]
    sent = [
        swap(add([part[rows:, cut] for part in near] + [part_of]).astype(BF16), "expert", 4)
        for cut, part_of in zip(cuts, upper)
    ]
    lower = swap(tie(add([part[:rows] for part in across]).astype(BF16), *upper), "expert", 2)
    return [
        scatter_far([part[:rows, cut] for part in near] + [lower[:, cut], part_of])
        for cut, part_of in zip(cuts, sent)
    ]


def dot(left, right):
    return jnp.dot(left, right, preferred_element_type=F32)


def dot_cols(left, right):
    return lax.dot_general(left, right, (((1,), (1,)), ((), ())), preferred_element_type=F32)


def dot_rows(left, right):
    return lax.dot_general(left, right, (((0,), (0,)), ((), ())), preferred_element_type=F32)


def cost(flops, bytes_accessed):
    return pl.CostEstimate(flops=int(flops), bytes_accessed=int(bytes_accessed), transcendentals=0)


def moved(step, blocks, place):
    return ((step // blocks) ^ place[1]) * blocks + step % blocks


def call(kernel, grid, ins, outs, place, scratch=(), mib=16, flops=0, reuse=None, weight=1e-6):
    total = sum(a.size * a.dtype.itemsize for a, _, _ in ins)
    for shape, kind, _, _ in outs:
        count = 1
        for extent in shape:
            count *= extent
        total += count * jnp.dtype(kind).itemsize

    def spec(block, index):
        if isinstance(block, tuple):
            return pl.BlockSpec(block, index)
        return pl.BlockSpec(memory_space=block)

    in_specs = [spec(block, index) for _, block, index in ins]
    arrays = [a for a, _, _ in ins]
    if reuse is not None:
        in_specs.append(pl.BlockSpec(memory_space=pl.ANY))
        arrays.append(reuse)
    return pl.pallas_call(
        kernel,
        grid_spec=pltpu.PrefetchScalarGridSpec(
            num_scalar_prefetch=1,
            grid=grid,
            in_specs=in_specs,
            out_specs=[spec(block, index) for _, _, block, index in outs],
            scratch_shapes=list(scratch),
        ),
        out_shape=[jax.ShapeDtypeStruct(shape, kind) for shape, kind, _, _ in outs],
        compiler_params=pltpu.CompilerParams(vmem_limit_bytes=mib * MIB),
        cost_estimate=cost(flops * weight, total * weight),
        input_output_aliases={} if reuse is None else {1 + len(ins): 0},
    )(place, *arrays)


def resident(kernel, ins, outs, place, mib=16, flops=0, scratch=()):
    return call(
        kernel,
        (),
        [(a, pltpu.VMEM, None) for a in ins],
        [(shape, kind, pltpu.VMEM, None) for shape, kind in outs],
        place,
        mib=mib,
        flops=flops,
        scratch=scratch,
    )


def step_of(extent):
    return next(size for size in (512, 256, 128) if extent % size == 0)


def tiles(extent, body):
    size = step_of(extent)
    for start in range(0, extent, size):
        body(start)


def whole2(*_):
    return (0, 0)


def whole3(*_):
    return (0, 0, 0)


def whole4(*_):
    return (0, 0, 0, 0)


def pack(place, parts):
    rows = sum(line[0].shape[0] for line in parts)
    cols = sum(part.shape[1] for part in parts[0])

    def kernel(place_ref, *refs):
        refs, out_ref = list(refs[:-1]), refs[-1]
        row = 0
        for line in parts:
            col = 0
            for part in line:
                height, width = part.shape
                out_ref[row : row + height, col : col + width] = refs.pop(0)[...]
                col += width
            row += line[0].shape[0]

    flat = [part for line in parts for part in line]
    return resident(kernel, flat, [((rows, cols), parts[0][0].dtype)], place)[0]


def dequant(place, codes, low, high, halves=1):
    count, height, cols = codes.shape
    groups = low.shape[1]
    size = height // groups
    held = groups // halves

    def kernel(place_ref, code_ref, low_ref, high_ref, out_ref):
        def block(i, carry):
            base = moved(i, held, place_ref) if halves > 1 else i
            source = pl.multiple_of(base * size, size)
            to = pl.multiple_of(i * size, size)
            for k in range(count):
                bottom = low_ref[k, pl.ds(base, 1), :]
                scale = (high_ref[k, pl.ds(base, 1), :] - bottom) * (1.0 / 255.0)
                vals = code_ref[k, pl.ds(source, size), :].astype(F32)
                out_ref[pl.ds(to, size), k * cols : (k + 1) * cols] = (
                    bottom + scale * vals
                ).astype(BF16)
            return carry

        lax.fori_loop(0, groups, block, 0)

    return resident(
        kernel, [codes, low, high], [((height, count * cols), BF16)], place
    )[0]


def hidden_rows(total_groups, size, halves):
    per = total_groups // halves
    while per > 3:
        per = next(f for f in range(2, per + 1) if per % f == 0) and per // next(
            f for f in range(2, per + 1) if per % f == 0
        )
    return per, per * size


def height_of(parts):
    return sum(part.shape[0] for part in parts)


def stacked(refs):
    return jnp.concatenate([ref[...] for ref in refs], axis=0)


def forward_in(place, x, w_in):
    rows = height_of(x)
    width, both = w_in.shape
    hidden = both // 2
    size = step_of(hidden)

    def kernel(place_ref, *refs):
        w_ref, hidden_ref, slope_ref, act_ref = refs[len(x) :]
        left = stacked(refs[: len(x)])

        def body(start):
            gate = dot(left, w_ref[:, pl.ds(start, size)])
            up = dot(left, w_ref[:, pl.ds(hidden + start, size)])
            sig = 1.0 / (1.0 + jnp.exp(-gate))
            act = gate * sig
            hidden_ref[:, pl.ds(start, size)] = (act * up).astype(BF16)
            slope_ref[:, pl.ds(start, size)] = up * sig * (1.0 + gate * (1.0 - sig))
            act_ref[:, pl.ds(start, size)] = act

        tiles(hidden, body)

    shape = (rows, hidden)
    return resident(
        kernel,
        [*x, w_in],
        [(shape, BF16), (shape, F32), (shape, F32)],
        place,
        flops=2 * rows * width * both,
    )


def route_weight(extra, place_ref, experts):
    lane = lax.broadcasted_iota(jnp.int32, extra.shape, 1)
    me = place_ref[0]
    named = (lane == me) | (lane == me + experts) | (lane == me + 2 * experts)
    return jnp.sum(jnp.where(named, extra.astype(F32), 0.0), axis=1, keepdims=True)


def forward_down(place, hidden, w_down, terms, c):
    experts = lax.axis_size("expert")
    rows = hidden[0].shape[0] // 2
    height, quarter = w_down.shape
    size = step_of(quarter)
    held = slice(c * rows, (c + 1) * rows)

    def kernel(place_ref, *refs):
        *hidden_refs, w_ref, own_ref, other_ref, out_own_ref, out_other_ref = refs
        left = jnp.concatenate([ref[...] for ref in hidden_refs], axis=1)
        own = route_weight(own_ref[held, :], place_ref, experts)
        other = route_weight(other_ref[held, :], place_ref, experts)

        def body(start):
            total = dot(left, w_ref[:, pl.ds(start, size)])
            out_own_ref[:, pl.ds(start, size)] = (own * total[:rows]).astype(BF16)
            out_other_ref[:, pl.ds(start, size)] = (other * total[rows:]).astype(BF16)

        tiles(quarter, body)

    return resident(
        kernel,
        [*hidden, w_down, *terms],
        [((rows, quarter), BF16)] * 2,
        place,
        flops=4 * rows * height * quarter,
    )


def backward_down(place, err_own, err_other, w_down, terms, c, halves):
    experts = lax.axis_size("expert")
    rows, quarter = height_of(err_own), err_own[0].shape[1]
    count = len(err_own)
    height = w_down.shape[0]
    own = height // halves
    size = step_of(own)
    held = slice(c * rows, (c + 1) * rows)

    def kernel(place_ref, *refs):
        own_ref, other_ref, w_ref, grad_ref, *outs = refs[2 * count :]
        weight = route_weight(own_ref[held, :], place_ref, experts)
        grad_ref[:rows, :] = (weight * stacked(refs[:count]).astype(F32)).astype(BF16)
        weight = route_weight(other_ref[held, :], place_ref, experts)
        grad_ref[rows:, :] = (weight * stacked(refs[count : 2 * count]).astype(F32)).astype(BF16)
        for d in reversed(range(halves)):

            def body(start):
                at = d * own + start
                part = dot_cols(grad_ref[...], w_ref[pl.ds(at, size), :])
                outs[d][:, pl.ds(start, size)] = part.astype(outs[d].dtype)

            tiles(own, body)

    shape = (2 * rows, own)
    return resident(
        kernel,
        [*err_own, *err_other, *terms, w_down],
        [((2 * rows, quarter), BF16), (shape, F32)] + [(shape, BF16)] * (halves - 1),
        place,
        flops=4 * rows * height * quarter,
    )


def backward_hidden(place, grad_own, arrived, slope, act, w_in, halves):
    both_rows, hidden = slope.shape
    rows = both_rows // 2
    quarter = w_in.shape[0] // halves
    size = step_of(quarter)
    count = len(arrived)

    def kernel(place_ref, grad_own_ref, *refs):
        arrived_refs = refs[:count]
        slope_ref, act_ref, w_ref, grad_ref, *outs = refs[count:]
        grad_hidden = grad_own_ref[...]
        for ref in arrived_refs:
            grad_hidden += ref[...].astype(F32)
        grad_ref[:, :hidden] = (grad_hidden * slope_ref[...]).astype(BF16)
        grad_ref[:, hidden:] = (grad_hidden * act_ref[...]).astype(BF16)
        for d in range(halves):

            def body(start):
                at = pl.multiple_of((place_ref[1] ^ d) * quarter + start, size)
                part = dot_cols(grad_ref[...], w_ref[pl.ds(at, size), :]).astype(BF16)
                outs[2 * d][:, pl.ds(start, size)] = part[:rows]
                outs[2 * d + 1][:, pl.ds(start, size)] = part[rows:]

            tiles(quarter, body)

    grad, *parts = resident(
        kernel,
        [grad_own, *arrived, slope, act, w_in],
        [((both_rows, 2 * hidden), BF16)] + [((rows, quarter), BF16)] * (2 * halves),
        place,
        flops=4 * both_rows * hidden * quarter * halves,
    )
    return grad, parts


def ends(grad, codes):
    upper = jnp.sum(grad * codes.astype(F32), axis=0, keepdims=True) * (1.0 / 255.0)
    return jnp.sum(grad, axis=0, keepdims=True) - upper, upper


def range_tile(left, right, size, step, codes, store):
    turned = left.T
    for start in range(0, right.shape[1], step):
        cols = slice(start, start + step)
        grad = dot(turned, right[:, cols])
        for g in range(turned.shape[0] // size):
            cut = slice(g * size, (g + 1) * size)
            low, high = ends(grad[cut], codes(cut, cols))
            store(g, cols, low, high)


def ranges_down(place, hidden, grad, codes, groups, halves, found=None):
    _, height, quarter = codes.shape
    size = height // groups
    per, rows = hidden_rows(groups, size, halves)
    blocks = height // halves // rows
    earlier = [] if found is None else [found]

    def kernel(place_ref, *refs):
        hidden_refs = refs[:halves]
        grad_ref, code_ref, *found_refs, out_ref = refs[halves:]
        step = pl.program_id(0)
        base = moved(step, blocks, place_ref) * per

        def store(g, cols, low, high):
            for k, value in ((0, low), (1, high)):
                for ref in found_refs:
                    value += ref[k, pl.ds(base + g, 1), cols]
                out_ref[k, pl.ds(base + g, 1), cols] = value

        for d in range(halves):

            @pl.when(step // blocks == d)
            def _():
                range_tile(
                    hidden_refs[d][...],
                    grad_ref,
                    size,
                    256,
                    lambda cut, cols: code_ref[0, cut, cols],
                    store,
                )

    shape = (2, groups, quarter)
    return call(
        kernel,
        (height // rows,),
        [(part, (part.shape[0], rows), lambda i, p: (0, i % blocks)) for part in hidden]
        + [
            (grad, pltpu.VMEM, None),
            (codes, (1, rows, quarter), lambda i, p: (0, moved(i, blocks, p), 0)),
        ]
        + [(array, pltpu.VMEM, None) for array in earlier],
        [(shape, F32, shape, whole3)],
        place,
        mib=20,
        flops=2 * grad.shape[0] * height * quarter,
    )[0]


def ranges_in(place, x, grads, codes, groups, part, parts, found):
    _, _, width, hidden = codes.shape
    size = width // groups
    held = groups // parts
    per = next(p for p in (4, 2, 1) if held % p == 0)
    rows = per * size
    blocks = held // per
    flat = [array for parts in x for array in parts]
    chunks = len(grads)
    tokens, both = grads[0].shape
    wide = 256 if hidden % 256 == 0 else hidden

    def kernel(place_ref, *refs):
        x_refs = refs[: len(flat)]
        grad_refs = refs[len(flat) : len(flat) + chunks]
        code_ref, out_ref, right_ref = refs[len(flat) + chunks], refs[-2], refs[-1]
        base = pl.program_id(0) * per

        @pl.when(pl.program_id(0) == 0)
        def _():
            for c in range(chunks):
                right_ref[c * tokens : (c + 1) * tokens, :] = grad_refs[c][...]

        def split(cols):
            k = cols.start // hidden
            return k, slice(cols.start - k * hidden, cols.stop - k * hidden)

        def codes_at(cut, cols):
            k, cols = split(cols)
            return code_ref[0, k, cut, cols]

        def store(g, cols, low, high):
            k, cols = split(cols)
            out_ref[2 * k, pl.ds(base + g, 1), cols] = low
            out_ref[2 * k + 1, pl.ds(base + g, 1), cols] = high

        left = jnp.concatenate([ref[...] for ref in x_refs], axis=0)
        range_tile(left, right_ref, size, wide, codes_at, store)

    shape = (4, groups, hidden)
    return call(
        kernel,
        (blocks,),
        [(a, (a.shape[0], rows), lambda i, p: (0, part * blocks + i)) for a in flat]
        + [(grad, pltpu.VMEM, None) for grad in grads]
        + [(codes, (1, 2, rows, hidden), lambda i, p: (0, 0, part * blocks + i, 0))],
        [(shape, F32, (4, held, hidden), lambda i, p: (0, part, 0))],
        place,
        scratch=[pltpu.VMEM((chunks * tokens, both), BF16)],
        mib=20,
        flops=2 * sum(grad.size for grad in grads) * (width // parts),
        reuse=found,
    )[0]


def prepare(place, routes, route_scores, extra):
    experts = lax.axis_size("expert")
    rows, top_count = routes.shape

    def kernel(place_ref, route_ref, score_ref, out_ref):
        scores = score_ref[...]
        weights = scores / jnp.sum(scores, axis=1, keepdims=True)
        names = route_ref[...]
        lane = lax.broadcasted_iota(jnp.int32, (rows, extra), 1)
        third = jnp.where(lane < experts, 0, jnp.where(lane < 2 * experts, 1, 2))
        expert = lane - third * experts
        table = jnp.zeros((rows, extra), F32)
        for k in range(top_count):
            table += jnp.where(expert == names[:, k : k + 1], weights[:, k : k + 1], 0.0)
        top = table.astype(BF16).astype(F32)
        middle = (table - top).astype(BF16).astype(F32)
        bottom = table - top - middle
        terms = jnp.where(third == 0, top, jnp.where(third == 1, middle, bottom))
        out_ref[...] = terms.astype(BF16)

    return resident(kernel, [routes, route_scores], [((rows, extra), BF16)], place)[0]


def local(
    tokens, target, routes, route_scores, in_codes, in_low, in_high, down_codes, down_low, down_high
):
    experts = lax.axis_size("expert")
    halves = lax.axis_size("half")
    place = jnp.stack([lax.axis_index("expert"), lax.axis_index("half")]).astype(jnp.int32)
    quarter = target.shape[1]
    parts = range(halves)
    chunks = (0, 1)

    far = join(gather_far(tokens)[1:])
    near_own = swap(tokens, "expert", 4)
    across_own = swap(tokens, "expert", 2)
    extra = -(-3 * experts // 128) * 128
    terms = prepare(place, routes, route_scores, extra)
    near_own = tie(near_own, terms)
    across_near = swap(near_own, "expert", 2)
    w_in = dequant(place, in_codes[0], tie(in_low, near_own)[0], in_high[0])
    far = tie(far, w_in, across_own, across_near)
    near_far = swap(far, "expert", 4)
    across_far = swap(far, "expert", 2)
    w_down = dequant(place, down_codes, tie(down_low, far), down_high, halves)
    first = pack(place, [[tokens], [tie(far, w_down)], [near_own]])
    first_other = swap(first, "expert", 1)
    terms = join(gather_far(terms, w_down))
    near_far = tie(near_far, w_down, terms)
    across_last = swap(near_far, "expert", 2)
    near_other = swap(near_far, "expert", 1)
    x = [[first, near_far, first_other, near_other]]
    near_terms = swap(terms, "expert", 4)

    hidden, slope, act = [], [], []
    for c in chunks:
        if c == 1:
            second = pack(place, [[across_own], [tie(across_far, near_other)], [across_near]])
            second_other = swap(second, "expert", 1)
            across_last = tie(across_last, hidden[0][0], near_terms, second_other)
            x.append([second, across_last, second_other, swap(across_last, "expert", 1)])
        own, chunk_slope, chunk_act = forward_in(place, x[c], w_in)
        hidden.append([own] + [swap(own, "half", d) for d in parts if d])
        slope.append(chunk_slope)
        act.append(chunk_act)
    terms = jnp.concatenate([terms, near_terms], axis=0)
    terms = jnp.concatenate([terms, swap(terms, "expert", 2)], axis=0)
    terms = (terms, swap(terms, "expert", 1))

    sums = []
    for c in chunks:
        if c == 1:
            hidden[1][1:] = [tie(part, sums[0][0]) for part in hidden[1][1:]]
        out_own, out_other = forward_down(place, hidden[c], w_down, terms, c)
        sums.append([out_own, swap(out_other, "expert", 1)])
    middle = quarter // 2
    cuts = [slice(0, middle), slice(middle, quarter)]
    mixed = scatter_rows(sums[0], sums[1], cuts)
    error = [
        (mixed[f] - target[:, cuts[f]].astype(F32)).astype(BF16) for f in range(len(cuts))
    ]

    kept = pack(place, [list(line) for line in zip(*[gather_far(part) for part in error])])
    near = swap(kept, "expert", 4)
    across_kept = swap(kept, "expert", 2)
    kept_other = swap(kept, "expert", 1)
    near = tie(near, across_kept, kept_other)
    across_near = swap(near, "expert", 2)
    across_other = swap(across_kept, "expert", 1)
    errors = [([kept, near], [kept_other, swap(near, "expert", 1)])]
    grads, grad_own, arrived = [], [], []
    down_groups = down_low.shape[1]
    for c in chunks:
        if c == 1:
            across_near = tie(across_near, grads[0], across_other)
            down_grad = ranges_down(place, hidden[0], grads[0], down_codes, down_groups, halves)
            last_other = tie(swap(across_near, "expert", 1), down_grad, *arrived[0])
            errors.append(([across_kept, across_near], [across_other, last_other]))
        grad, own, *others = backward_down(place, *errors[c], w_down, terms, c, halves)
        grads.append(grad)
        grad_own.append(own)
        arrived.append([swap(other, "half", d + 1) for d, other in enumerate(others)])

    grad_in, kinds = [], []
    down_grad = ranges_down(
        place, hidden[1], grads[1], down_codes, down_groups, halves, down_grad
    )
    for c in chunks:
        if c == 1:
            arrived[1] = [tie(part, grad_in[0], down_grad) for part in arrived[1]]
        grad, found = backward_hidden(
            place, grad_own[c], arrived[c], slope[c], act[c], w_in, halves
        )
        grad_in.append(grad)
        kinds.append(found)
    kinds[0] = [tie(part, grad_in[1]) for part in kinds[0]]
    rows = height_of(errors[0][0])
    lower, upper = slice(0, rows // 2), slice(rows // 2, rows)
    keep, go = [
        [[found[2 * d], swap(found[2 * d + 1], "expert", 1)] for d in parts] for found in kinds
    ]
    stay, leave = keep[0], go[0]
    outer = [(d, keep[d]) for d in parts if d]
    crossed = [
        (
            swap(add([part[upper] for part in go[d]]).astype(BF16), "half", d),
            swap(add([part[lower] for part in go[d]]).astype(BF16), "expert", 2),
        )
        for d in parts
        if d
    ]

    def ranges(part, pieces, found, *after):
        held = [tie(grad, *after) for grad in grad_in] if after else grad_in
        return ranges_in(place, x, held, in_codes, in_low.shape[2], part, pieces, found)

    by_half = [pair[0] for pair in crossed]
    across_upper = swap(
        add([part[upper] for part in leave] + by_half).astype(BF16), "expert", 2
    )
    arrived_upper = [
        swap(tie(add([part[upper] for part in keep]).astype(BF16), *by_half), "half", d)
        for d, keep in outer
    ]
    in_grad = ranges(0, 2, None, *by_half)
    near = swap(
        tie(
            add([part[upper] for part in stay] + arrived_upper + [across_upper]).astype(BF16),
            in_grad,
        ),
        "expert",
        4,
    )
    across_lower = swap(
        tie(add([part[lower] for part in leave]).astype(BF16), across_upper), "expert", 2
    )
    arrived_lower = [
        swap(
            tie(
                add([part[lower] for part in keep] + [pair[1]]).astype(BF16), *arrived_upper
            ),
            "half",
            d,
        )
        for (d, keep), pair in zip(outer, crossed)
    ]
    in_grad = ranges(2, 4, in_grad)
    near = tie(near, in_grad)
    grad_tokens = scatter_far(
        [part[lower] for part in stay] + arrived_lower + [across_lower, near]
    )

    in_grad = ranges(3, 4, in_grad)
    return (grad_tokens.astype(BF16), in_grad[None], down_grad[None])


def solution(mesh):
    placed = (
        P("expert", None),
        P("expert", "half"),
        P("expert", None),
        P("expert", None),
        P("expert", None, None, "half"),
        P("expert", None, None, "half"),
        P("expert", None, None, "half"),
        P("expert", None, "half"),
        P("expert", None, "half"),
        P("expert", None, "half"),
    )
    return jax.shard_map(
        local,
        mesh=mesh,
        in_specs=placed,
        out_specs=(
            P("expert", "half"),
            P("expert", None, None, "half"),
            P("expert", None, None, "half"),
        ),
        check_vma=False,
    )
```

```python
import functools

import jax
import jax.numpy as jnp
from jax import lax
from jax.experimental import pallas as pl
from jax.experimental.pallas import tpu as pltpu
from jax.sharding import PartitionSpec as P

BF16 = jnp.bfloat16
F32 = jnp.float32
MIB = 1 << 20


def swap(array, axis, distance):
    size = lax.axis_size(axis)
    return lax.ppermute(array, axis, [(i, i ^ distance) for i in range(size)])


def tie(array, *others):
    return lax.optimization_barrier((array, *others))[0]


def far_distances():
    experts = lax.axis_size("expert")
    distances = []
    distance = experts // 2
    while distance > 4:
        distances.append(distance)
        distance //= 2
    return distances


def join(parts):
    return parts[0] if len(parts) == 1 else jnp.concatenate(parts, axis=0)


def gather_far(block):
    parts = [block]
    for distance in far_distances():
        parts.append(swap(join(parts), "expert", distance))
    return parts


def add(parts):
    total = parts[0].astype(F32)
    for part in parts[1:]:
        total = total + part.astype(F32)
    return total


def scatter_far(terms):
    for distance in reversed(far_distances()):
        half = terms[0].shape[0] // 2
        sent = swap(add([part[half:] for part in terms]).astype(BF16), "expert", distance)
        terms = [part[:half] for part in terms] + [sent]
    return add(terms)


def scatter_rows(near, across, cuts):
    rows = near[0].shape[0] // 2
    upper = [swap(add([part[rows:, cut] for part in across]).astype(BF16), "expert", 2) for cut in cuts]
    sent = [
        swap(add([part[rows:, cut] for part in near] + [part_of]).astype(BF16), "expert", 4)
        for cut, part_of in zip(cuts, upper)
    ]
    lower = swap(tie(add([part[:rows] for part in across]).astype(BF16), *upper), "expert", 2)
    return [
        scatter_far([part[:rows, cut] for part in near] + [lower[:, cut], part_of])
        for cut, part_of in zip(cuts, sent)
    ]


def dot(left, right):
    return jnp.dot(left, right, preferred_element_type=F32)


def dot_cols(left, right):
    return lax.dot_general(left, right, (((1,), (1,)), ((), ())), preferred_element_type=F32)


def dot_rows(left, right):
    return lax.dot_general(left, right, (((0,), (0,)), ((), ())), preferred_element_type=F32)


def cost(flops, bytes_accessed):
    return pl.CostEstimate(flops=int(flops), bytes_accessed=int(bytes_accessed), transcendentals=0)


def moved(step, blocks, place):
    return ((step // blocks) ^ place[1]) * blocks + step % blocks


def call(kernel, grid, ins, outs, place, scratch=(), mib=16, flops=0, reuse=None, weight=1e-6):
    total = sum(a.size * a.dtype.itemsize for a, _, _ in ins)
    for shape, kind, _, _ in outs:
        count = 1
        for extent in shape:
            count *= extent
        total += count * jnp.dtype(kind).itemsize

    def spec(block, index):
        if isinstance(block, tuple):
            return pl.BlockSpec(block, index)
        return pl.BlockSpec(memory_space=block)

    in_specs = [spec(block, index) for _, block, index in ins]
    arrays = [a for a, _, _ in ins]
    if reuse is not None:
        in_specs.append(pl.BlockSpec(memory_space=pl.ANY))
        arrays.append(reuse)
    return pl.pallas_call(
        kernel,
        grid_spec=pltpu.PrefetchScalarGridSpec(
            num_scalar_prefetch=1,
            grid=grid,
            in_specs=in_specs,
            out_specs=[spec(block, index) for _, _, block, index in outs],
            scratch_shapes=list(scratch),
        ),
        out_shape=[jax.ShapeDtypeStruct(shape, kind) for shape, kind, _, _ in outs],
        compiler_params=pltpu.CompilerParams(vmem_limit_bytes=mib * MIB),
        cost_estimate=cost(flops * weight, total * weight),
        input_output_aliases={} if reuse is None else {1 + len(ins): 0},
    )(place, *arrays)


def resident(kernel, ins, outs, place, mib=16, flops=0, scratch=()):
    return call(
        kernel,
        (),
        [(a, pltpu.VMEM, None) for a in ins],
        [(shape, kind, pltpu.VMEM, None) for shape, kind in outs],
        place,
        mib=mib,
        flops=flops,
        scratch=scratch,
    )


def step_of(extent):
    return next(size for size in (512, 256, 128) if extent % size == 0)


def tiles(extent, body):
    size = step_of(extent)
    for start in range(0, extent, size):
        body(start)


def whole2(*_):
    return (0, 0)


def whole3(*_):
    return (0, 0, 0)


def whole4(*_):
    return (0, 0, 0, 0)


def pack(place, parts):
    rows = sum(line[0].shape[0] for line in parts)
    cols = sum(part.shape[1] for part in parts[0])

    def kernel(place_ref, *refs):
        refs, out_ref = list(refs[:-1]), refs[-1]
        row = 0
        for line in parts:
            col = 0
            for part in line:
                height, width = part.shape
                out_ref[row : row + height, col : col + width] = refs.pop(0)[...]
                col += width
            row += line[0].shape[0]

    flat = [part for line in parts for part in line]
    return resident(kernel, flat, [((rows, cols), parts[0][0].dtype)], place)[0]


def dequant(place, codes, low, high, halves=1):
    count, height, cols = codes.shape
    groups = low.shape[1]
    size = height // groups
    held = groups // halves

    def kernel(place_ref, code_ref, low_ref, high_ref, out_ref):
        def block(i, carry):
            base = moved(i, held, place_ref) if halves > 1 else i
            source = pl.multiple_of(base * size, size)
            to = pl.multiple_of(i * size, size)
            for k in range(count):
                bottom = low_ref[k, pl.ds(base, 1), :]
                scale = (high_ref[k, pl.ds(base, 1), :] - bottom) * (1.0 / 255.0)
                vals = code_ref[k, pl.ds(source, size), :].astype(F32)
                out_ref[pl.ds(to, size), k * cols : (k + 1) * cols] = (
                    bottom + scale * vals
                ).astype(BF16)
            return carry

        lax.fori_loop(0, groups, block, 0)

    return resident(
        kernel, [codes, low, high], [((height, count * cols), BF16)], place
    )[0]


def dequant_wide(place, codes, low, high, mib):
    count, height, cols = codes.shape
    groups = low.shape[1]
    size = height // groups
    per = next(p for p in (4, 2, 1) if groups % p == 0)
    steps = groups // per
    rows = per * size

    def kernel(place_ref, code_hbm, low_hbm, high_hbm, out_ref, code_ref, low_ref, high_ref, sems):
        ends = [
            pltpu.make_async_copy(low_hbm, low_ref, sems.at[steps]),
            pltpu.make_async_copy(high_hbm, high_ref, sems.at[steps + 1]),
        ]
        blocks = []
        for i in range(steps):
            held = slice(i * rows, (i + 1) * rows)
            blocks.append(
                pltpu.make_async_copy(code_hbm.at[:, held, :], code_ref.at[:, held, :], sems.at[i])
            )
        for copy in ends + blocks:
            copy.start()
        for copy in ends:
            copy.wait()
        for i in range(steps):
            blocks[i].wait()

            def group(j, carry):
                at = i * per + j
                held = pl.ds(pl.multiple_of(at * size, size), size)
                for k in range(count):
                    bottom = low_ref[k, pl.ds(at, 1), :]
                    scale = (high_ref[k, pl.ds(at, 1), :] - bottom) * (1.0 / 255.0)
                    vals = code_ref[k, held, :].astype(F32)
                    out_ref[held, k * cols : (k + 1) * cols] = (bottom + scale * vals).astype(BF16)
                return carry

            lax.fori_loop(0, per, group, 0)

    return call(
        kernel,
        (),
        [(a, pltpu.HBM, None) for a in (codes, low, high)],
        [((height, count * cols), BF16, pltpu.VMEM, None)],
        place,
        scratch=[
            pltpu.VMEM(codes.shape, BF16),
            pltpu.VMEM(low.shape, F32),
            pltpu.VMEM(high.shape, F32),
            pltpu.SemaphoreType.DMA((steps + 2,)),
        ],
        mib=mib,
    )[0]


def hidden_rows(total_groups, size, halves):
    per = total_groups // halves
    while per > 3:
        per = next(f for f in range(2, per + 1) if per % f == 0) and per // next(
            f for f in range(2, per + 1) if per % f == 0
        )
    return per, per * size


def height_of(parts):
    return sum(part.shape[0] for part in parts)


def stacked(refs):
    return jnp.concatenate([ref[...] for ref in refs], axis=0)


def forward_in(place, x, w_in):
    rows = height_of(x)
    width, both = w_in.shape
    hidden = both // 2
    size = step_of(hidden)

    def kernel(place_ref, *refs):
        w_ref, hidden_ref, slope_ref, act_ref = refs[len(x) :]
        left = stacked(refs[: len(x)])

        def body(start):
            gate = dot(left, w_ref[:, pl.ds(start, size)])
            up = dot(left, w_ref[:, pl.ds(hidden + start, size)])
            sig = 1.0 / (1.0 + jnp.exp(-gate))
            act = gate * sig
            hidden_ref[:, pl.ds(start, size)] = (act * up).astype(BF16)
            slope_ref[:, pl.ds(start, size)] = up * sig * (1.0 + gate * (1.0 - sig))
            act_ref[:, pl.ds(start, size)] = act

        tiles(hidden, body)

    shape = (rows, hidden)
    return resident(
        kernel,
        [*x, w_in],
        [(shape, BF16), (shape, F32), (shape, F32)],
        place,
        flops=2 * rows * width * both,
    )


def route_weight(extra, place_ref, experts):
    lane = lax.broadcasted_iota(jnp.int32, extra.shape, 1)
    me = place_ref[0]
    named = (lane == me) | (lane == me + experts) | (lane == me + 2 * experts)
    return jnp.sum(jnp.where(named, extra.astype(F32), 0.0), axis=1, keepdims=True)


def forward_down(place, hidden, w_down, terms, c):
    experts = lax.axis_size("expert")
    rows = hidden[0].shape[0] // 2
    height, quarter = w_down.shape
    size = step_of(quarter)
    held = slice(c * rows, (c + 1) * rows)

    def kernel(place_ref, *refs):
        *hidden_refs, w_ref, own_ref, other_ref, out_own_ref, out_other_ref = refs
        left = jnp.concatenate([ref[...] for ref in hidden_refs], axis=1)
        own = route_weight(own_ref[held, :], place_ref, experts)
        other = route_weight(other_ref[held, :], place_ref, experts)

        def body(start):
            total = dot(left, w_ref[:, pl.ds(start, size)])
            out_own_ref[:, pl.ds(start, size)] = (own * total[:rows]).astype(BF16)
            out_other_ref[:, pl.ds(start, size)] = (other * total[rows:]).astype(BF16)

        tiles(quarter, body)

    return resident(
        kernel,
        [*hidden, w_down, *terms],
        [((rows, quarter), BF16)] * 2,
        place,
        flops=4 * rows * height * quarter,
    )


def backward_down(place, err_own, err_other, w_down, terms, c, halves):
    experts = lax.axis_size("expert")
    rows, quarter = height_of(err_own), err_own[0].shape[1]
    count = len(err_own)
    height = w_down.shape[0]
    own = height // halves
    size = step_of(own)
    held = slice(c * rows, (c + 1) * rows)

    def kernel(place_ref, *refs):
        own_ref, other_ref, w_ref, grad_ref, *outs = refs[2 * count :]
        weight = route_weight(own_ref[held, :], place_ref, experts)
        grad_ref[:rows, :] = (weight * stacked(refs[:count]).astype(F32)).astype(BF16)
        weight = route_weight(other_ref[held, :], place_ref, experts)
        grad_ref[rows:, :] = (weight * stacked(refs[count : 2 * count]).astype(F32)).astype(BF16)
        for d in reversed(range(halves)):

            def body(start):
                at = d * own + start
                part = dot_cols(grad_ref[...], w_ref[pl.ds(at, size), :])
                outs[d][:, pl.ds(start, size)] = part.astype(outs[d].dtype)

            tiles(own, body)

    shape = (2 * rows, own)
    return resident(
        kernel,
        [*err_own, *err_other, *terms, w_down],
        [((2 * rows, quarter), BF16), (shape, F32)] + [(shape, BF16)] * (halves - 1),
        place,
        flops=4 * rows * height * quarter,
    )


def backward_hidden(place, grad_own, arrived, slope, act, w_in, halves):
    both_rows, hidden = slope.shape
    rows = both_rows // 2
    quarter = w_in.shape[0] // halves
    size = step_of(quarter)
    count = len(arrived)

    def kernel(place_ref, grad_own_ref, *refs):
        arrived_refs = refs[:count]
        slope_ref, act_ref, w_ref, grad_ref, *outs = refs[count:]
        grad_hidden = grad_own_ref[...]
        for ref in arrived_refs:
            grad_hidden += ref[...].astype(F32)
        grad_ref[:, :hidden] = (grad_hidden * slope_ref[...]).astype(BF16)
        grad_ref[:, hidden:] = (grad_hidden * act_ref[...]).astype(BF16)
        for d in range(halves):

            def body(start):
                at = pl.multiple_of((place_ref[1] ^ d) * quarter + start, size)
                part = dot_cols(grad_ref[...], w_ref[pl.ds(at, size), :]).astype(BF16)
                outs[2 * d][:, pl.ds(start, size)] = part[:rows]
                outs[2 * d + 1][:, pl.ds(start, size)] = part[rows:]

            tiles(quarter, body)

    grad, *parts = resident(
        kernel,
        [grad_own, *arrived, slope, act, w_in],
        [((both_rows, 2 * hidden), BF16)] + [((rows, quarter), BF16)] * (2 * halves),
        place,
        flops=4 * both_rows * hidden * quarter * halves,
    )
    return grad, parts


def ends(grad, codes):
    upper = jnp.sum(grad * codes.astype(F32), axis=0, keepdims=True) * (1.0 / 255.0)
    return jnp.sum(grad, axis=0, keepdims=True) - upper, upper


def range_tile(left, right, size, step, codes, store):
    turned = left.T
    for start in range(0, right.shape[1], step):
        cols = slice(start, start + step)
        grad = dot(turned, right[:, cols])
        for g in range(turned.shape[0] // size):
            cut = slice(g * size, (g + 1) * size)
            low, high = ends(grad[cut], codes(cut, cols))
            store(g, cols, low, high)


def ranges_down(place, hidden, grad, codes, groups, halves, found=None):
    _, height, quarter = codes.shape
    size = height // groups
    per, rows = hidden_rows(groups, size, halves)
    blocks = height // halves // rows
    earlier = [] if found is None else [found]

    def kernel(place_ref, *refs):
        hidden_refs = refs[:halves]
        grad_ref, code_ref, *found_refs, out_ref = refs[halves:]
        step = pl.program_id(0)
        base = moved(step, blocks, place_ref) * per

        def store(g, cols, low, high):
            for k, value in ((0, low), (1, high)):
                for ref in found_refs:
                    value += ref[k, pl.ds(base + g, 1), cols]
                out_ref[k, pl.ds(base + g, 1), cols] = value

        for d in range(halves):

            @pl.when(step // blocks == d)
            def _():
                range_tile(
                    hidden_refs[d][...],
                    grad_ref,
                    size,
                    256,
                    lambda cut, cols: code_ref[0, cut, cols],
                    store,
                )

    shape = (2, groups, quarter)
    return call(
        kernel,
        (height // rows,),
        [(part, (part.shape[0], rows), lambda i, p: (0, i % blocks)) for part in hidden]
        + [
            (grad, pltpu.VMEM, None),
            (codes, (1, rows, quarter), lambda i, p: (0, moved(i, blocks, p), 0)),
        ]
        + [(array, pltpu.VMEM, None) for array in earlier],
        [(shape, F32, shape, whole3)],
        place,
        mib=20,
        flops=2 * grad.shape[0] * height * quarter,
    )[0]


def ranges_in(place, x, grads, codes, groups, part, parts, found):
    _, _, width, hidden = codes.shape
    size = width // groups
    held = groups // parts
    per = next(p for p in (4, 2, 1) if held % p == 0)
    rows = per * size
    blocks = held // per
    flat = [array for parts in x for array in parts]
    chunks = len(grads)
    tokens, both = grads[0].shape
    wide = 256 if hidden % 256 == 0 else hidden

    def kernel(place_ref, *refs):
        x_refs = refs[: len(flat)]
        grad_refs = refs[len(flat) : len(flat) + chunks]
        code_ref, out_ref, right_ref = refs[len(flat) + chunks], refs[-2], refs[-1]
        base = pl.program_id(0) * per

        @pl.when(pl.program_id(0) == 0)
        def _():
            for c in range(chunks):
                right_ref[c * tokens : (c + 1) * tokens, :] = grad_refs[c][...]

        def split(cols):
            k = cols.start // hidden
            return k, slice(cols.start - k * hidden, cols.stop - k * hidden)

        def codes_at(cut, cols):
            k, cols = split(cols)
            return code_ref[0, k, cut, cols]

        def store(g, cols, low, high):
            k, cols = split(cols)
            out_ref[2 * k, pl.ds(base + g, 1), cols] = low
            out_ref[2 * k + 1, pl.ds(base + g, 1), cols] = high

        left = jnp.concatenate([ref[...] for ref in x_refs], axis=0)
        range_tile(left, right_ref, size, wide, codes_at, store)

    shape = (4, groups, hidden)
    return call(
        kernel,
        (blocks,),
        [(a, (a.shape[0], rows), lambda i, p: (0, part * blocks + i)) for a in flat]
        + [(grad, pltpu.VMEM, None) for grad in grads]
        + [(codes, (1, 2, rows, hidden), lambda i, p: (0, 0, part * blocks + i, 0))],
        [(shape, F32, (4, held, hidden), lambda i, p: (0, part, 0))],
        place,
        scratch=[pltpu.VMEM((chunks * tokens, both), BF16)],
        mib=20,
        flops=2 * sum(grad.size for grad in grads) * (width // parts),
        reuse=found,
    )[0]


def prepare(place, routes, route_scores, extra):
    experts = lax.axis_size("expert")
    rows, top_count = routes.shape

    def kernel(place_ref, route_ref, score_ref, out_ref):
        scores = score_ref[...]
        weights = scores / jnp.sum(scores, axis=1, keepdims=True)
        names = route_ref[...]
        lane = lax.broadcasted_iota(jnp.int32, (rows, extra), 1)
        third = jnp.where(lane < experts, 0, jnp.where(lane < 2 * experts, 1, 2))
        expert = lane - third * experts
        table = jnp.zeros((rows, extra), F32)
        for k in range(top_count):
            table += jnp.where(expert == names[:, k : k + 1], weights[:, k : k + 1], 0.0)
        top = table.astype(BF16).astype(F32)
        middle = (table - top).astype(BF16).astype(F32)
        bottom = table - top - middle
        terms = jnp.where(third == 0, top, jnp.where(third == 1, middle, bottom))
        out_ref[...] = terms.astype(BF16)

    return resident(kernel, [routes, route_scores], [((rows, extra), BF16)], place)[0]


def local(
    tokens, target, routes, route_scores, in_codes, in_low, in_high, down_codes, down_low, down_high
):
    experts = lax.axis_size("expert")
    halves = lax.axis_size("half")
    place = jnp.stack([lax.axis_index("expert"), lax.axis_index("half")]).astype(jnp.int32)
    quarter = target.shape[1]
    parts = range(halves)
    chunks = (0, 1)

    far = join(gather_far(tokens)[1:])
    near_own = swap(tokens, "expert", 4)
    across_own = swap(tokens, "expert", 2)
    extra = -(-3 * experts // 128) * 128
    terms = prepare(place, routes, route_scores, extra)
    near_own = tie(near_own, terms)
    across_near = swap(near_own, "expert", 2)
    terms = join(gather_far(terms))
    far = tie(far, across_own, across_near, terms)
    near_far = swap(far, "expert", 4)
    across_far = swap(far, "expert", 2)
    w_in = dequant_wide(place, in_codes[0], tie(in_low, far)[0], in_high[0], 30)
    near_far = tie(near_far, w_in)
    first = pack(place, [[tokens], [far], [near_own]])
    first_other = swap(first, "expert", 1)
    across_last = swap(near_far, "expert", 2)
    near_other = swap(near_far, "expert", 1)
    x = [[first, near_far, first_other, near_other]]
    near_terms = swap(terms, "expert", 4)

    hidden, slope, act = [], [], []
    for c in chunks:
        if c == 1:
            second = pack(place, [[across_own], [tie(across_far, near_other)], [across_near]])
            second_other = swap(second, "expert", 1)
            across_last = tie(across_last, w_down, near_terms, second_other)
            x.append([second, across_last, second_other, swap(across_last, "expert", 1)])
        own, chunk_slope, chunk_act = forward_in(place, x[c], w_in)
        if c == 0:
            w_down = dequant(place, down_codes, tie(down_low, own), down_high, halves)
        hidden.append([own] + [swap(own, "half", d) for d in parts if d])
        slope.append(chunk_slope)
        act.append(chunk_act)
    terms = jnp.concatenate([terms, near_terms], axis=0)
    terms = jnp.concatenate([terms, swap(terms, "expert", 2)], axis=0)
    terms = (terms, swap(terms, "expert", 1))

    sums = []
    for c in chunks:
        if c == 1:
            hidden[1][1:] = [tie(part, sums[0][0]) for part in hidden[1][1:]]
        out_own, out_other = forward_down(place, hidden[c], w_down, terms, c)
        sums.append([out_own, swap(out_other, "expert", 1)])
    middle = quarter // 2
    cuts = [slice(0, middle), slice(middle, quarter)]
    mixed = scatter_rows(sums[0], sums[1], cuts)
    error = [
        (mixed[f] - target[:, cuts[f]].astype(F32)).astype(BF16) for f in range(len(cuts))
    ]

    kept = pack(place, [list(line) for line in zip(*[gather_far(part) for part in error])])
    near = swap(kept, "expert", 4)
    across_kept = swap(kept, "expert", 2)
    kept_other = swap(kept, "expert", 1)
    near = tie(near, across_kept, kept_other)
    across_near = swap(near, "expert", 2)
    across_other = swap(across_kept, "expert", 1)
    errors = [([kept, near], [kept_other, swap(near, "expert", 1)])]
    grads, grad_own, arrived = [], [], []
    down_groups = down_low.shape[1]
    for c in chunks:
        if c == 1:
            across_near = tie(across_near, grads[0], across_other)
            down_grad = ranges_down(place, hidden[0], grads[0], down_codes, down_groups, halves)
            last_other = tie(swap(across_near, "expert", 1), down_grad, *arrived[0])
            errors.append(([across_kept, across_near], [across_other, last_other]))
        grad, own, *others = backward_down(place, *errors[c], w_down, terms, c, halves)
        grads.append(grad)
        grad_own.append(own)
        arrived.append([swap(other, "half", d + 1) for d, other in enumerate(others)])

    grad_in, kinds = [], []
    down_grad = ranges_down(
        place, hidden[1], grads[1], down_codes, down_groups, halves, down_grad
    )
    for c in chunks:
        if c == 1:
            arrived[1] = [tie(part, grad_in[0], down_grad) for part in arrived[1]]
        grad, found = backward_hidden(
            place, grad_own[c], arrived[c], slope[c], act[c], w_in, halves
        )
        grad_in.append(grad)
        kinds.append(found)
    kinds[0] = [tie(part, grad_in[1]) for part in kinds[0]]
    rows = height_of(errors[0][0])
    lower, upper = slice(0, rows // 2), slice(rows // 2, rows)
    keep, go = [
        [[found[2 * d], swap(found[2 * d + 1], "expert", 1)] for d in parts] for found in kinds
    ]
    stay, leave = keep[0], go[0]
    outer = [(d, keep[d]) for d in parts if d]
    crossed = [
        (
            swap(add([part[upper] for part in go[d]]).astype(BF16), "half", d),
            swap(add([part[lower] for part in go[d]]).astype(BF16), "expert", 2),
        )
        for d in parts
        if d
    ]

    def ranges(part, pieces, found, *after):
        held = [tie(grad, *after) for grad in grad_in] if after else grad_in
        return ranges_in(place, x, held, in_codes, in_low.shape[2], part, pieces, found)

    by_half = [pair[0] for pair in crossed]
    across_upper = swap(
        add([part[upper] for part in leave] + by_half).astype(BF16), "expert", 2
    )
    arrived_upper = [
        swap(tie(add([part[upper] for part in keep]).astype(BF16), *by_half), "half", d)
        for d, keep in outer
    ]
    in_grad = ranges(0, 2, None, *by_half)
    near = swap(
        tie(
            add([part[upper] for part in stay] + arrived_upper + [across_upper]).astype(BF16),
            in_grad,
        ),
        "expert",
        4,
    )
    across_lower = swap(
        tie(add([part[lower] for part in leave]).astype(BF16), across_upper), "expert", 2
    )
    arrived_lower = [
        swap(
            tie(
                add([part[lower] for part in keep] + [pair[1]]).astype(BF16), *arrived_upper
            ),
            "half",
            d,
        )
        for (d, keep), pair in zip(outer, crossed)
    ]
    in_grad = ranges(2, 4, in_grad)
    near = tie(near, in_grad)
    grad_tokens = scatter_far(
        [part[lower] for part in stay] + arrived_lower + [across_lower, near]
    )

    in_grad = ranges(3, 4, in_grad)
    return (grad_tokens.astype(BF16), in_grad[None], down_grad[None])


def solution(mesh):
    placed = (
        P("expert", None),
        P("expert", "half"),
        P("expert", None),
        P("expert", None),
        P("expert", None, None, "half"),
        P("expert", None, None, "half"),
        P("expert", None, None, "half"),
        P("expert", None, "half"),
        P("expert", None, "half"),
        P("expert", None, "half"),
    )
    return jax.shard_map(
        local,
        mesh=mesh,
        in_specs=placed,
        out_specs=(
            P("expert", "half"),
            P("expert", None, None, "half"),
            P("expert", None, None, "half"),
        ),
        check_vma=False,
    )
```

```python
import functools

import jax
import jax.numpy as jnp
from jax import lax
from jax.experimental import pallas as pl
from jax.experimental.pallas import tpu as pltpu
from jax.sharding import PartitionSpec as P

BF16 = jnp.bfloat16
F32 = jnp.float32
MIB = 1 << 20


def swap(array, axis, distance):
    size = lax.axis_size(axis)
    return lax.ppermute(array, axis, [(i, i ^ distance) for i in range(size)])


def tie(array, *others):
    return lax.optimization_barrier((array, *others))[0]


def far_distances():
    experts = lax.axis_size("expert")
    distances = []
    distance = experts // 2
    while distance > 4:
        distances.append(distance)
        distance //= 2
    return distances


def join(parts):
    return parts[0] if len(parts) == 1 else jnp.concatenate(parts, axis=0)


def gather_far(block):
    parts = [block]
    for distance in far_distances():
        parts.append(swap(join(parts), "expert", distance))
    return parts


def add(parts):
    total = parts[0].astype(F32)
    for part in parts[1:]:
        total = total + part.astype(F32)
    return total


def scatter_far(terms):
    for distance in reversed(far_distances()):
        half = terms[0].shape[0] // 2
        sent = swap(add([part[half:] for part in terms]).astype(BF16), "expert", distance)
        terms = [part[:half] for part in terms] + [sent]
    return add(terms)


def scatter_rows(near, across, cuts):
    rows = near[0].shape[0] // 2
    upper = [swap(add([part[rows:, cut] for part in across]).astype(BF16), "expert", 2) for cut in cuts]
    sent = [
        swap(add([part[rows:, cut] for part in near] + [part_of]).astype(BF16), "expert", 4)
        for cut, part_of in zip(cuts, upper)
    ]
    lower = swap(tie(add([part[:rows] for part in across]).astype(BF16), *upper), "expert", 2)
    return [
        scatter_far([part[:rows, cut] for part in near] + [lower[:, cut], part_of])
        for cut, part_of in zip(cuts, sent)
    ]


def dot(left, right):
    return jnp.dot(left, right, preferred_element_type=F32)


def dot_cols(left, right):
    return lax.dot_general(left, right, (((1,), (1,)), ((), ())), preferred_element_type=F32)


def dot_rows(left, right):
    return lax.dot_general(left, right, (((0,), (0,)), ((), ())), preferred_element_type=F32)


def cost(flops, bytes_accessed):
    return pl.CostEstimate(flops=int(flops), bytes_accessed=int(bytes_accessed), transcendentals=0)


def moved(step, blocks, place):
    return ((step // blocks) ^ place[1]) * blocks + step % blocks


def call(kernel, grid, ins, outs, place, scratch=(), mib=16, flops=0, reuse=None, weight=1e-6):
    total = sum(a.size * a.dtype.itemsize for a, _, _ in ins)
    for shape, kind, _, _ in outs:
        count = 1
        for extent in shape:
            count *= extent
        total += count * jnp.dtype(kind).itemsize

    def spec(block, index):
        if isinstance(block, tuple):
            return pl.BlockSpec(block, index)
        return pl.BlockSpec(memory_space=block)

    in_specs = [spec(block, index) for _, block, index in ins]
    arrays = [a for a, _, _ in ins]
    if reuse is not None:
        in_specs.append(pl.BlockSpec(memory_space=pl.ANY))
        arrays.append(reuse)
    return pl.pallas_call(
        kernel,
        grid_spec=pltpu.PrefetchScalarGridSpec(
            num_scalar_prefetch=1,
            grid=grid,
            in_specs=in_specs,
            out_specs=[spec(block, index) for _, _, block, index in outs],
            scratch_shapes=list(scratch),
        ),
        out_shape=[jax.ShapeDtypeStruct(shape, kind) for shape, kind, _, _ in outs],
        compiler_params=pltpu.CompilerParams(vmem_limit_bytes=mib * MIB),
        cost_estimate=cost(flops * weight, total * weight),
        input_output_aliases={} if reuse is None else {1 + len(ins): 0},
    )(place, *arrays)


def resident(kernel, ins, outs, place, mib=16, flops=0, scratch=()):
    return call(
        kernel,
        (),
        [(a, pltpu.VMEM, None) for a in ins],
        [(shape, kind, pltpu.VMEM, None) for shape, kind in outs],
        place,
        mib=mib,
        flops=flops,
        scratch=scratch,
    )


def step_of(extent):
    return next(size for size in (512, 256, 128) if extent % size == 0)


def tiles(extent, body):
    size = step_of(extent)
    for start in range(0, extent, size):
        body(start)


def whole2(*_):
    return (0, 0)


def whole3(*_):
    return (0, 0, 0)


def whole4(*_):
    return (0, 0, 0, 0)


def pack(place, parts):
    rows = sum(line[0].shape[0] for line in parts)
    cols = sum(part.shape[1] for part in parts[0])

    def kernel(place_ref, *refs):
        refs, out_ref = list(refs[:-1]), refs[-1]
        row = 0
        for line in parts:
            col = 0
            for part in line:
                height, width = part.shape
                out_ref[row : row + height, col : col + width] = refs.pop(0)[...]
                col += width
            row += line[0].shape[0]

    flat = [part for line in parts for part in line]
    return resident(kernel, flat, [((rows, cols), parts[0][0].dtype)], place)[0]


def dequant(place, codes, low, high, halves=1):
    count, height, cols = codes.shape
    groups = low.shape[1]
    size = height // groups
    held = groups // halves

    def kernel(place_ref, code_ref, low_ref, high_ref, out_ref):
        def block(i, carry):
            base = moved(i, held, place_ref) if halves > 1 else i
            source = pl.multiple_of(base * size, size)
            to = pl.multiple_of(i * size, size)
            for k in range(count):
                bottom = low_ref[k, pl.ds(base, 1), :]
                scale = (high_ref[k, pl.ds(base, 1), :] - bottom) * (1.0 / 255.0)
                vals = code_ref[k, pl.ds(source, size), :].astype(F32)
                out_ref[pl.ds(to, size), k * cols : (k + 1) * cols] = (
                    bottom + scale * vals
                ).astype(BF16)
            return carry

        lax.fori_loop(0, groups, block, 0)

    return resident(
        kernel, [codes, low, high], [((height, count * cols), BF16)], place
    )[0]


def dequant_wide(place, codes, low, high, mib):
    count, height, cols = codes.shape
    groups = low.shape[1]
    size = height // groups
    per = next(p for p in (4, 2, 1) if groups % p == 0)
    steps = groups // per
    rows = per * size

    def kernel(place_ref, code_hbm, low_hbm, high_hbm, out_ref, code_ref, low_ref, high_ref, sems):
        ends = [
            pltpu.make_async_copy(low_hbm, low_ref, sems.at[steps]),
            pltpu.make_async_copy(high_hbm, high_ref, sems.at[steps + 1]),
        ]
        blocks = []
        for i in range(steps):
            held = slice(i * rows, (i + 1) * rows)
            blocks.append(
                pltpu.make_async_copy(code_hbm.at[:, held, :], code_ref.at[:, held, :], sems.at[i])
            )
        for copy in ends + blocks:
            copy.start()
        for copy in ends:
            copy.wait()
        for i in range(steps):
            blocks[i].wait()

            def group(j, carry):
                at = i * per + j
                held = pl.ds(pl.multiple_of(at * size, size), size)
                for k in range(count):
                    bottom = low_ref[k, pl.ds(at, 1), :]
                    scale = (high_ref[k, pl.ds(at, 1), :] - bottom) * (1.0 / 255.0)
                    vals = code_ref[k, held, :].astype(F32)
                    out_ref[held, k * cols : (k + 1) * cols] = (bottom + scale * vals).astype(BF16)
                return carry

            lax.fori_loop(0, per, group, 0)

    return call(
        kernel,
        (),
        [(a, pltpu.HBM, None) for a in (codes, low, high)],
        [((height, count * cols), BF16, pltpu.VMEM, None)],
        place,
        scratch=[
            pltpu.VMEM(codes.shape, BF16),
            pltpu.VMEM(low.shape, F32),
            pltpu.VMEM(high.shape, F32),
            pltpu.SemaphoreType.DMA((steps + 2,)),
        ],
        mib=mib,
    )[0]


def hidden_rows(total_groups, size, halves):
    per = total_groups // halves
    while per > 3:
        per = next(f for f in range(2, per + 1) if per % f == 0) and per // next(
            f for f in range(2, per + 1) if per % f == 0
        )
    return per, per * size


def height_of(parts):
    return sum(part.shape[0] for part in parts)


def stacked(refs):
    return jnp.concatenate([ref[...] for ref in refs], axis=0)


def forward_in(place, x, w_in):
    rows = height_of(x)
    width, both = w_in.shape
    hidden = both // 2
    size = step_of(hidden)

    def kernel(place_ref, *refs):
        w_ref, hidden_ref, slope_ref, act_ref = refs[len(x) :]
        left = stacked(refs[: len(x)])

        def body(start):
            gate = dot(left, w_ref[:, pl.ds(start, size)])
            up = dot(left, w_ref[:, pl.ds(hidden + start, size)])
            sig = 1.0 / (1.0 + jnp.exp(-gate))
            act = gate * sig
            hidden_ref[:, pl.ds(start, size)] = (act * up).astype(BF16)
            slope_ref[:, pl.ds(start, size)] = up * sig * (1.0 + gate * (1.0 - sig))
            act_ref[:, pl.ds(start, size)] = act

        tiles(hidden, body)

    shape = (rows, hidden)
    return resident(
        kernel,
        [*x, w_in],
        [(shape, BF16), (shape, F32), (shape, F32)],
        place,
        flops=2 * rows * width * both,
    )


def route_weight(extra, place_ref, experts):
    lane = lax.broadcasted_iota(jnp.int32, extra.shape, 1)
    me = place_ref[0]
    named = (lane == me) | (lane == me + experts) | (lane == me + 2 * experts)
    return jnp.sum(jnp.where(named, extra.astype(F32), 0.0), axis=1, keepdims=True)


def forward_down(place, hidden, w_down, terms, c):
    experts = lax.axis_size("expert")
    rows = hidden[0].shape[0] // 2
    height, quarter = w_down.shape
    size = step_of(quarter)
    held = slice(c * rows, (c + 1) * rows)

    def kernel(place_ref, *refs):
        *hidden_refs, w_ref, own_ref, other_ref, out_own_ref, out_other_ref = refs
        left = jnp.concatenate([ref[...] for ref in hidden_refs], axis=1)
        own = route_weight(own_ref[held, :], place_ref, experts)
        other = route_weight(other_ref[held, :], place_ref, experts)

        def body(start):
            total = dot(left, w_ref[:, pl.ds(start, size)])
            out_own_ref[:, pl.ds(start, size)] = (own * total[:rows]).astype(BF16)
            out_other_ref[:, pl.ds(start, size)] = (other * total[rows:]).astype(BF16)

        tiles(quarter, body)

    return resident(
        kernel,
        [*hidden, w_down, *terms],
        [((rows, quarter), BF16)] * 2,
        place,
        flops=4 * rows * height * quarter,
    )


def backward_down(place, err_own, err_other, w_down, terms, c, halves):
    experts = lax.axis_size("expert")
    rows, quarter = height_of(err_own), err_own[0].shape[1]
    count = len(err_own)
    height = w_down.shape[0]
    own = height // halves
    size = step_of(own)
    held = slice(c * rows, (c + 1) * rows)

    def kernel(place_ref, *refs):
        own_ref, other_ref, w_ref, grad_ref, *outs = refs[2 * count :]
        weight = route_weight(own_ref[held, :], place_ref, experts)
        grad_ref[:rows, :] = (weight * stacked(refs[:count]).astype(F32)).astype(BF16)
        weight = route_weight(other_ref[held, :], place_ref, experts)
        grad_ref[rows:, :] = (weight * stacked(refs[count : 2 * count]).astype(F32)).astype(BF16)
        for d in reversed(range(halves)):

            def body(start):
                at = d * own + start
                part = dot_cols(grad_ref[...], w_ref[pl.ds(at, size), :])
                outs[d][:, pl.ds(start, size)] = part.astype(outs[d].dtype)

            tiles(own, body)

    shape = (2 * rows, own)
    return resident(
        kernel,
        [*err_own, *err_other, *terms, w_down],
        [((2 * rows, quarter), BF16), (shape, F32)] + [(shape, BF16)] * (halves - 1),
        place,
        flops=4 * rows * height * quarter,
    )


def backward_hidden(place, grad_own, arrived, slope, act, w_in, halves):
    both_rows, hidden = slope.shape
    rows = both_rows // 2
    quarter = w_in.shape[0] // halves
    size = step_of(quarter)
    count = len(arrived)

    def kernel(place_ref, grad_own_ref, *refs):
        arrived_refs = refs[:count]
        slope_ref, act_ref, w_ref, grad_ref, *outs = refs[count:]
        grad_hidden = grad_own_ref[...]
        for ref in arrived_refs:
            grad_hidden += ref[...].astype(F32)
        grad_ref[:, :hidden] = (grad_hidden * slope_ref[...]).astype(BF16)
        grad_ref[:, hidden:] = (grad_hidden * act_ref[...]).astype(BF16)
        for d in range(halves):

            def body(start):
                at = pl.multiple_of((place_ref[1] ^ d) * quarter + start, size)
                part = dot_cols(grad_ref[...], w_ref[pl.ds(at, size), :]).astype(BF16)
                outs[2 * d][:, pl.ds(start, size)] = part[:rows]
                outs[2 * d + 1][:, pl.ds(start, size)] = part[rows:]

            tiles(quarter, body)

    grad, *parts = resident(
        kernel,
        [grad_own, *arrived, slope, act, w_in],
        [((both_rows, 2 * hidden), BF16)] + [((rows, quarter), BF16)] * (2 * halves),
        place,
        flops=4 * both_rows * hidden * quarter * halves,
    )
    return grad, parts


def ends(grad, codes):
    upper = jnp.sum(grad * codes.astype(F32), axis=0, keepdims=True) * (1.0 / 255.0)
    return jnp.sum(grad, axis=0, keepdims=True) - upper, upper


def range_tile(left, right, size, step, codes, store):
    turned = left.T
    for start in range(0, right.shape[1], step):
        cols = slice(start, start + step)
        grad = dot(turned, right[:, cols])
        for g in range(turned.shape[0] // size):
            cut = slice(g * size, (g + 1) * size)
            low, high = ends(grad[cut], codes(cut, cols))
            store(g, cols, low, high)


def ranges_down(place, hidden, grad, codes, groups, halves, found=None):
    _, height, quarter = codes.shape
    size = height // groups
    per, rows = hidden_rows(groups, size, halves)
    blocks = height // halves // rows
    earlier = [] if found is None else [found]

    def kernel(place_ref, *refs):
        hidden_refs = refs[:halves]
        grad_ref, code_ref, *found_refs, out_ref = refs[halves:]
        step = pl.program_id(0)
        base = moved(step, blocks, place_ref) * per

        def store(g, cols, low, high):
            for k, value in ((0, low), (1, high)):
                for ref in found_refs:
                    value += ref[k, pl.ds(base + g, 1), cols]
                out_ref[k, pl.ds(base + g, 1), cols] = value

        for d in range(halves):

            @pl.when(step // blocks == d)
            def _():
                range_tile(
                    hidden_refs[d][...],
                    grad_ref,
                    size,
                    256,
                    lambda cut, cols: code_ref[0, cut, cols],
                    store,
                )

    shape = (2, groups, quarter)
    return call(
        kernel,
        (height // rows,),
        [(part, (part.shape[0], rows), lambda i, p: (0, i % blocks)) for part in hidden]
        + [
            (grad, pltpu.VMEM, None),
            (codes, (1, rows, quarter), lambda i, p: (0, moved(i, blocks, p), 0)),
        ]
        + [(array, pltpu.VMEM, None) for array in earlier],
        [(shape, F32, shape, whole3)],
        place,
        mib=20,
        flops=2 * grad.shape[0] * height * quarter,
    )[0]


def ranges_in(place, x, grads, codes, groups, part, parts, found):
    _, _, width, hidden = codes.shape
    size = width // groups
    held = groups // parts
    per = next(p for p in (4, 2, 1) if held % p == 0)
    rows = per * size
    blocks = held // per
    flat = [array for parts in x for array in parts]
    chunks = len(grads)
    tokens, both = grads[0].shape
    wide = 256 if hidden % 256 == 0 else hidden

    def kernel(place_ref, *refs):
        x_refs = refs[: len(flat)]
        grad_refs = refs[len(flat) : len(flat) + chunks]
        code_ref, out_ref, right_ref = refs[len(flat) + chunks], refs[-2], refs[-1]
        base = pl.program_id(0) * per

        @pl.when(pl.program_id(0) == 0)
        def _():
            for c in range(chunks):
                right_ref[c * tokens : (c + 1) * tokens, :] = grad_refs[c][...]

        def split(cols):
            k = cols.start // hidden
            return k, slice(cols.start - k * hidden, cols.stop - k * hidden)

        def codes_at(cut, cols):
            k, cols = split(cols)
            return code_ref[0, k, cut, cols]

        def store(g, cols, low, high):
            k, cols = split(cols)
            out_ref[2 * k, pl.ds(base + g, 1), cols] = low
            out_ref[2 * k + 1, pl.ds(base + g, 1), cols] = high

        left = jnp.concatenate([ref[...] for ref in x_refs], axis=0)
        range_tile(left, right_ref, size, wide, codes_at, store)

    shape = (4, groups, hidden)
    return call(
        kernel,
        (blocks,),
        [(a, (a.shape[0], rows), lambda i, p: (0, part * blocks + i)) for a in flat]
        + [(grad, pltpu.VMEM, None) for grad in grads]
        + [(codes, (1, 2, rows, hidden), lambda i, p: (0, 0, part * blocks + i, 0))],
        [(shape, F32, (4, held, hidden), lambda i, p: (0, part, 0))],
        place,
        scratch=[pltpu.VMEM((chunks * tokens, both), BF16)],
        mib=20,
        flops=2 * sum(grad.size for grad in grads) * (width // parts),
        reuse=found,
    )[0]


def prepare(place, routes, route_scores, extra):
    experts = lax.axis_size("expert")
    rows, top_count = routes.shape

    def kernel(place_ref, route_ref, score_ref, out_ref):
        scores = score_ref[...]
        weights = scores / jnp.sum(scores, axis=1, keepdims=True)
        names = route_ref[...]
        lane = lax.broadcasted_iota(jnp.int32, (rows, extra), 1)
        third = jnp.where(lane < experts, 0, jnp.where(lane < 2 * experts, 1, 2))
        expert = lane - third * experts
        table = jnp.zeros((rows, extra), F32)
        for k in range(top_count):
            table += jnp.where(expert == names[:, k : k + 1], weights[:, k : k + 1], 0.0)
        top = table.astype(BF16).astype(F32)
        middle = (table - top).astype(BF16).astype(F32)
        bottom = table - top - middle
        terms = jnp.where(third == 0, top, jnp.where(third == 1, middle, bottom))
        out_ref[...] = terms.astype(BF16)

    return resident(kernel, [routes, route_scores], [((rows, extra), BF16)], place)[0]


def local(
    tokens, target, routes, route_scores, in_codes, in_low, in_high, down_codes, down_low, down_high
):
    experts = lax.axis_size("expert")
    halves = lax.axis_size("half")
    place = jnp.stack([lax.axis_index("expert"), lax.axis_index("half")]).astype(jnp.int32)
    quarter = target.shape[1]
    parts = range(halves)
    chunks = (0, 1)

    far = join(gather_far(tokens)[1:])
    near_own = swap(tokens, "expert", 4)
    across_own = swap(tokens, "expert", 2)
    extra = -(-3 * experts // 128) * 128
    terms = prepare(place, routes, route_scores, extra)
    w_in = dequant_wide(place, in_codes[0], tie(in_low, terms)[0], in_high[0], 30)
    near_own = tie(near_own, w_in)
    across_near = swap(near_own, "expert", 2)
    far = tie(far, w_in, across_own)
    near_far = swap(far, "expert", 4)
    across_far = swap(far, "expert", 2)
    terms = join(gather_far(terms))
    near_far = tie(near_far, across_near, terms)
    first = pack(place, [[tokens], [far], [near_own]])
    first_other = swap(first, "expert", 1)
    across_last = swap(near_far, "expert", 2)
    near_other = swap(near_far, "expert", 1)
    x = [[first, near_far, first_other, near_other]]
    near_terms = swap(terms, "expert", 4)

    hidden, slope, act = [], [], []
    for c in chunks:
        if c == 1:
            second = pack(place, [[across_own], [tie(across_far, near_other)], [across_near]])
            second_other = swap(second, "expert", 1)
            across_last = tie(across_last, hidden[0][0], near_terms, second_other)
            x.append([second, across_last, second_other, swap(across_last, "expert", 1)])
        own, chunk_slope, chunk_act = forward_in(place, x[c], w_in)
        if c == 1:
            w_down = dequant(place, down_codes, tie(down_low, own), down_high, halves)
        hidden.append([own] + [swap(own, "half", d) for d in parts if d])
        slope.append(chunk_slope)
        act.append(chunk_act)
    terms = jnp.concatenate([terms, near_terms], axis=0)
    terms = jnp.concatenate([terms, swap(terms, "expert", 2)], axis=0)
    terms = (terms, swap(terms, "expert", 1))

    sums = []
    for c in chunks:
        if c == 1:
            hidden[1][1:] = [tie(part, sums[0][0]) for part in hidden[1][1:]]
        out_own, out_other = forward_down(place, hidden[c], w_down, terms, c)
        sums.append([out_own, swap(out_other, "expert", 1)])
    middle = quarter // 2
    cuts = [slice(0, middle), slice(middle, quarter)]
    mixed = scatter_rows(sums[0], sums[1], cuts)
    error = [
        (mixed[f] - target[:, cuts[f]].astype(F32)).astype(BF16) for f in range(len(cuts))
    ]

    kept = pack(place, [list(line) for line in zip(*[gather_far(part) for part in error])])
    near = swap(kept, "expert", 4)
    across_kept = swap(kept, "expert", 2)
    kept_other = swap(kept, "expert", 1)
    near = tie(near, across_kept, kept_other)
    across_near = swap(near, "expert", 2)
    across_other = swap(across_kept, "expert", 1)
    errors = [([kept, near], [kept_other, swap(near, "expert", 1)])]
    grads, grad_own, arrived = [], [], []
    down_groups = down_low.shape[1]
    for c in chunks:
        if c == 1:
            across_near = tie(across_near, grads[0], across_other)
            down_grad = ranges_down(place, hidden[0], grads[0], down_codes, down_groups, halves)
            last_other = tie(swap(across_near, "expert", 1), down_grad, *arrived[0])
            errors.append(([across_kept, across_near], [across_other, last_other]))
        grad, own, *others = backward_down(place, *errors[c], w_down, terms, c, halves)
        grads.append(grad)
        grad_own.append(own)
        arrived.append([swap(other, "half", d + 1) for d, other in enumerate(others)])

    grad_in, kinds = [], []
    down_grad = ranges_down(
        place, hidden[1], grads[1], down_codes, down_groups, halves, down_grad
    )
    for c in chunks:
        if c == 1:
            arrived[1] = [tie(part, grad_in[0], down_grad) for part in arrived[1]]
        grad, found = backward_hidden(
            place, grad_own[c], arrived[c], slope[c], act[c], w_in, halves
        )
        grad_in.append(grad)
        kinds.append(found)
    kinds[0] = [tie(part, grad_in[1]) for part in kinds[0]]
    rows = height_of(errors[0][0])
    lower, upper = slice(0, rows // 2), slice(rows // 2, rows)
    keep, go = [
        [[found[2 * d], swap(found[2 * d + 1], "expert", 1)] for d in parts] for found in kinds
    ]
    stay, leave = keep[0], go[0]
    outer = [(d, keep[d]) for d in parts if d]
    crossed = [
        (
            swap(add([part[upper] for part in go[d]]).astype(BF16), "half", d),
            swap(add([part[lower] for part in go[d]]).astype(BF16), "expert", 2),
        )
        for d in parts
        if d
    ]

    def ranges(part, pieces, found, *after):
        held = [tie(grad, *after) for grad in grad_in] if after else grad_in
        return ranges_in(place, x, held, in_codes, in_low.shape[2], part, pieces, found)

    by_half = [pair[0] for pair in crossed]
    across_upper = swap(
        add([part[upper] for part in leave] + by_half).astype(BF16), "expert", 2
    )
    arrived_upper = [
        swap(tie(add([part[upper] for part in keep]).astype(BF16), *by_half), "half", d)
        for d, keep in outer
    ]
    in_grad = ranges(0, 2, None, *by_half)
    near = swap(
        tie(
            add([part[upper] for part in stay] + arrived_upper + [across_upper]).astype(BF16),
            in_grad,
        ),
        "expert",
        4,
    )
    across_lower = swap(
        tie(add([part[lower] for part in leave]).astype(BF16), across_upper), "expert", 2
    )
    arrived_lower = [
        swap(
            tie(
                add([part[lower] for part in keep] + [pair[1]]).astype(BF16), *arrived_upper
            ),
            "half",
            d,
        )
        for (d, keep), pair in zip(outer, crossed)
    ]
    in_grad = ranges(2, 4, in_grad)
    near = tie(near, in_grad)
    grad_tokens = scatter_far(
        [part[lower] for part in stay] + arrived_lower + [across_lower, near]
    )

    in_grad = ranges(3, 4, in_grad)
    return (grad_tokens.astype(BF16), in_grad[None], down_grad[None])


def solution(mesh):
    placed = (
        P("expert", None),
        P("expert", "half"),
        P("expert", None),
        P("expert", None),
        P("expert", None, None, "half"),
        P("expert", None, None, "half"),
        P("expert", None, None, "half"),
        P("expert", None, "half"),
        P("expert", None, "half"),
        P("expert", None, "half"),
    )
    return jax.shard_map(
        local,
        mesh=mesh,
        in_specs=placed,
        out_specs=(
            P("expert", "half"),
            P("expert", None, None, "half"),
            P("expert", None, None, "half"),
        ),
        check_vma=False,
    )
```

```python
import functools

import jax
import jax.numpy as jnp
from jax import lax
from jax.experimental import pallas as pl
from jax.experimental.pallas import tpu as pltpu
from jax.sharding import PartitionSpec as P

BF16 = jnp.bfloat16
F32 = jnp.float32
MIB = 1 << 20


def swap(array, axis, distance):
    size = lax.axis_size(axis)
    return lax.ppermute(array, axis, [(i, i ^ distance) for i in range(size)])


def tie(array, *others):
    return lax.optimization_barrier((array, *others))[0]


def far_distances():
    experts = lax.axis_size("expert")
    distances = []
    distance = experts // 2
    while distance > 4:
        distances.append(distance)
        distance //= 2
    return distances


def join(parts):
    return parts[0] if len(parts) == 1 else jnp.concatenate(parts, axis=0)


def gather_far(block):
    parts = [block]
    for distance in far_distances():
        parts.append(swap(join(parts), "expert", distance))
    return parts


def add(parts):
    total = parts[0].astype(F32)
    for part in parts[1:]:
        total = total + part.astype(F32)
    return total


def scatter_far(terms):
    for distance in reversed(far_distances()):
        half = terms[0].shape[0] // 2
        sent = swap(add([part[half:] for part in terms]).astype(BF16), "expert", distance)
        terms = [part[:half] for part in terms] + [sent]
    return add(terms)


def scatter_rows(near, across, cuts):
    rows = near[0].shape[0] // 2
    upper = [swap(add([part[rows:, cut] for part in across]).astype(BF16), "expert", 2) for cut in cuts]
    sent = [
        swap(add([part[rows:, cut] for part in near] + [part_of]).astype(BF16), "expert", 4)
        for cut, part_of in zip(cuts, upper)
    ]
    lower = swap(tie(add([part[:rows] for part in across]).astype(BF16), *upper), "expert", 2)
    return [
        scatter_far([part[:rows, cut] for part in near] + [lower[:, cut], part_of])
        for cut, part_of in zip(cuts, sent)
    ]


def dot(left, right):
    return jnp.dot(left, right, preferred_element_type=F32)


def dot_cols(left, right):
    return lax.dot_general(left, right, (((1,), (1,)), ((), ())), preferred_element_type=F32)


def dot_rows(left, right):
    return lax.dot_general(left, right, (((0,), (0,)), ((), ())), preferred_element_type=F32)


def cost(flops, bytes_accessed):
    return pl.CostEstimate(flops=int(flops), bytes_accessed=int(bytes_accessed), transcendentals=0)


def moved(step, blocks, place):
    return ((step // blocks) ^ place[1]) * blocks + step % blocks


def call(kernel, grid, ins, outs, place, scratch=(), mib=16, flops=0, reuse=None, weight=1e-6):
    total = sum(a.size * a.dtype.itemsize for a, _, _ in ins)
    for shape, kind, _, _ in outs:
        count = 1
        for extent in shape:
            count *= extent
        total += count * jnp.dtype(kind).itemsize

    def spec(block, index):
        if isinstance(block, tuple):
            return pl.BlockSpec(block, index)
        return pl.BlockSpec(memory_space=block)

    in_specs = [spec(block, index) for _, block, index in ins]
    arrays = [a for a, _, _ in ins]
    if reuse is not None:
        in_specs.append(pl.BlockSpec(memory_space=pl.ANY))
        arrays.append(reuse)
    return pl.pallas_call(
        kernel,
        grid_spec=pltpu.PrefetchScalarGridSpec(
            num_scalar_prefetch=1,
            grid=grid,
            in_specs=in_specs,
            out_specs=[spec(block, index) for _, _, block, index in outs],
            scratch_shapes=list(scratch),
        ),
        out_shape=[jax.ShapeDtypeStruct(shape, kind) for shape, kind, _, _ in outs],
        compiler_params=pltpu.CompilerParams(vmem_limit_bytes=mib * MIB),
        cost_estimate=cost(flops * weight, total * weight),
        input_output_aliases={} if reuse is None else {1 + len(ins): 0},
    )(place, *arrays)


def resident(kernel, ins, outs, place, mib=16, flops=0, scratch=()):
    return call(
        kernel,
        (),
        [(a, pltpu.VMEM, None) for a in ins],
        [(shape, kind, pltpu.VMEM, None) for shape, kind in outs],
        place,
        mib=mib,
        flops=flops,
        scratch=scratch,
    )


def step_of(extent):
    return next(size for size in (512, 256, 128) if extent % size == 0)


def tiles(extent, body):
    size = step_of(extent)
    for start in range(0, extent, size):
        body(start)


def whole2(*_):
    return (0, 0)


def whole3(*_):
    return (0, 0, 0)


def whole4(*_):
    return (0, 0, 0, 0)


def pack(place, parts):
    rows = sum(line[0].shape[0] for line in parts)
    cols = sum(part.shape[1] for part in parts[0])

    def kernel(place_ref, *refs):
        refs, out_ref = list(refs[:-1]), refs[-1]
        row = 0
        for line in parts:
            col = 0
            for part in line:
                height, width = part.shape
                out_ref[row : row + height, col : col + width] = refs.pop(0)[...]
                col += width
            row += line[0].shape[0]

    flat = [part for line in parts for part in line]
    return resident(kernel, flat, [((rows, cols), parts[0][0].dtype)], place)[0]


def dequant(place, codes, low, high, halves=1):
    count, height, cols = codes.shape
    groups = low.shape[1]
    size = height // groups
    held = groups // halves

    def kernel(place_ref, code_ref, low_ref, high_ref, out_ref):
        def block(i, carry):
            base = moved(i, held, place_ref) if halves > 1 else i
            source = pl.multiple_of(base * size, size)
            to = pl.multiple_of(i * size, size)
            for k in range(count):
                bottom = low_ref[k, pl.ds(base, 1), :]
                scale = (high_ref[k, pl.ds(base, 1), :] - bottom) * (1.0 / 255.0)
                vals = code_ref[k, pl.ds(source, size), :].astype(F32)
                out_ref[pl.ds(to, size), k * cols : (k + 1) * cols] = (
                    bottom + scale * vals
                ).astype(BF16)
            return carry

        lax.fori_loop(0, groups, block, 0)

    return resident(
        kernel, [codes, low, high], [((height, count * cols), BF16)], place
    )[0]


def dequant_wide(place, codes, low, high, mib):
    count, height, cols = codes.shape
    groups = low.shape[1]
    size = height // groups
    per = next(p for p in (4, 2, 1) if groups % p == 0)
    steps = groups // per
    rows = per * size

    def kernel(place_ref, code_hbm, low_hbm, high_hbm, out_ref, code_ref, low_ref, high_ref, sems):
        ends = [
            pltpu.make_async_copy(low_hbm, low_ref, sems.at[steps]),
            pltpu.make_async_copy(high_hbm, high_ref, sems.at[steps + 1]),
        ]
        blocks = []
        for i in range(steps):
            held = slice(i * rows, (i + 1) * rows)
            blocks.append(
                pltpu.make_async_copy(code_hbm.at[:, held, :], code_ref.at[:, held, :], sems.at[i])
            )
        for copy in ends + blocks:
            copy.start()
        for copy in ends:
            copy.wait()
        for i in range(steps):
            blocks[i].wait()

            def group(j, carry):
                at = i * per + j
                held = pl.ds(pl.multiple_of(at * size, size), size)
                for k in range(count):
                    bottom = low_ref[k, pl.ds(at, 1), :]
                    scale = (high_ref[k, pl.ds(at, 1), :] - bottom) * (1.0 / 255.0)
                    vals = code_ref[k, held, :].astype(F32)
                    out_ref[held, k * cols : (k + 1) * cols] = (bottom + scale * vals).astype(BF16)
                return carry

            lax.fori_loop(0, per, group, 0)

    return call(
        kernel,
        (),
        [(a, pltpu.HBM, None) for a in (codes, low, high)],
        [((height, count * cols), BF16, pltpu.VMEM, None)],
        place,
        scratch=[
            pltpu.VMEM(codes.shape, BF16),
            pltpu.VMEM(low.shape, F32),
            pltpu.VMEM(high.shape, F32),
            pltpu.SemaphoreType.DMA((steps + 2,)),
        ],
        mib=mib,
    )[0]


def hidden_rows(total_groups, size, halves):
    per = total_groups // halves
    while per > 3:
        per = next(f for f in range(2, per + 1) if per % f == 0) and per // next(
            f for f in range(2, per + 1) if per % f == 0
        )
    return per, per * size


def height_of(parts):
    return sum(part.shape[0] for part in parts)


def stacked(refs):
    return jnp.concatenate([ref[...] for ref in refs], axis=0)


def forward_in(place, x, w_in):
    rows = height_of(x)
    width, both = w_in.shape
    hidden = both // 2
    size = step_of(hidden)

    def kernel(place_ref, *refs):
        w_ref, hidden_ref, slope_ref, act_ref = refs[len(x) :]
        left = stacked(refs[: len(x)])

        def body(start):
            gate = dot(left, w_ref[:, pl.ds(start, size)])
            up = dot(left, w_ref[:, pl.ds(hidden + start, size)])
            sig = 1.0 / (1.0 + jnp.exp(-gate))
            act = gate * sig
            hidden_ref[:, pl.ds(start, size)] = (act * up).astype(BF16)
            slope_ref[:, pl.ds(start, size)] = up * sig * (1.0 + gate * (1.0 - sig))
            act_ref[:, pl.ds(start, size)] = act

        tiles(hidden, body)

    shape = (rows, hidden)
    return resident(
        kernel,
        [*x, w_in],
        [(shape, BF16), (shape, F32), (shape, F32)],
        place,
        flops=2 * rows * width * both,
    )


def route_weight(extra, place_ref, experts):
    lane = lax.broadcasted_iota(jnp.int32, extra.shape, 1)
    me = place_ref[0]
    named = (lane == me) | (lane == me + experts) | (lane == me + 2 * experts)
    return jnp.sum(jnp.where(named, extra.astype(F32), 0.0), axis=1, keepdims=True)


def forward_down(place, hidden, w_down, terms, c):
    experts = lax.axis_size("expert")
    rows = hidden[0].shape[0] // 2
    height, quarter = w_down.shape
    size = step_of(quarter)
    held = slice(c * rows, (c + 1) * rows)

    def kernel(place_ref, *refs):
        *hidden_refs, w_ref, own_ref, other_ref, out_own_ref, out_other_ref = refs
        left = jnp.concatenate([ref[...] for ref in hidden_refs], axis=1)
        own = route_weight(own_ref[held, :], place_ref, experts)
        other = route_weight(other_ref[held, :], place_ref, experts)

        def body(start):
            total = dot(left, w_ref[:, pl.ds(start, size)])
            out_own_ref[:, pl.ds(start, size)] = (own * total[:rows]).astype(BF16)
            out_other_ref[:, pl.ds(start, size)] = (other * total[rows:]).astype(BF16)

        tiles(quarter, body)

    return resident(
        kernel,
        [*hidden, w_down, *terms],
        [((rows, quarter), BF16)] * 2,
        place,
        flops=4 * rows * height * quarter,
    )


def backward_down(place, err_own, err_other, w_down, terms, c, halves):
    experts = lax.axis_size("expert")
    rows, quarter = height_of(err_own), err_own[0].shape[1]
    count = len(err_own)
    height = w_down.shape[0]
    own = height // halves
    size = step_of(own)
    held = slice(c * rows, (c + 1) * rows)

    def kernel(place_ref, *refs):
        own_ref, other_ref, w_ref, grad_ref, *outs = refs[2 * count :]
        weight = route_weight(own_ref[held, :], place_ref, experts)
        grad_ref[:rows, :] = (weight * stacked(refs[:count]).astype(F32)).astype(BF16)
        weight = route_weight(other_ref[held, :], place_ref, experts)
        grad_ref[rows:, :] = (weight * stacked(refs[count : 2 * count]).astype(F32)).astype(BF16)
        for d in reversed(range(halves)):

            def body(start):
                at = d * own + start
                part = dot_cols(grad_ref[...], w_ref[pl.ds(at, size), :])
                outs[d][:, pl.ds(start, size)] = part.astype(outs[d].dtype)

            tiles(own, body)

    shape = (2 * rows, own)
    return resident(
        kernel,
        [*err_own, *err_other, *terms, w_down],
        [((2 * rows, quarter), BF16), (shape, F32)] + [(shape, BF16)] * (halves - 1),
        place,
        flops=4 * rows * height * quarter,
    )


def backward_hidden(place, grad_own, arrived, slope, act, w_in, halves):
    both_rows, hidden = slope.shape
    rows = both_rows // 2
    quarter = w_in.shape[0] // halves
    size = step_of(quarter)
    count = len(arrived)

    def kernel(place_ref, grad_own_ref, *refs):
        arrived_refs = refs[:count]
        slope_ref, act_ref, w_ref, grad_ref, *outs = refs[count:]
        grad_hidden = grad_own_ref[...]
        for ref in arrived_refs:
            grad_hidden += ref[...].astype(F32)
        grad_ref[:, :hidden] = (grad_hidden * slope_ref[...]).astype(BF16)
        grad_ref[:, hidden:] = (grad_hidden * act_ref[...]).astype(BF16)
        for d in range(halves):

            def body(start):
                at = pl.multiple_of((place_ref[1] ^ d) * quarter + start, size)
                part = dot_cols(grad_ref[...], w_ref[pl.ds(at, size), :]).astype(BF16)
                outs[2 * d][:, pl.ds(start, size)] = part[:rows]
                outs[2 * d + 1][:, pl.ds(start, size)] = part[rows:]

            tiles(quarter, body)

    grad, *parts = resident(
        kernel,
        [grad_own, *arrived, slope, act, w_in],
        [((both_rows, 2 * hidden), BF16)] + [((rows, quarter), BF16)] * (2 * halves),
        place,
        flops=4 * both_rows * hidden * quarter * halves,
    )
    return grad, parts


def ends(grad, codes):
    upper = jnp.sum(grad * codes.astype(F32), axis=0, keepdims=True) * (1.0 / 255.0)
    return jnp.sum(grad, axis=0, keepdims=True) - upper, upper


def range_tile(left, right, size, step, codes, store):
    turned = left.T
    for start in range(0, right.shape[1], step):
        cols = slice(start, start + step)
        grad = dot(turned, right[:, cols])
        for g in range(turned.shape[0] // size):
            cut = slice(g * size, (g + 1) * size)
            low, high = ends(grad[cut], codes(cut, cols))
            store(g, cols, low, high)


def ranges_down(place, hidden, grad, codes, groups, halves, found=None):
    _, height, quarter = codes.shape
    size = height // groups
    per, rows = hidden_rows(groups, size, halves)
    blocks = height // halves // rows
    earlier = [] if found is None else [found]

    def kernel(place_ref, *refs):
        hidden_refs = refs[:halves]
        grad_ref, code_ref, *found_refs, out_ref = refs[halves:]
        step = pl.program_id(0)
        base = moved(step, blocks, place_ref) * per

        def store(g, cols, low, high):
            for k, value in ((0, low), (1, high)):
                for ref in found_refs:
                    value += ref[k, pl.ds(base + g, 1), cols]
                out_ref[k, pl.ds(base + g, 1), cols] = value

        for d in range(halves):

            @pl.when(step // blocks == d)
            def _():
                range_tile(
                    hidden_refs[d][...],
                    grad_ref,
                    size,
                    256,
                    lambda cut, cols: code_ref[0, cut, cols],
                    store,
                )

    shape = (2, groups, quarter)
    return call(
        kernel,
        (height // rows,),
        [(part, (part.shape[0], rows), lambda i, p: (0, i % blocks)) for part in hidden]
        + [
            (grad, pltpu.VMEM, None),
            (codes, (1, rows, quarter), lambda i, p: (0, moved(i, blocks, p), 0)),
        ]
        + [(array, pltpu.VMEM, None) for array in earlier],
        [(shape, F32, shape, whole3)],
        place,
        mib=20,
        flops=2 * grad.shape[0] * height * quarter,
    )[0]


def ranges_in(place, x, grads, codes, groups, part, parts, found):
    _, _, width, hidden = codes.shape
    size = width // groups
    held = groups // parts
    per = next(p for p in (4, 2, 1) if held % p == 0)
    rows = per * size
    blocks = held // per
    flat = [array for parts in x for array in parts]
    chunks = len(grads)
    tokens, both = grads[0].shape
    wide = 256 if hidden % 256 == 0 else hidden

    def kernel(place_ref, *refs):
        x_refs = refs[: len(flat)]
        grad_refs = refs[len(flat) : len(flat) + chunks]
        code_ref, out_ref, right_ref = refs[len(flat) + chunks], refs[-2], refs[-1]
        base = pl.program_id(0) * per

        @pl.when(pl.program_id(0) == 0)
        def _():
            for c in range(chunks):
                right_ref[c * tokens : (c + 1) * tokens, :] = grad_refs[c][...]

        def split(cols):
            k = cols.start // hidden
            return k, slice(cols.start - k * hidden, cols.stop - k * hidden)

        def codes_at(cut, cols):
            k, cols = split(cols)
            return code_ref[0, k, cut, cols]

        def store(g, cols, low, high):
            k, cols = split(cols)
            out_ref[2 * k, pl.ds(base + g, 1), cols] = low
            out_ref[2 * k + 1, pl.ds(base + g, 1), cols] = high

        left = jnp.concatenate([ref[...] for ref in x_refs], axis=0)
        range_tile(left, right_ref, size, wide, codes_at, store)

    shape = (4, groups, hidden)
    return call(
        kernel,
        (blocks,),
        [(a, (a.shape[0], rows), lambda i, p: (0, part * blocks + i)) for a in flat]
        + [(grad, pltpu.VMEM, None) for grad in grads]
        + [(codes, (1, 2, rows, hidden), lambda i, p: (0, 0, part * blocks + i, 0))],
        [(shape, F32, (4, held, hidden), lambda i, p: (0, part, 0))],
        place,
        scratch=[pltpu.VMEM((chunks * tokens, both), BF16)],
        mib=20,
        flops=2 * sum(grad.size for grad in grads) * (width // parts),
        reuse=found,
    )[0]


def prepare(place, routes, route_scores, extra):
    experts = lax.axis_size("expert")
    rows, top_count = routes.shape

    def kernel(place_ref, route_ref, score_ref, out_ref):
        scores = score_ref[...]
        weights = scores / jnp.sum(scores, axis=1, keepdims=True)
        names = route_ref[...]
        lane = lax.broadcasted_iota(jnp.int32, (rows, extra), 1)
        third = jnp.where(lane < experts, 0, jnp.where(lane < 2 * experts, 1, 2))
        expert = lane - third * experts
        table = jnp.zeros((rows, extra), F32)
        for k in range(top_count):
            table += jnp.where(expert == names[:, k : k + 1], weights[:, k : k + 1], 0.0)
        top = table.astype(BF16).astype(F32)
        middle = (table - top).astype(BF16).astype(F32)
        bottom = table - top - middle
        terms = jnp.where(third == 0, top, jnp.where(third == 1, middle, bottom))
        out_ref[...] = terms.astype(BF16)

    return resident(kernel, [routes, route_scores], [((rows, extra), BF16)], place)[0]


def local(
    tokens, target, routes, route_scores, in_codes, in_low, in_high, down_codes, down_low, down_high
):
    experts = lax.axis_size("expert")
    halves = lax.axis_size("half")
    place = jnp.stack([lax.axis_index("expert"), lax.axis_index("half")]).astype(jnp.int32)
    quarter = target.shape[1]
    parts = range(halves)
    chunks = (0, 1)

    far = join(gather_far(tokens)[1:])
    near_own = swap(tokens, "expert", 4)
    across_own = swap(tokens, "expert", 2)
    extra = -(-3 * experts // 128) * 128
    terms = prepare(place, routes, route_scores, extra)
    w_in = dequant_wide(place, in_codes[0], tie(in_low, terms)[0], in_high[0], 30)
    near_own = tie(near_own, w_in)
    across_near = swap(near_own, "expert", 2)
    far = tie(far, w_in, across_own)
    near_far = swap(far, "expert", 4)
    across_far = swap(far, "expert", 2)
    near_far = tie(near_far, across_near)
    first = pack(place, [[tokens], [far], [near_own]])
    first_other = swap(first, "expert", 1)
    across_last = swap(near_far, "expert", 2)
    near_other = swap(near_far, "expert", 1)
    x = [[first, near_far, first_other, near_other]]

    hidden, slope, act = [], [], []
    for c in chunks:
        if c == 1:
            second = pack(place, [[across_own], [tie(across_far, near_other)], [across_near]])
            second_other = swap(second, "expert", 1)
            across_last = tie(across_last, hidden[0][0], second_other)
            x.append([second, across_last, second_other, swap(across_last, "expert", 1)])
        own, chunk_slope, chunk_act = forward_in(place, x[c], w_in)
        if c == 1:
            w_down = dequant(place, down_codes, tie(down_low, own), down_high, halves)
        hidden.append([own] + [swap(own, "half", d) for d in parts if d])
        slope.append(chunk_slope)
        act.append(chunk_act)
    terms = join(gather_far(tie(terms, hidden[1][0])))
    for distance in (4, 2):
        terms = jnp.concatenate([terms, swap(terms, "expert", distance)], axis=0)
    terms = (terms, swap(terms, "expert", 1))

    sums = []
    for c in chunks:
        if c == 1:
            hidden[1][1:] = [tie(part, sums[0][0]) for part in hidden[1][1:]]
        out_own, out_other = forward_down(place, hidden[c], w_down, terms, c)
        sums.append([out_own, swap(out_other, "expert", 1)])
    middle = quarter // 2
    cuts = [slice(0, middle), slice(middle, quarter)]
    mixed = scatter_rows(sums[0], sums[1], cuts)
    error = [
        (mixed[f] - target[:, cuts[f]].astype(F32)).astype(BF16) for f in range(len(cuts))
    ]

    kept = pack(place, [list(line) for line in zip(*[gather_far(part) for part in error])])
    near = swap(kept, "expert", 4)
    across_kept = swap(kept, "expert", 2)
    kept_other = swap(kept, "expert", 1)
    near = tie(near, across_kept, kept_other)
    across_near = swap(near, "expert", 2)
    across_other = swap(across_kept, "expert", 1)
    errors = [([kept, near], [kept_other, swap(near, "expert", 1)])]
    grads, grad_own, arrived = [], [], []
    down_groups = down_low.shape[1]
    for c in chunks:
        if c == 1:
            across_near = tie(across_near, grads[0], across_other)
            down_grad = ranges_down(place, hidden[0], grads[0], down_codes, down_groups, halves)
            last_other = tie(swap(across_near, "expert", 1), down_grad, *arrived[0])
            errors.append(([across_kept, across_near], [across_other, last_other]))
        grad, own, *others = backward_down(place, *errors[c], w_down, terms, c, halves)
        grads.append(grad)
        grad_own.append(own)
        arrived.append([swap(other, "half", d + 1) for d, other in enumerate(others)])

    grad_in, kinds = [], []
    down_grad = ranges_down(
        place, hidden[1], grads[1], down_codes, down_groups, halves, down_grad
    )
    for c in chunks:
        if c == 1:
            arrived[1] = [tie(part, grad_in[0], down_grad) for part in arrived[1]]
        grad, found = backward_hidden(
            place, grad_own[c], arrived[c], slope[c], act[c], w_in, halves
        )
        grad_in.append(grad)
        kinds.append(found)
    kinds[0] = [tie(part, grad_in[1]) for part in kinds[0]]
    rows = height_of(errors[0][0])
    lower, upper = slice(0, rows // 2), slice(rows // 2, rows)
    keep, go = [
        [[found[2 * d], swap(found[2 * d + 1], "expert", 1)] for d in parts] for found in kinds
    ]
    stay, leave = keep[0], go[0]
    outer = [(d, keep[d]) for d in parts if d]
    crossed = [
        (
            swap(add([part[upper] for part in go[d]]).astype(BF16), "half", d),
            swap(add([part[lower] for part in go[d]]).astype(BF16), "expert", 2),
        )
        for d in parts
        if d
    ]

    def ranges(part, pieces, found, *after):
        held = [tie(grad, *after) for grad in grad_in] if after else grad_in
        return ranges_in(place, x, held, in_codes, in_low.shape[2], part, pieces, found)

    by_half = [pair[0] for pair in crossed]
    across_upper = swap(
        add([part[upper] for part in leave] + by_half).astype(BF16), "expert", 2
    )
    arrived_upper = [
        swap(tie(add([part[upper] for part in keep]).astype(BF16), *by_half), "half", d)
        for d, keep in outer
    ]
    in_grad = ranges(0, 2, None, *by_half)
    near = swap(
        tie(
            add([part[upper] for part in stay] + arrived_upper + [across_upper]).astype(BF16),
            in_grad,
        ),
        "expert",
        4,
    )
    across_lower = swap(
        tie(add([part[lower] for part in leave]).astype(BF16), across_upper), "expert", 2
    )
    arrived_lower = [
        swap(
            tie(
                add([part[lower] for part in keep] + [pair[1]]).astype(BF16), *arrived_upper
            ),
            "half",
            d,
        )
        for (d, keep), pair in zip(outer, crossed)
    ]
    in_grad = ranges(2, 4, in_grad)
    near = tie(near, in_grad)
    grad_tokens = scatter_far(
        [part[lower] for part in stay] + arrived_lower + [across_lower, near]
    )

    in_grad = ranges(3, 4, in_grad)
    return (grad_tokens.astype(BF16), in_grad[None], down_grad[None])


def solution(mesh):
    placed = (
        P("expert", None),
        P("expert", "half"),
        P("expert", None),
        P("expert", None),
        P("expert", None, None, "half"),
        P("expert", None, None, "half"),
        P("expert", None, None, "half"),
        P("expert", None, "half"),
        P("expert", None, "half"),
        P("expert", None, "half"),
    )
    return jax.shard_map(
        local,
        mesh=mesh,
        in_specs=placed,
        out_specs=(
            P("expert", "half"),
            P("expert", None, None, "half"),
            P("expert", None, None, "half"),
        ),
        check_vma=False,
    )
```

```python
import functools

import jax
import jax.numpy as jnp
from jax import lax
from jax.experimental import pallas as pl
from jax.experimental.pallas import tpu as pltpu
from jax.sharding import PartitionSpec as P

BF16 = jnp.bfloat16
F32 = jnp.float32
MIB = 1 << 20


def swap(array, axis, distance):
    size = lax.axis_size(axis)
    return lax.ppermute(array, axis, [(i, i ^ distance) for i in range(size)])


def tie(array, *others):
    return lax.optimization_barrier((array, *others))[0]


def far_distances():
    experts = lax.axis_size("expert")
    distances = []
    distance = experts // 2
    while distance > 4:
        distances.append(distance)
        distance //= 2
    return distances


def join(parts):
    return parts[0] if len(parts) == 1 else jnp.concatenate(parts, axis=0)


def gather_far(block):
    parts = [block]
    for distance in far_distances():
        parts.append(swap(join(parts), "expert", distance))
    return parts


def add(parts):
    total = parts[0].astype(F32)
    for part in parts[1:]:
        total = total + part.astype(F32)
    return total


def scatter_far(terms):
    for distance in reversed(far_distances()):
        half = terms[0].shape[0] // 2
        sent = swap(add([part[half:] for part in terms]).astype(BF16), "expert", distance)
        terms = [part[:half] for part in terms] + [sent]
    return add(terms)


def scatter_rows(near, across, cuts):
    rows = near[0].shape[0] // 2
    upper = [swap(add([part[rows:, cut] for part in across]).astype(BF16), "expert", 2) for cut in cuts]
    sent = [
        swap(add([part[rows:, cut] for part in near] + [part_of]).astype(BF16), "expert", 4)
        for cut, part_of in zip(cuts, upper)
    ]
    lower = swap(tie(add([part[:rows] for part in across]).astype(BF16), *upper), "expert", 2)
    return [
        scatter_far([part[:rows, cut] for part in near] + [lower[:, cut], part_of])
        for cut, part_of in zip(cuts, sent)
    ]


def dot(left, right):
    return jnp.dot(left, right, preferred_element_type=F32)


def dot_cols(left, right):
    return lax.dot_general(left, right, (((1,), (1,)), ((), ())), preferred_element_type=F32)


def dot_rows(left, right):
    return lax.dot_general(left, right, (((0,), (0,)), ((), ())), preferred_element_type=F32)


def cost(flops, bytes_accessed):
    return pl.CostEstimate(flops=int(flops), bytes_accessed=int(bytes_accessed), transcendentals=0)


def moved(step, blocks, place):
    return ((step // blocks) ^ place[1]) * blocks + step % blocks


def call(kernel, grid, ins, outs, place, scratch=(), mib=16, flops=0, reuse=None, weight=1e-6):
    total = sum(a.size * a.dtype.itemsize for a, _, _ in ins)
    for shape, kind, _, _ in outs:
        count = 1
        for extent in shape:
            count *= extent
        total += count * jnp.dtype(kind).itemsize

    def spec(block, index):
        if isinstance(block, tuple):
            return pl.BlockSpec(block, index)
        return pl.BlockSpec(memory_space=block)

    in_specs = [spec(block, index) for _, block, index in ins]
    arrays = [a for a, _, _ in ins]
    if reuse is not None:
        in_specs.append(pl.BlockSpec(memory_space=pl.ANY))
        arrays.append(reuse)
    return pl.pallas_call(
        kernel,
        grid_spec=pltpu.PrefetchScalarGridSpec(
            num_scalar_prefetch=1,
            grid=grid,
            in_specs=in_specs,
            out_specs=[spec(block, index) for _, _, block, index in outs],
            scratch_shapes=list(scratch),
        ),
        out_shape=[jax.ShapeDtypeStruct(shape, kind) for shape, kind, _, _ in outs],
        compiler_params=pltpu.CompilerParams(vmem_limit_bytes=mib * MIB),
        cost_estimate=cost(flops * weight, total * weight),
        input_output_aliases={} if reuse is None else {1 + len(ins): 0},
    )(place, *arrays)


def resident(kernel, ins, outs, place, mib=16, flops=0, scratch=()):
    return call(
        kernel,
        (),
        [(a, pltpu.VMEM, None) for a in ins],
        [(shape, kind, pltpu.VMEM, None) for shape, kind in outs],
        place,
        mib=mib,
        flops=flops,
        scratch=scratch,
    )


def step_of(extent):
    return next(size for size in (512, 256, 128) if extent % size == 0)


def tiles(extent, body):
    size = step_of(extent)
    for start in range(0, extent, size):
        body(start)


def whole2(*_):
    return (0, 0)


def whole3(*_):
    return (0, 0, 0)


def whole4(*_):
    return (0, 0, 0, 0)


def pack(place, parts):
    rows = sum(line[0].shape[0] for line in parts)
    cols = sum(part.shape[1] for part in parts[0])

    def kernel(place_ref, *refs):
        refs, out_ref = list(refs[:-1]), refs[-1]
        row = 0
        for line in parts:
            col = 0
            for part in line:
                height, width = part.shape
                out_ref[row : row + height, col : col + width] = refs.pop(0)[...]
                col += width
            row += line[0].shape[0]

    flat = [part for line in parts for part in line]
    return resident(kernel, flat, [((rows, cols), parts[0][0].dtype)], place)[0]


def dequant(place, codes, low, high, halves=1):
    count, height, cols = codes.shape
    groups = low.shape[1]
    size = height // groups
    held = groups // halves

    def kernel(place_ref, code_ref, low_ref, high_ref, out_ref):
        def block(i, carry):
            base = moved(i, held, place_ref) if halves > 1 else i
            source = pl.multiple_of(base * size, size)
            to = pl.multiple_of(i * size, size)
            for k in range(count):
                bottom = low_ref[k, pl.ds(base, 1), :]
                scale = (high_ref[k, pl.ds(base, 1), :] - bottom) * (1.0 / 255.0)
                vals = code_ref[k, pl.ds(source, size), :].astype(F32)
                out_ref[pl.ds(to, size), k * cols : (k + 1) * cols] = (
                    bottom + scale * vals
                ).astype(BF16)
            return carry

        lax.fori_loop(0, groups, block, 0)

    return resident(
        kernel, [codes, low, high], [((height, count * cols), BF16)], place
    )[0]


def dequant_wide(place, codes, low, high, mib):
    count, height, cols = codes.shape
    groups = low.shape[1]
    size = height // groups
    per = next(p for p in (4, 2, 1) if groups % p == 0)
    steps = groups // per
    rows = per * size

    def kernel(place_ref, code_hbm, low_hbm, high_hbm, out_ref, code_ref, low_ref, high_ref, sems):
        ends = [
            pltpu.make_async_copy(low_hbm, low_ref, sems.at[steps]),
            pltpu.make_async_copy(high_hbm, high_ref, sems.at[steps + 1]),
        ]
        blocks = []
        for i in range(steps):
            held = slice(i * rows, (i + 1) * rows)
            blocks.append(
                pltpu.make_async_copy(code_hbm.at[:, held, :], code_ref.at[:, held, :], sems.at[i])
            )
        for copy in ends + blocks:
            copy.start()
        for copy in ends:
            copy.wait()
        for i in range(steps):
            blocks[i].wait()

            def group(j, carry):
                at = i * per + j
                held = pl.ds(pl.multiple_of(at * size, size), size)
                for k in range(count):
                    bottom = low_ref[k, pl.ds(at, 1), :]
                    scale = (high_ref[k, pl.ds(at, 1), :] - bottom) * (1.0 / 255.0)
                    vals = code_ref[k, held, :].astype(F32)
                    out_ref[held, k * cols : (k + 1) * cols] = (bottom + scale * vals).astype(BF16)
                return carry

            lax.fori_loop(0, per, group, 0)

    return call(
        kernel,
        (),
        [(a, pltpu.HBM, None) for a in (codes, low, high)],
        [((height, count * cols), BF16, pltpu.VMEM, None)],
        place,
        scratch=[
            pltpu.VMEM(codes.shape, BF16),
            pltpu.VMEM(low.shape, F32),
            pltpu.VMEM(high.shape, F32),
            pltpu.SemaphoreType.DMA((steps + 2,)),
        ],
        mib=mib,
    )[0]


def hidden_rows(total_groups, size, halves):
    per = total_groups // halves
    while per > 3:
        per = next(f for f in range(2, per + 1) if per % f == 0) and per // next(
            f for f in range(2, per + 1) if per % f == 0
        )
    return per, per * size


def height_of(parts):
    return sum(part.shape[0] for part in parts)


def stacked(refs):
    return jnp.concatenate([ref[...] for ref in refs], axis=0)


def rows_of(array, start=0, stop=None):
    return (array, start, array.shape[0] if stop is None else stop)


def stacked_rows(refs, pieces):
    return jnp.concatenate(
        [ref[start:stop, :] for ref, (_, start, stop) in zip(refs, pieces)], axis=0
    )


def forward_in(place, x, w_in):
    rows = sum(stop - start for _, start, stop in x)
    width, both = w_in.shape
    hidden = both // 2
    size = step_of(hidden)

    def kernel(place_ref, *refs):
        w_ref, hidden_ref, slope_ref, act_ref = refs[len(x) :]
        left = stacked_rows(refs[: len(x)], x)

        def body(start):
            gate = dot(left, w_ref[:, pl.ds(start, size)])
            up = dot(left, w_ref[:, pl.ds(hidden + start, size)])
            sig = 1.0 / (1.0 + jnp.exp(-gate))
            act = gate * sig
            hidden_ref[:, pl.ds(start, size)] = (act * up).astype(BF16)
            slope_ref[:, pl.ds(start, size)] = up * sig * (1.0 + gate * (1.0 - sig))
            act_ref[:, pl.ds(start, size)] = act

        tiles(hidden, body)

    shape = (rows, hidden)
    return resident(
        kernel,
        [*[array for array, _, _ in x], w_in],
        [(shape, BF16), (shape, F32), (shape, F32)],
        place,
        flops=2 * rows * width * both,
    )


def route_weight(extra, place_ref, experts):
    lane = lax.broadcasted_iota(jnp.int32, extra.shape, 1)
    me = place_ref[0]
    named = (lane == me) | (lane == me + experts) | (lane == me + 2 * experts)
    return jnp.sum(jnp.where(named, extra.astype(F32), 0.0), axis=1, keepdims=True)


def forward_down(place, hidden, w_down, terms, c):
    experts = lax.axis_size("expert")
    rows = hidden[0].shape[0] // 2
    height, quarter = w_down.shape
    size = step_of(quarter)
    held = slice(c * rows, (c + 1) * rows)

    def kernel(place_ref, *refs):
        *hidden_refs, w_ref, own_ref, other_ref, out_own_ref, out_other_ref = refs
        left = jnp.concatenate([ref[...] for ref in hidden_refs], axis=1)
        own = route_weight(own_ref[held, :], place_ref, experts)
        other = route_weight(other_ref[held, :], place_ref, experts)

        def body(start):
            total = dot(left, w_ref[:, pl.ds(start, size)])
            out_own_ref[:, pl.ds(start, size)] = (own * total[:rows]).astype(BF16)
            out_other_ref[:, pl.ds(start, size)] = (other * total[rows:]).astype(BF16)

        tiles(quarter, body)

    return resident(
        kernel,
        [*hidden, w_down, *terms],
        [((rows, quarter), BF16)] * 2,
        place,
        flops=4 * rows * height * quarter,
    )


def backward_down(place, err_own, err_other, w_down, terms, c, halves):
    experts = lax.axis_size("expert")
    rows, quarter = height_of(err_own), err_own[0].shape[1]
    count = len(err_own)
    height = w_down.shape[0]
    own = height // halves
    size = step_of(own)
    held = slice(c * rows, (c + 1) * rows)

    def kernel(place_ref, *refs):
        own_ref, other_ref, w_ref, grad_ref, *outs = refs[2 * count :]
        weight = route_weight(own_ref[held, :], place_ref, experts)
        grad_ref[:rows, :] = (weight * stacked(refs[:count]).astype(F32)).astype(BF16)
        weight = route_weight(other_ref[held, :], place_ref, experts)
        grad_ref[rows:, :] = (weight * stacked(refs[count : 2 * count]).astype(F32)).astype(BF16)
        for d in reversed(range(halves)):

            def body(start):
                at = d * own + start
                part = dot_cols(grad_ref[...], w_ref[pl.ds(at, size), :])
                outs[d][:, pl.ds(start, size)] = part.astype(outs[d].dtype)

            tiles(own, body)

    shape = (2 * rows, own)
    return resident(
        kernel,
        [*err_own, *err_other, *terms, w_down],
        [((2 * rows, quarter), BF16), (shape, F32)] + [(shape, BF16)] * (halves - 1),
        place,
        flops=4 * rows * height * quarter,
    )


def backward_hidden(place, grad_own, arrived, slope, act, w_in, halves):
    both_rows, hidden = slope.shape
    rows = both_rows // 2
    quarter = w_in.shape[0] // halves
    size = step_of(quarter)
    count = len(arrived)

    def kernel(place_ref, grad_own_ref, *refs):
        arrived_refs = refs[:count]
        slope_ref, act_ref, w_ref, grad_ref, *outs = refs[count:]
        grad_hidden = grad_own_ref[...]
        for ref in arrived_refs:
            grad_hidden += ref[...].astype(F32)
        grad_ref[:, :hidden] = (grad_hidden * slope_ref[...]).astype(BF16)
        grad_ref[:, hidden:] = (grad_hidden * act_ref[...]).astype(BF16)
        for d in range(halves):

            def body(start):
                at = pl.multiple_of((place_ref[1] ^ d) * quarter + start, size)
                part = dot_cols(grad_ref[...], w_ref[pl.ds(at, size), :]).astype(BF16)
                outs[2 * d][:, pl.ds(start, size)] = part[:rows]
                outs[2 * d + 1][:, pl.ds(start, size)] = part[rows:]

            tiles(quarter, body)

    grad, *parts = resident(
        kernel,
        [grad_own, *arrived, slope, act, w_in],
        [((both_rows, 2 * hidden), BF16)] + [((rows, quarter), BF16)] * (2 * halves),
        place,
        flops=4 * both_rows * hidden * quarter * halves,
    )
    return grad, parts


def ends(grad, codes):
    upper = jnp.sum(grad * codes.astype(F32), axis=0, keepdims=True) * (1.0 / 255.0)
    return jnp.sum(grad, axis=0, keepdims=True) - upper, upper


def range_tile(left, right, size, step, codes, store):
    turned = left.T
    for start in range(0, right.shape[1], step):
        cols = slice(start, start + step)
        grad = dot(turned, right[:, cols])
        for g in range(turned.shape[0] // size):
            cut = slice(g * size, (g + 1) * size)
            low, high = ends(grad[cut], codes(cut, cols))
            store(g, cols, low, high)


def ranges_down(place, hidden, grad, codes, groups, halves, found=None):
    _, height, quarter = codes.shape
    size = height // groups
    per, rows = hidden_rows(groups, size, halves)
    blocks = height // halves // rows
    earlier = [] if found is None else [found]

    def kernel(place_ref, *refs):
        hidden_refs = refs[:halves]
        grad_ref, code_ref, *found_refs, out_ref = refs[halves:]
        step = pl.program_id(0)
        base = moved(step, blocks, place_ref) * per

        def store(g, cols, low, high):
            for k, value in ((0, low), (1, high)):
                for ref in found_refs:
                    value += ref[k, pl.ds(base + g, 1), cols]
                out_ref[k, pl.ds(base + g, 1), cols] = value

        for d in range(halves):

            @pl.when(step // blocks == d)
            def _():
                range_tile(
                    hidden_refs[d][...],
                    grad_ref,
                    size,
                    256,
                    lambda cut, cols: code_ref[0, cut, cols],
                    store,
                )

    shape = (2, groups, quarter)
    return call(
        kernel,
        (height // rows,),
        [(part, (part.shape[0], rows), lambda i, p: (0, i % blocks)) for part in hidden]
        + [
            (grad, pltpu.VMEM, None),
            (codes, (1, rows, quarter), lambda i, p: (0, moved(i, blocks, p), 0)),
        ]
        + [(array, pltpu.VMEM, None) for array in earlier],
        [(shape, F32, shape, whole3)],
        place,
        mib=20,
        flops=2 * grad.shape[0] * height * quarter,
    )[0]


def ranges_in(place, x, grads, codes, groups, part, parts, found):
    _, _, width, hidden = codes.shape
    size = width // groups
    held = groups // parts
    per = next(p for p in (4, 2, 1) if held % p == 0)
    rows = per * size
    blocks = held // per
    flat = [piece for parts in x for piece in parts]
    chunks = len(grads)
    tokens, both = grads[0].shape
    wide = 256 if hidden % 256 == 0 else hidden

    def kernel(place_ref, *refs):
        x_refs = refs[: len(flat)]
        grad_refs = refs[len(flat) : len(flat) + chunks]
        code_ref, out_ref, right_ref = refs[len(flat) + chunks], refs[-2], refs[-1]
        base = pl.program_id(0) * per

        @pl.when(pl.program_id(0) == 0)
        def _():
            for c in range(chunks):
                right_ref[c * tokens : (c + 1) * tokens, :] = grad_refs[c][...]

        def split(cols):
            k = cols.start // hidden
            return k, slice(cols.start - k * hidden, cols.stop - k * hidden)

        def codes_at(cut, cols):
            k, cols = split(cols)
            return code_ref[0, k, cut, cols]

        def store(g, cols, low, high):
            k, cols = split(cols)
            out_ref[2 * k, pl.ds(base + g, 1), cols] = low
            out_ref[2 * k + 1, pl.ds(base + g, 1), cols] = high

        left = stacked_rows(x_refs, flat)
        range_tile(left, right_ref, size, wide, codes_at, store)

    shape = (4, groups, hidden)
    return call(
        kernel,
        (blocks,),
        [(a, (a.shape[0], rows), lambda i, p: (0, part * blocks + i)) for a, _, _ in flat]
        + [(grad, pltpu.VMEM, None) for grad in grads]
        + [(codes, (1, 2, rows, hidden), lambda i, p: (0, 0, part * blocks + i, 0))],
        [(shape, F32, (4, held, hidden), lambda i, p: (0, part, 0))],
        place,
        scratch=[pltpu.VMEM((chunks * tokens, both), BF16)],
        mib=20,
        flops=2 * sum(grad.size for grad in grads) * (width // parts),
        reuse=found,
    )[0]


def prepare(place, routes, route_scores, extra):
    experts = lax.axis_size("expert")
    rows, top_count = routes.shape

    def kernel(place_ref, route_ref, score_ref, out_ref):
        scores = score_ref[...]
        weights = scores / jnp.sum(scores, axis=1, keepdims=True)
        names = route_ref[...]
        lane = lax.broadcasted_iota(jnp.int32, (rows, extra), 1)
        third = jnp.where(lane < experts, 0, jnp.where(lane < 2 * experts, 1, 2))
        expert = lane - third * experts
        table = jnp.zeros((rows, extra), F32)
        for k in range(top_count):
            table += jnp.where(expert == names[:, k : k + 1], weights[:, k : k + 1], 0.0)
        top = table.astype(BF16).astype(F32)
        middle = (table - top).astype(BF16).astype(F32)
        bottom = table - top - middle
        terms = jnp.where(third == 0, top, jnp.where(third == 1, middle, bottom))
        out_ref[...] = terms.astype(BF16)

    return resident(kernel, [routes, route_scores], [((rows, extra), BF16)], place)[0]


def local(
    tokens, target, routes, route_scores, in_codes, in_low, in_high, down_codes, down_low, down_high
):
    experts = lax.axis_size("expert")
    halves = lax.axis_size("half")
    place = jnp.stack([lax.axis_index("expert"), lax.axis_index("half")]).astype(jnp.int32)
    quarter = target.shape[1]
    parts = range(halves)
    chunks = (0, 1)

    far = join(gather_far(tokens)[1:])
    near_own = swap(tokens, "expert", 4)
    across_own = swap(tokens, "expert", 2)
    extra = -(-3 * experts // 128) * 128
    terms = prepare(place, routes, route_scores, extra)
    w_in = dequant_wide(place, in_codes[0], tie(in_low, terms)[0], in_high[0], 30)
    near_own = tie(near_own, w_in)
    across_near = swap(near_own, "expert", 2)
    far = tie(far, w_in, across_own)
    near_far = swap(far, "expert", 4)
    terms = join(gather_far(terms))
    near_far = tie(near_far, across_near, terms)
    last = pack(place, [[far], [near_far]])
    across_last = swap(last, "expert", 2)
    first = pack(place, [[tokens], [tie(far, terms)], [near_own]])
    near_other = swap(near_far, "expert", 1)
    x = [[rows_of(part) for part in (first, near_far, swap(first, "expert", 1), near_other)]]

    hidden, slope, act = [], [], []
    for c in chunks:
        if c == 1:
            second = pack(place, [[across_own], [tie(across_near, near_other)]])
            second_other = swap(second, "expert", 1)
            across_last = tie(across_last, w_down, second_other)
            last_other = swap(across_last, "expert", 1)
            size = tokens.shape[0]
            x.append([])
            for early, late in ((second, across_last), (second_other, last_other)):
                count = late.shape[0] // 2
                x[1] += [
                    rows_of(early, 0, size),
                    rows_of(late, 0, count),
                    rows_of(early, size),
                    rows_of(late, count),
                ]
        own, chunk_slope, chunk_act = forward_in(place, x[c], w_in)
        if c == 0:
            w_down = dequant(place, down_codes, tie(down_low, own), down_high, halves)
        hidden.append([own] + [swap(own, "half", d) for d in parts if d])
        slope.append(chunk_slope)
        act.append(chunk_act)
    terms = tie(terms, hidden[1][0])
    for distance in (4, 2):
        terms = jnp.concatenate([terms, swap(terms, "expert", distance)], axis=0)
    terms = (terms, swap(terms, "expert", 1))

    sums = []
    for c in chunks:
        if c == 1:
            hidden[1][1:] = [tie(part, sums[0][0]) for part in hidden[1][1:]]
        out_own, out_other = forward_down(place, hidden[c], w_down, terms, c)
        sums.append([out_own, swap(out_other, "expert", 1)])
    middle = quarter // 2
    cuts = [slice(0, middle), slice(middle, quarter)]
    mixed = scatter_rows(sums[0], sums[1], cuts)
    error = [
        (mixed[f] - target[:, cuts[f]].astype(F32)).astype(BF16) for f in range(len(cuts))
    ]

    kept = pack(place, [list(line) for line in zip(*[gather_far(part) for part in error])])
    near = swap(kept, "expert", 4)
    across_kept = swap(kept, "expert", 2)
    kept_other = swap(kept, "expert", 1)
    near = tie(near, across_kept, kept_other)
    across_near = swap(near, "expert", 2)
    across_other = swap(across_kept, "expert", 1)
    errors = [([kept, near], [kept_other, swap(near, "expert", 1)])]
    grads, grad_own, arrived = [], [], []
    down_groups = down_low.shape[1]
    for c in chunks:
        if c == 1:
            across_near = tie(across_near, grads[0], across_other)
            down_grad = ranges_down(place, hidden[0], grads[0], down_codes, down_groups, halves)
            last_other = tie(swap(across_near, "expert", 1), down_grad, *arrived[0])
            errors.append(([across_kept, across_near], [across_other, last_other]))
        grad, own, *others = backward_down(place, *errors[c], w_down, terms, c, halves)
        grads.append(grad)
        grad_own.append(own)
        arrived.append([swap(other, "half", d + 1) for d, other in enumerate(others)])

    grad_in, kinds = [], []
    down_grad = ranges_down(
        place, hidden[1], grads[1], down_codes, down_groups, halves, down_grad
    )
    for c in chunks:
        if c == 1:
            arrived[1] = [tie(part, grad_in[0], down_grad) for part in arrived[1]]
        grad, found = backward_hidden(
            place, grad_own[c], arrived[c], slope[c], act[c], w_in, halves
        )
        grad_in.append(grad)
        kinds.append(found)
    kinds[0] = [tie(part, grad_in[1]) for part in kinds[0]]
    rows = height_of(errors[0][0])
    lower, upper = slice(0, rows // 2), slice(rows // 2, rows)
    keep, go = [
        [[found[2 * d], swap(found[2 * d + 1], "expert", 1)] for d in parts] for found in kinds
    ]
    stay, leave = keep[0], go[0]
    outer = [(d, keep[d]) for d in parts if d]
    crossed = [
        (
            swap(add([part[upper] for part in go[d]]).astype(BF16), "half", d),
            swap(add([part[lower] for part in go[d]]).astype(BF16), "expert", 2),
        )
        for d in parts
        if d
    ]

    def ranges(part, pieces, found, *after):
        held = [tie(grad, *after) for grad in grad_in] if after else grad_in
        return ranges_in(place, x, held, in_codes, in_low.shape[2], part, pieces, found)

    by_half = [pair[0] for pair in crossed]
    across_upper = swap(
        add([part[upper] for part in leave] + by_half).astype(BF16), "expert", 2
    )
    arrived_upper = [
        swap(tie(add([part[upper] for part in keep]).astype(BF16), *by_half), "half", d)
        for d, keep in outer
    ]
    in_grad = ranges(0, 2, None, *by_half)
    near = swap(
        tie(
            add([part[upper] for part in stay] + arrived_upper + [across_upper]).astype(BF16),
            in_grad,
        ),
        "expert",
        4,
    )
    across_lower = swap(
        tie(add([part[lower] for part in leave]).astype(BF16), across_upper), "expert", 2
    )
    arrived_lower = [
        swap(
            tie(
                add([part[lower] for part in keep] + [pair[1]]).astype(BF16), *arrived_upper
            ),
            "half",
            d,
        )
        for (d, keep), pair in zip(outer, crossed)
    ]
    in_grad = ranges(2, 4, in_grad)
    near = tie(near, in_grad)
    grad_tokens = scatter_far(
        [part[lower] for part in stay] + arrived_lower + [across_lower, near]
    )

    in_grad = ranges(3, 4, in_grad)
    return (grad_tokens.astype(BF16), in_grad[None], down_grad[None])


def solution(mesh):
    placed = (
        P("expert", None),
        P("expert", "half"),
        P("expert", None),
        P("expert", None),
        P("expert", None, None, "half"),
        P("expert", None, None, "half"),
        P("expert", None, None, "half"),
        P("expert", None, "half"),
        P("expert", None, "half"),
        P("expert", None, "half"),
    )
    return jax.shard_map(
        local,
        mesh=mesh,
        in_specs=placed,
        out_specs=(
            P("expert", "half"),
            P("expert", None, None, "half"),
            P("expert", None, None, "half"),
        ),
        check_vma=False,
    )
```

```python
import functools

import jax
import jax.numpy as jnp
from jax import lax
from jax.experimental import pallas as pl
from jax.experimental.pallas import tpu as pltpu
from jax.sharding import PartitionSpec as P

BF16 = jnp.bfloat16
F32 = jnp.float32
MIB = 1 << 20


def swap(array, axis, distance):
    size = lax.axis_size(axis)
    return lax.ppermute(array, axis, [(i, i ^ distance) for i in range(size)])


def tie(array, *others):
    return lax.optimization_barrier((array, *others))[0]


def far_distances():
    experts = lax.axis_size("expert")
    distances = []
    distance = experts // 2
    while distance > 4:
        distances.append(distance)
        distance //= 2
    return distances


def join(parts):
    return parts[0] if len(parts) == 1 else jnp.concatenate(parts, axis=0)


def gather_far(block):
    parts = [block]
    for distance in far_distances():
        parts.append(swap(join(parts), "expert", distance))
    return parts


def add(parts):
    total = parts[0].astype(F32)
    for part in parts[1:]:
        total = total + part.astype(F32)
    return total


def scatter_far(terms):
    for distance in reversed(far_distances()):
        half = terms[0].shape[0] // 2
        sent = swap(add([part[half:] for part in terms]).astype(BF16), "expert", distance)
        terms = [part[:half] for part in terms] + [sent]
    return add(terms)


def scatter_rows(near, across, cuts):
    rows = near[0].shape[0] // 2
    upper = [swap(add([part[rows:, cut] for part in across]).astype(BF16), "expert", 2) for cut in cuts]
    sent = [
        swap(add([part[rows:, cut] for part in near] + [part_of]).astype(BF16), "expert", 4)
        for cut, part_of in zip(cuts, upper)
    ]
    lower = swap(tie(add([part[:rows] for part in across]).astype(BF16), *upper), "expert", 2)
    return [
        scatter_far([part[:rows, cut] for part in near] + [lower[:, cut], part_of])
        for cut, part_of in zip(cuts, sent)
    ]


def dot(left, right):
    return jnp.dot(left, right, preferred_element_type=F32)


def dot_cols(left, right):
    return lax.dot_general(left, right, (((1,), (1,)), ((), ())), preferred_element_type=F32)


def dot_rows(left, right):
    return lax.dot_general(left, right, (((0,), (0,)), ((), ())), preferred_element_type=F32)


def cost(flops, bytes_accessed):
    return pl.CostEstimate(flops=int(flops), bytes_accessed=int(bytes_accessed), transcendentals=0)


def moved(step, blocks, place):
    return ((step // blocks) ^ place[1]) * blocks + step % blocks


def call(kernel, grid, ins, outs, place, scratch=(), mib=16, flops=0, reuse=None, weight=1e-6):
    total = sum(a.size * a.dtype.itemsize for a, _, _ in ins)
    for shape, kind, _, _ in outs:
        count = 1
        for extent in shape:
            count *= extent
        total += count * jnp.dtype(kind).itemsize

    def spec(block, index):
        if isinstance(block, tuple):
            return pl.BlockSpec(block, index)
        return pl.BlockSpec(memory_space=block)

    in_specs = [spec(block, index) for _, block, index in ins]
    arrays = [a for a, _, _ in ins]
    if reuse is not None:
        in_specs.append(pl.BlockSpec(memory_space=pl.ANY))
        arrays.append(reuse)
    return pl.pallas_call(
        kernel,
        grid_spec=pltpu.PrefetchScalarGridSpec(
            num_scalar_prefetch=1,
            grid=grid,
            in_specs=in_specs,
            out_specs=[spec(block, index) for _, _, block, index in outs],
            scratch_shapes=list(scratch),
        ),
        out_shape=[jax.ShapeDtypeStruct(shape, kind) for shape, kind, _, _ in outs],
        compiler_params=pltpu.CompilerParams(vmem_limit_bytes=mib * MIB),
        cost_estimate=cost(flops * weight, total * weight),
        input_output_aliases={} if reuse is None else {1 + len(ins): 0},
    )(place, *arrays)


def resident(kernel, ins, outs, place, mib=16, flops=0, scratch=()):
    return call(
        kernel,
        (),
        [(a, pltpu.VMEM, None) for a in ins],
        [(shape, kind, pltpu.VMEM, None) for shape, kind in outs],
        place,
        mib=mib,
        flops=flops,
        scratch=scratch,
    )


def step_of(extent):
    return next(size for size in (512, 256, 128) if extent % size == 0)


def tiles(extent, body):
    size = step_of(extent)
    for start in range(0, extent, size):
        body(start)


def whole2(*_):
    return (0, 0)


def whole3(*_):
    return (0, 0, 0)


def whole4(*_):
    return (0, 0, 0, 0)


def pack(place, parts):
    rows = sum(line[0].shape[0] for line in parts)
    cols = sum(part.shape[1] for part in parts[0])

    def kernel(place_ref, *refs):
        refs, out_ref = list(refs[:-1]), refs[-1]
        row = 0
        for line in parts:
            col = 0
            for part in line:
                height, width = part.shape
                out_ref[row : row + height, col : col + width] = refs.pop(0)[...]
                col += width
            row += line[0].shape[0]

    flat = [part for line in parts for part in line]
    return resident(kernel, flat, [((rows, cols), parts[0][0].dtype)], place)[0]


def dequant(place, codes, low, high, halves=1):
    count, height, cols = codes.shape
    groups = low.shape[1]
    size = height // groups
    held = groups // halves

    def kernel(place_ref, code_ref, low_ref, high_ref, out_ref):
        def block(i, carry):
            base = moved(i, held, place_ref) if halves > 1 else i
            source = pl.multiple_of(base * size, size)
            to = pl.multiple_of(i * size, size)
            for k in range(count):
                bottom = low_ref[k, pl.ds(base, 1), :]
                scale = (high_ref[k, pl.ds(base, 1), :] - bottom) * (1.0 / 255.0)
                vals = code_ref[k, pl.ds(source, size), :].astype(F32)
                out_ref[pl.ds(to, size), k * cols : (k + 1) * cols] = (
                    bottom + scale * vals
                ).astype(BF16)
            return carry

        lax.fori_loop(0, groups, block, 0)

    return resident(
        kernel, [codes, low, high], [((height, count * cols), BF16)], place
    )[0]


def dequant_wide(place, codes, low, high, mib):
    count, height, cols = codes.shape
    groups = low.shape[1]
    size = height // groups
    per = next(p for p in (4, 2, 1) if groups % p == 0)
    steps = groups // per
    rows = per * size

    def kernel(place_ref, code_hbm, low_hbm, high_hbm, out_ref, code_ref, low_ref, high_ref, sems):
        ends = [
            pltpu.make_async_copy(low_hbm, low_ref, sems.at[steps]),
            pltpu.make_async_copy(high_hbm, high_ref, sems.at[steps + 1]),
        ]
        blocks = []
        for i in range(steps):
            held = slice(i * rows, (i + 1) * rows)
            blocks.append(
                pltpu.make_async_copy(code_hbm.at[:, held, :], code_ref.at[:, held, :], sems.at[i])
            )
        for copy in ends + blocks:
            copy.start()
        for copy in ends:
            copy.wait()
        for i in range(steps):
            blocks[i].wait()

            def group(j, carry):
                at = i * per + j
                held = pl.ds(pl.multiple_of(at * size, size), size)
                for k in range(count):
                    bottom = low_ref[k, pl.ds(at, 1), :]
                    scale = (high_ref[k, pl.ds(at, 1), :] - bottom) * (1.0 / 255.0)
                    vals = code_ref[k, held, :].astype(F32)
                    out_ref[held, k * cols : (k + 1) * cols] = (bottom + scale * vals).astype(BF16)
                return carry

            lax.fori_loop(0, per, group, 0)

    return call(
        kernel,
        (),
        [(a, pltpu.HBM, None) for a in (codes, low, high)],
        [((height, count * cols), BF16, pltpu.VMEM, None)],
        place,
        scratch=[
            pltpu.VMEM(codes.shape, BF16),
            pltpu.VMEM(low.shape, F32),
            pltpu.VMEM(high.shape, F32),
            pltpu.SemaphoreType.DMA((steps + 2,)),
        ],
        mib=mib,
    )[0]


def hidden_rows(total_groups, size, halves):
    per = total_groups // halves
    while per > 3:
        per = next(f for f in range(2, per + 1) if per % f == 0) and per // next(
            f for f in range(2, per + 1) if per % f == 0
        )
    return per, per * size


def height_of(parts):
    return sum(part.shape[0] for part in parts)


def stacked(refs):
    return jnp.concatenate([ref[...] for ref in refs], axis=0)


def rows_of(array, start=0, stop=None):
    return (array, start, array.shape[0] if stop is None else stop)


def stacked_rows(refs, pieces):
    return jnp.concatenate(
        [ref[start:stop, :] for ref, (_, start, stop) in zip(refs, pieces)], axis=0
    )


def forward_in(place, x, w_in):
    rows = sum(stop - start for _, start, stop in x)
    width, both = w_in.shape
    hidden = both // 2
    size = step_of(hidden)

    def kernel(place_ref, *refs):
        w_ref, hidden_ref, slope_ref, act_ref = refs[len(x) :]
        left = stacked_rows(refs[: len(x)], x)

        def body(start):
            gate = dot(left, w_ref[:, pl.ds(start, size)])
            up = dot(left, w_ref[:, pl.ds(hidden + start, size)])
            sig = 1.0 / (1.0 + jnp.exp(-gate))
            act = gate * sig
            hidden_ref[:, pl.ds(start, size)] = (act * up).astype(BF16)
            slope_ref[:, pl.ds(start, size)] = up * sig * (1.0 + gate * (1.0 - sig))
            act_ref[:, pl.ds(start, size)] = act

        tiles(hidden, body)

    shape = (rows, hidden)
    return resident(
        kernel,
        [*[array for array, _, _ in x], w_in],
        [(shape, BF16), (shape, F32), (shape, F32)],
        place,
        flops=2 * rows * width * both,
    )


def route_weight(extra, place_ref, experts):
    lane = lax.broadcasted_iota(jnp.int32, extra.shape, 1)
    me = place_ref[0]
    named = (lane == me) | (lane == me + experts) | (lane == me + 2 * experts)
    return jnp.sum(jnp.where(named, extra.astype(F32), 0.0), axis=1, keepdims=True)


def forward_down(place, hidden, w_down, terms, c):
    experts = lax.axis_size("expert")
    rows = hidden[0].shape[0] // 2
    height, quarter = w_down.shape
    size = step_of(quarter)
    held = slice(c * rows, (c + 1) * rows)

    def kernel(place_ref, *refs):
        *hidden_refs, w_ref, own_ref, other_ref, out_own_ref, out_other_ref = refs
        left = jnp.concatenate([ref[...] for ref in hidden_refs], axis=1)
        own = route_weight(own_ref[held, :], place_ref, experts)
        other = route_weight(other_ref[held, :], place_ref, experts)

        def body(start):
            total = dot(left, w_ref[:, pl.ds(start, size)])
            out_own_ref[:, pl.ds(start, size)] = (own * total[:rows]).astype(BF16)
            out_other_ref[:, pl.ds(start, size)] = (other * total[rows:]).astype(BF16)

        tiles(quarter, body)

    return resident(
        kernel,
        [*hidden, w_down, *terms],
        [((rows, quarter), BF16)] * 2,
        place,
        flops=4 * rows * height * quarter,
    )


def backward_down(place, err_own, err_other, w_down, terms, c, halves):
    experts = lax.axis_size("expert")
    rows, quarter = height_of(err_own), err_own[0].shape[1]
    count = len(err_own)
    height = w_down.shape[0]
    own = height // halves
    size = step_of(own)
    held = slice(c * rows, (c + 1) * rows)

    def kernel(place_ref, *refs):
        own_ref, other_ref, w_ref, grad_ref, *outs = refs[2 * count :]
        weight = route_weight(own_ref[held, :], place_ref, experts)
        grad_ref[:rows, :] = (weight * stacked(refs[:count]).astype(F32)).astype(BF16)
        weight = route_weight(other_ref[held, :], place_ref, experts)
        grad_ref[rows:, :] = (weight * stacked(refs[count : 2 * count]).astype(F32)).astype(BF16)
        for d in reversed(range(halves)):

            def body(start):
                at = d * own + start
                part = dot_cols(grad_ref[...], w_ref[pl.ds(at, size), :])
                outs[d][:, pl.ds(start, size)] = part.astype(outs[d].dtype)

            tiles(own, body)

    shape = (2 * rows, own)
    return resident(
        kernel,
        [*err_own, *err_other, *terms, w_down],
        [((2 * rows, quarter), BF16), (shape, F32)] + [(shape, BF16)] * (halves - 1),
        place,
        flops=4 * rows * height * quarter,
    )


def backward_hidden(place, grad_own, arrived, slope, act, w_in, halves):
    both_rows, hidden = slope.shape
    rows = both_rows // 2
    quarter = w_in.shape[0] // halves
    size = step_of(quarter)
    count = len(arrived)

    def kernel(place_ref, grad_own_ref, *refs):
        arrived_refs = refs[:count]
        slope_ref, act_ref, w_ref, grad_ref, *outs = refs[count:]
        grad_hidden = grad_own_ref[...]
        for ref in arrived_refs:
            grad_hidden += ref[...].astype(F32)
        grad_ref[:, :hidden] = (grad_hidden * slope_ref[...]).astype(BF16)
        grad_ref[:, hidden:] = (grad_hidden * act_ref[...]).astype(BF16)
        for d in range(halves):

            def body(start):
                at = pl.multiple_of((place_ref[1] ^ d) * quarter + start, size)
                part = dot_cols(grad_ref[...], w_ref[pl.ds(at, size), :]).astype(BF16)
                outs[2 * d][:, pl.ds(start, size)] = part[:rows]
                outs[2 * d + 1][:, pl.ds(start, size)] = part[rows:]

            tiles(quarter, body)

    grad, *parts = resident(
        kernel,
        [grad_own, *arrived, slope, act, w_in],
        [((both_rows, 2 * hidden), BF16)] + [((rows, quarter), BF16)] * (2 * halves),
        place,
        flops=4 * both_rows * hidden * quarter * halves,
    )
    return grad, parts


def ends(grad, codes):
    upper = jnp.sum(grad * codes.astype(F32), axis=0, keepdims=True) * (1.0 / 255.0)
    return jnp.sum(grad, axis=0, keepdims=True) - upper, upper


def range_tile(left, right, size, step, codes, store):
    turned = left.T
    for start in range(0, right.shape[1], step):
        cols = slice(start, start + step)
        grad = dot(turned, right[:, cols])
        for g in range(turned.shape[0] // size):
            cut = slice(g * size, (g + 1) * size)
            low, high = ends(grad[cut], codes(cut, cols))
            store(g, cols, low, high)


def ranges_down(place, hidden, grad, codes, groups, halves, found=None):
    _, height, quarter = codes.shape
    size = height // groups
    per, rows = hidden_rows(groups, size, halves)
    blocks = height // halves // rows
    earlier = [] if found is None else [found]

    def kernel(place_ref, *refs):
        hidden_refs = refs[:halves]
        grad_ref, code_ref, *found_refs, out_ref = refs[halves:]
        step = pl.program_id(0)
        base = moved(step, blocks, place_ref) * per

        def store(g, cols, low, high):
            for k, value in ((0, low), (1, high)):
                for ref in found_refs:
                    value += ref[k, pl.ds(base + g, 1), cols]
                out_ref[k, pl.ds(base + g, 1), cols] = value

        for d in range(halves):

            @pl.when(step // blocks == d)
            def _():
                range_tile(
                    hidden_refs[d][...],
                    grad_ref,
                    size,
                    256,
                    lambda cut, cols: code_ref[0, cut, cols],
                    store,
                )

    shape = (2, groups, quarter)
    return call(
        kernel,
        (height // rows,),
        [(part, (part.shape[0], rows), lambda i, p: (0, i % blocks)) for part in hidden]
        + [
            (grad, pltpu.VMEM, None),
            (codes, (1, rows, quarter), lambda i, p: (0, moved(i, blocks, p), 0)),
        ]
        + [(array, pltpu.VMEM, None) for array in earlier],
        [(shape, F32, shape, whole3)],
        place,
        mib=20,
        flops=2 * grad.shape[0] * height * quarter,
    )[0]


def ranges_in(place, x, grads, codes, groups, part, parts, found):
    _, _, width, hidden = codes.shape
    size = width // groups
    held = groups // parts
    per = next(p for p in (4, 2, 1) if held % p == 0)
    rows = per * size
    blocks = held // per
    flat = [piece for parts in x for piece in parts]
    chunks = len(grads)
    tokens, both = grads[0].shape
    wide = 256 if hidden % 256 == 0 else hidden

    def kernel(place_ref, *refs):
        x_refs = refs[: len(flat)]
        grad_refs = refs[len(flat) : len(flat) + chunks]
        code_ref, out_ref, right_ref = refs[len(flat) + chunks], refs[-2], refs[-1]
        base = pl.program_id(0) * per

        @pl.when(pl.program_id(0) == 0)
        def _():
            for c in range(chunks):
                right_ref[c * tokens : (c + 1) * tokens, :] = grad_refs[c][...]

        def split(cols):
            k = cols.start // hidden
            return k, slice(cols.start - k * hidden, cols.stop - k * hidden)

        def codes_at(cut, cols):
            k, cols = split(cols)
            return code_ref[0, k, cut, cols]

        def store(g, cols, low, high):
            k, cols = split(cols)
            out_ref[2 * k, pl.ds(base + g, 1), cols] = low
            out_ref[2 * k + 1, pl.ds(base + g, 1), cols] = high

        left = stacked_rows(x_refs, flat)
        range_tile(left, right_ref, size, wide, codes_at, store)

    shape = (4, groups, hidden)
    return call(
        kernel,
        (blocks,),
        [(a, (a.shape[0], rows), lambda i, p: (0, part * blocks + i)) for a, _, _ in flat]
        + [(grad, pltpu.VMEM, None) for grad in grads]
        + [(codes, (1, 2, rows, hidden), lambda i, p: (0, 0, part * blocks + i, 0))],
        [(shape, F32, (4, held, hidden), lambda i, p: (0, part, 0))],
        place,
        scratch=[pltpu.VMEM((chunks * tokens, both), BF16)],
        mib=20,
        flops=2 * sum(grad.size for grad in grads) * (width // parts),
        reuse=found,
    )[0]


def prepare(place, routes, route_scores, extra):
    experts = lax.axis_size("expert")
    rows, top_count = routes.shape

    def kernel(place_ref, route_ref, score_ref, out_ref):
        scores = score_ref[...]
        weights = scores / jnp.sum(scores, axis=1, keepdims=True)
        names = route_ref[...]
        lane = lax.broadcasted_iota(jnp.int32, (rows, extra), 1)
        third = jnp.where(lane < experts, 0, jnp.where(lane < 2 * experts, 1, 2))
        expert = lane - third * experts
        table = jnp.zeros((rows, extra), F32)
        for k in range(top_count):
            table += jnp.where(expert == names[:, k : k + 1], weights[:, k : k + 1], 0.0)
        top = table.astype(BF16).astype(F32)
        middle = (table - top).astype(BF16).astype(F32)
        bottom = table - top - middle
        terms = jnp.where(third == 0, top, jnp.where(third == 1, middle, bottom))
        out_ref[...] = terms.astype(BF16)

    return resident(kernel, [routes, route_scores], [((rows, extra), BF16)], place)[0]


def local(
    tokens, target, routes, route_scores, in_codes, in_low, in_high, down_codes, down_low, down_high
):
    experts = lax.axis_size("expert")
    halves = lax.axis_size("half")
    place = jnp.stack([lax.axis_index("expert"), lax.axis_index("half")]).astype(jnp.int32)
    quarter = target.shape[1]
    parts = range(halves)
    chunks = (0, 1)

    far = join(gather_far(tokens)[1:])
    near_own = swap(tokens, "expert", 4)
    across_own = swap(tokens, "expert", 2)
    extra = -(-3 * experts // 128) * 128
    terms = prepare(place, routes, route_scores, extra)
    w_in = dequant_wide(place, in_codes[0], tie(in_low, terms)[0], in_high[0], 30)
    near_own = tie(near_own, w_in)
    across_near = swap(near_own, "expert", 2)
    far = tie(far, w_in, across_own)
    near_far = swap(far, "expert", 4)
    terms = join(gather_far(terms))
    near_far = tie(near_far, across_near, terms)
    last = pack(place, [[far], [near_far]])
    across_last = swap(last, "expert", 2)
    first = pack(place, [[tokens], [tie(far, terms)], [near_own]])
    near_other = swap(near_far, "expert", 1)
    x = [[rows_of(part) for part in (first, near_far, swap(first, "expert", 1), near_other)]]

    hidden, slope, act = [], [], []
    for c in chunks:
        if c == 1:
            second = pack(place, [[across_own], [tie(across_near, near_other)]])
            second_other = swap(second, "expert", 1)
            across_last = tie(across_last, w_down, second_other, near_terms, *hidden[0][1:])
            last_other = swap(across_last, "expert", 1)
            size = tokens.shape[0]
            x.append([])
            for early, late in ((second, across_last), (second_other, last_other)):
                count = late.shape[0] // 2
                x[1] += [
                    rows_of(early, 0, size),
                    rows_of(late, 0, count),
                    rows_of(early, size),
                    rows_of(late, count),
                ]
        own, chunk_slope, chunk_act = forward_in(place, x[c], w_in)
        if c == 0:
            w_down = dequant(place, down_codes, tie(down_low, own), down_high, halves)
            near_terms = swap(tie(terms, w_down), "expert", 4)
        hidden.append([own] + [swap(own, "half", d) for d in parts if d])
        slope.append(chunk_slope)
        act.append(chunk_act)
    terms = jnp.concatenate([terms, tie(near_terms, hidden[1][0])], axis=0)
    terms = jnp.concatenate([terms, swap(terms, "expert", 2)], axis=0)
    terms = (terms, swap(terms, "expert", 1))

    sums = []
    for c in chunks:
        if c == 1:
            hidden[1][1:] = [tie(part, sums[0][0]) for part in hidden[1][1:]]
        out_own, out_other = forward_down(place, hidden[c], w_down, terms, c)
        sums.append([out_own, swap(out_other, "expert", 1)])
    middle = quarter // 2
    cuts = [slice(0, middle), slice(middle, quarter)]
    mixed = scatter_rows(sums[0], sums[1], cuts)
    error = [
        (mixed[f] - target[:, cuts[f]].astype(F32)).astype(BF16) for f in range(len(cuts))
    ]

    kept = pack(place, [list(line) for line in zip(*[gather_far(part) for part in error])])
    near = swap(kept, "expert", 4)
    across_kept = swap(kept, "expert", 2)
    kept_other = swap(kept, "expert", 1)
    near = tie(near, across_kept, kept_other)
    across_near = swap(near, "expert", 2)
    across_other = swap(across_kept, "expert", 1)
    errors = [([kept, near], [kept_other, swap(near, "expert", 1)])]
    grads, grad_own, arrived = [], [], []
    down_groups = down_low.shape[1]
    for c in chunks:
        if c == 1:
            across_near = tie(across_near, grads[0], across_other)
            down_grad = ranges_down(place, hidden[0], grads[0], down_codes, down_groups, halves)
            last_other = tie(swap(across_near, "expert", 1), down_grad, *arrived[0])
            errors.append(([across_kept, across_near], [across_other, last_other]))
        grad, own, *others = backward_down(place, *errors[c], w_down, terms, c, halves)
        grads.append(grad)
        grad_own.append(own)
        arrived.append([swap(other, "half", d + 1) for d, other in enumerate(others)])

    grad_in, kinds = [], []
    down_grad = ranges_down(
        place, hidden[1], grads[1], down_codes, down_groups, halves, down_grad
    )
    for c in chunks:
        if c == 1:
            arrived[1] = [tie(part, grad_in[0], down_grad) for part in arrived[1]]
        grad, found = backward_hidden(
            place, grad_own[c], arrived[c], slope[c], act[c], w_in, halves
        )
        grad_in.append(grad)
        kinds.append(found)
    kinds[0] = [tie(part, grad_in[1]) for part in kinds[0]]
    rows = height_of(errors[0][0])
    lower, upper = slice(0, rows // 2), slice(rows // 2, rows)
    keep, go = [
        [[found[2 * d], swap(found[2 * d + 1], "expert", 1)] for d in parts] for found in kinds
    ]
    stay, leave = keep[0], go[0]
    outer = [(d, keep[d]) for d in parts if d]
    crossed = [
        (
            swap(add([part[upper] for part in go[d]]).astype(BF16), "half", d),
            swap(add([part[lower] for part in go[d]]).astype(BF16), "expert", 2),
        )
        for d in parts
        if d
    ]

    def ranges(part, pieces, found, *after):
        held = [tie(grad, *after) for grad in grad_in] if after else grad_in
        return ranges_in(place, x, held, in_codes, in_low.shape[2], part, pieces, found)

    by_half = [pair[0] for pair in crossed]
    across_upper = swap(
        add([part[upper] for part in leave] + by_half).astype(BF16), "expert", 2
    )
    arrived_upper = [
        swap(tie(add([part[upper] for part in keep]).astype(BF16), *by_half), "half", d)
        for d, keep in outer
    ]
    in_grad = ranges(0, 2, None, *by_half)
    near = swap(
        tie(
            add([part[upper] for part in stay] + arrived_upper + [across_upper]).astype(BF16),
            in_grad,
        ),
        "expert",
        4,
    )
    across_lower = swap(
        tie(add([part[lower] for part in leave]).astype(BF16), across_upper), "expert", 2
    )
    arrived_lower = [
        swap(
            tie(
                add([part[lower] for part in keep] + [pair[1]]).astype(BF16), *arrived_upper
            ),
            "half",
            d,
        )
        for (d, keep), pair in zip(outer, crossed)
    ]
    in_grad = ranges(2, 4, in_grad)
    near = tie(near, in_grad)
    grad_tokens = scatter_far(
        [part[lower] for part in stay] + arrived_lower + [across_lower, near]
    )

    in_grad = ranges(3, 4, in_grad)
    return (grad_tokens.astype(BF16), in_grad[None], down_grad[None])


def solution(mesh):
    placed = (
        P("expert", None),
        P("expert", "half"),
        P("expert", None),
        P("expert", None),
        P("expert", None, None, "half"),
        P("expert", None, None, "half"),
        P("expert", None, None, "half"),
        P("expert", None, "half"),
        P("expert", None, "half"),
        P("expert", None, "half"),
    )
    return jax.shard_map(
        local,
        mesh=mesh,
        in_specs=placed,
        out_specs=(
            P("expert", "half"),
            P("expert", None, None, "half"),
            P("expert", None, None, "half"),
        ),
        check_vma=False,
    )
```

```python
import functools

import jax
import jax.numpy as jnp
from jax import lax
from jax.experimental import pallas as pl
from jax.experimental.pallas import tpu as pltpu
from jax.sharding import PartitionSpec as P

BF16 = jnp.bfloat16
F32 = jnp.float32
MIB = 1 << 20


def swap(array, axis, distance):
    size = lax.axis_size(axis)
    return lax.ppermute(array, axis, [(i, i ^ distance) for i in range(size)])


def tie(array, *others):
    return lax.optimization_barrier((array, *others))[0]


def far_distances():
    experts = lax.axis_size("expert")
    distances = []
    distance = experts // 2
    while distance > 4:
        distances.append(distance)
        distance //= 2
    return distances


def join(parts):
    return parts[0] if len(parts) == 1 else jnp.concatenate(parts, axis=0)


def gather_far(block):
    parts = [block]
    for distance in far_distances():
        parts.append(swap(join(parts), "expert", distance))
    return parts


def add(parts):
    total = parts[0].astype(F32)
    for part in parts[1:]:
        total = total + part.astype(F32)
    return total


def scatter_far(terms):
    for distance in reversed(far_distances()):
        half = terms[0].shape[0] // 2
        sent = swap(add([part[half:] for part in terms]).astype(BF16), "expert", distance)
        terms = [part[:half] for part in terms] + [sent]
    return add(terms)


def scatter_rows(near, across, cuts):
    rows = near[0].shape[0] // 2
    upper = [swap(add([part[rows:, cut] for part in across]).astype(BF16), "expert", 2) for cut in cuts]
    sent = [
        swap(add([part[rows:, cut] for part in near] + [part_of]).astype(BF16), "expert", 4)
        for cut, part_of in zip(cuts, upper)
    ]
    lower = swap(tie(add([part[:rows] for part in across]).astype(BF16), *upper), "expert", 2)
    return [
        scatter_far([part[:rows, cut] for part in near] + [lower[:, cut], part_of])
        for cut, part_of in zip(cuts, sent)
    ]


def dot(left, right):
    return jnp.dot(left, right, preferred_element_type=F32)


def dot_cols(left, right):
    return lax.dot_general(left, right, (((1,), (1,)), ((), ())), preferred_element_type=F32)


def dot_rows(left, right):
    return lax.dot_general(left, right, (((0,), (0,)), ((), ())), preferred_element_type=F32)


def cost(flops, bytes_accessed):
    return pl.CostEstimate(flops=int(flops), bytes_accessed=int(bytes_accessed), transcendentals=0)


def moved(step, blocks, place):
    return ((step // blocks) ^ place[1]) * blocks + step % blocks


def call(kernel, grid, ins, outs, place, scratch=(), mib=16, flops=0, reuse=None, weight=1e-6):
    total = sum(a.size * a.dtype.itemsize for a, _, _ in ins)
    for shape, kind, _, _ in outs:
        count = 1
        for extent in shape:
            count *= extent
        total += count * jnp.dtype(kind).itemsize

    def spec(block, index):
        if isinstance(block, tuple):
            return pl.BlockSpec(block, index)
        return pl.BlockSpec(memory_space=block)

    in_specs = [spec(block, index) for _, block, index in ins]
    arrays = [a for a, _, _ in ins]
    if reuse is not None:
        in_specs.append(pl.BlockSpec(memory_space=pl.ANY))
        arrays.append(reuse)
    return pl.pallas_call(
        kernel,
        grid_spec=pltpu.PrefetchScalarGridSpec(
            num_scalar_prefetch=1,
            grid=grid,
            in_specs=in_specs,
            out_specs=[spec(block, index) for _, _, block, index in outs],
            scratch_shapes=list(scratch),
        ),
        out_shape=[jax.ShapeDtypeStruct(shape, kind) for shape, kind, _, _ in outs],
        compiler_params=pltpu.CompilerParams(vmem_limit_bytes=mib * MIB),
        cost_estimate=cost(flops * weight, total * weight),
        input_output_aliases={} if reuse is None else {1 + len(ins): 0},
    )(place, *arrays)


def resident(kernel, ins, outs, place, mib=16, flops=0, scratch=()):
    return call(
        kernel,
        (),
        [(a, pltpu.VMEM, None) for a in ins],
        [(shape, kind, pltpu.VMEM, None) for shape, kind in outs],
        place,
        mib=mib,
        flops=flops,
        scratch=scratch,
    )


def step_of(extent):
    return next(size for size in (512, 256, 128) if extent % size == 0)


def tiles(extent, body):
    size = step_of(extent)
    for start in range(0, extent, size):
        body(start)


def whole2(*_):
    return (0, 0)


def whole3(*_):
    return (0, 0, 0)


def whole4(*_):
    return (0, 0, 0, 0)


def pack(place, parts):
    rows = sum(line[0].shape[0] for line in parts)
    cols = sum(part.shape[1] for part in parts[0])

    def kernel(place_ref, *refs):
        refs, out_ref = list(refs[:-1]), refs[-1]
        row = 0
        for line in parts:
            col = 0
            for part in line:
                height, width = part.shape
                out_ref[row : row + height, col : col + width] = refs.pop(0)[...]
                col += width
            row += line[0].shape[0]

    flat = [part for line in parts for part in line]
    return resident(kernel, flat, [((rows, cols), parts[0][0].dtype)], place)[0]


def dequant(place, codes, low, high, halves=1):
    count, height, cols = codes.shape
    groups = low.shape[1]
    size = height // groups
    held = groups // halves

    def kernel(place_ref, code_ref, low_ref, high_ref, out_ref):
        def block(i, carry):
            base = moved(i, held, place_ref) if halves > 1 else i
            source = pl.multiple_of(base * size, size)
            to = pl.multiple_of(i * size, size)
            for k in range(count):
                bottom = low_ref[k, pl.ds(base, 1), :]
                scale = (high_ref[k, pl.ds(base, 1), :] - bottom) * (1.0 / 255.0)
                vals = code_ref[k, pl.ds(source, size), :].astype(F32)
                out_ref[pl.ds(to, size), k * cols : (k + 1) * cols] = (
                    bottom + scale * vals
                ).astype(BF16)
            return carry

        lax.fori_loop(0, groups, block, 0)

    return resident(
        kernel, [codes, low, high], [((height, count * cols), BF16)], place
    )[0]


def dequant_wide(place, codes, low, high, mib):
    count, height, cols = codes.shape
    groups = low.shape[1]
    size = height // groups
    per = next(p for p in (4, 2, 1) if groups % p == 0)
    steps = groups // per
    rows = per * size

    def kernel(place_ref, code_hbm, low_hbm, high_hbm, out_ref, code_ref, low_ref, high_ref, sems):
        ends = [
            pltpu.make_async_copy(low_hbm, low_ref, sems.at[steps]),
            pltpu.make_async_copy(high_hbm, high_ref, sems.at[steps + 1]),
        ]
        blocks = []
        for i in range(steps):
            held = slice(i * rows, (i + 1) * rows)
            blocks.append(
                pltpu.make_async_copy(code_hbm.at[:, held, :], code_ref.at[:, held, :], sems.at[i])
            )
        for copy in ends + blocks:
            copy.start()
        for copy in ends:
            copy.wait()
        for i in range(steps):
            blocks[i].wait()

            def group(j, carry):
                at = i * per + j
                held = pl.ds(pl.multiple_of(at * size, size), size)
                for k in range(count):
                    bottom = low_ref[k, pl.ds(at, 1), :]
                    scale = (high_ref[k, pl.ds(at, 1), :] - bottom) * (1.0 / 255.0)
                    vals = code_ref[k, held, :].astype(F32)
                    out_ref[held, k * cols : (k + 1) * cols] = (bottom + scale * vals).astype(BF16)
                return carry

            lax.fori_loop(0, per, group, 0)

    return call(
        kernel,
        (),
        [(a, pltpu.HBM, None) for a in (codes, low, high)],
        [((height, count * cols), BF16, pltpu.VMEM, None)],
        place,
        scratch=[
            pltpu.VMEM(codes.shape, BF16),
            pltpu.VMEM(low.shape, F32),
            pltpu.VMEM(high.shape, F32),
            pltpu.SemaphoreType.DMA((steps + 2,)),
        ],
        mib=mib,
    )[0]


def hidden_rows(total_groups, size, halves):
    per = total_groups // halves
    while per > 3:
        per = next(f for f in range(2, per + 1) if per % f == 0) and per // next(
            f for f in range(2, per + 1) if per % f == 0
        )
    return per, per * size


def height_of(parts):
    return sum(part.shape[0] for part in parts)


def stacked(refs):
    return jnp.concatenate([ref[...] for ref in refs], axis=0)


def rows_of(array, start=0, stop=None):
    return (array, start, array.shape[0] if stop is None else stop)


def stacked_rows(refs, pieces):
    return jnp.concatenate(
        [ref[start:stop, :] for ref, (_, start, stop) in zip(refs, pieces)], axis=0
    )


def forward_in(place, x, w_in):
    rows = sum(stop - start for _, start, stop in x)
    width, both = w_in.shape
    hidden = both // 2
    size = step_of(hidden)

    def kernel(place_ref, *refs):
        w_ref, hidden_ref, slope_ref, act_ref = refs[len(x) :]
        left = stacked_rows(refs[: len(x)], x)

        def body(start):
            gate = dot(left, w_ref[:, pl.ds(start, size)])
            up = dot(left, w_ref[:, pl.ds(hidden + start, size)])
            sig = 1.0 / (1.0 + jnp.exp(-gate))
            act = gate * sig
            hidden_ref[:, pl.ds(start, size)] = (act * up).astype(BF16)
            slope_ref[:, pl.ds(start, size)] = up * sig * (1.0 + gate * (1.0 - sig))
            act_ref[:, pl.ds(start, size)] = act

        tiles(hidden, body)

    shape = (rows, hidden)
    return resident(
        kernel,
        [*[array for array, _, _ in x], w_in],
        [(shape, BF16), (shape, F32), (shape, F32)],
        place,
        flops=2 * rows * width * both,
    )


def route_weight(extra, place_ref, experts):
    lane = lax.broadcasted_iota(jnp.int32, extra.shape, 1)
    me = place_ref[0]
    named = (lane == me) | (lane == me + experts) | (lane == me + 2 * experts)
    return jnp.sum(jnp.where(named, extra.astype(F32), 0.0), axis=1, keepdims=True)


def forward_down(place, hidden, w_down, terms, c):
    experts = lax.axis_size("expert")
    rows = hidden[0].shape[0] // 2
    height, quarter = w_down.shape
    size = step_of(quarter)
    held = slice(c * rows, (c + 1) * rows)

    def kernel(place_ref, *refs):
        *hidden_refs, w_ref, own_ref, other_ref, out_own_ref, out_other_ref = refs
        left = jnp.concatenate([ref[...] for ref in hidden_refs], axis=1)
        own = route_weight(own_ref[held, :], place_ref, experts)
        other = route_weight(other_ref[held, :], place_ref, experts)

        def body(start):
            total = dot(left, w_ref[:, pl.ds(start, size)])
            out_own_ref[:, pl.ds(start, size)] = (own * total[:rows]).astype(BF16)
            out_other_ref[:, pl.ds(start, size)] = (other * total[rows:]).astype(BF16)

        tiles(quarter, body)

    return resident(
        kernel,
        [*hidden, w_down, *terms],
        [((rows, quarter), BF16)] * 2,
        place,
        flops=4 * rows * height * quarter,
    )


def backward_down(place, err_own, err_other, w_down, terms, c, halves):
    experts = lax.axis_size("expert")
    rows, quarter = height_of(err_own), err_own[0].shape[1]
    count = len(err_own)
    height = w_down.shape[0]
    own = height // halves
    size = step_of(own)
    held = slice(c * rows, (c + 1) * rows)

    def kernel(place_ref, *refs):
        own_ref, other_ref, w_ref, grad_ref, *outs = refs[2 * count :]
        weight = route_weight(own_ref[held, :], place_ref, experts)
        grad_ref[:rows, :] = (weight * stacked(refs[:count]).astype(F32)).astype(BF16)
        weight = route_weight(other_ref[held, :], place_ref, experts)
        grad_ref[rows:, :] = (weight * stacked(refs[count : 2 * count]).astype(F32)).astype(BF16)
        for d in reversed(range(halves)):

            def body(start):
                at = d * own + start
                part = dot_cols(grad_ref[...], w_ref[pl.ds(at, size), :])
                outs[d][:, pl.ds(start, size)] = part.astype(outs[d].dtype)

            tiles(own, body)

    shape = (2 * rows, own)
    return resident(
        kernel,
        [*err_own, *err_other, *terms, w_down],
        [((2 * rows, quarter), BF16), (shape, F32)] + [(shape, BF16)] * (halves - 1),
        place,
        flops=4 * rows * height * quarter,
    )


def backward_hidden(place, grad_own, arrived, slope, act, w_in, halves):
    both_rows, hidden = slope.shape
    rows = both_rows // 2
    quarter = w_in.shape[0] // halves
    size = step_of(quarter)
    count = len(arrived)

    def kernel(place_ref, grad_own_ref, *refs):
        arrived_refs = refs[:count]
        slope_ref, act_ref, w_ref, grad_ref, *outs = refs[count:]
        grad_hidden = grad_own_ref[...]
        for ref in arrived_refs:
            grad_hidden += ref[...].astype(F32)
        grad_ref[:, :hidden] = (grad_hidden * slope_ref[...]).astype(BF16)
        grad_ref[:, hidden:] = (grad_hidden * act_ref[...]).astype(BF16)
        for d in range(halves):

            def body(start):
                at = pl.multiple_of((place_ref[1] ^ d) * quarter + start, size)
                part = dot_cols(grad_ref[...], w_ref[pl.ds(at, size), :]).astype(BF16)
                outs[2 * d][:, pl.ds(start, size)] = part[:rows]
                outs[2 * d + 1][:, pl.ds(start, size)] = part[rows:]

            tiles(quarter, body)

    grad, *parts = resident(
        kernel,
        [grad_own, *arrived, slope, act, w_in],
        [((both_rows, 2 * hidden), BF16)] + [((rows, quarter), BF16)] * (2 * halves),
        place,
        flops=4 * both_rows * hidden * quarter * halves,
    )
    return grad, parts


def ends(grad, codes):
    upper = jnp.sum(grad * codes.astype(F32), axis=0, keepdims=True) * (1.0 / 255.0)
    return jnp.sum(grad, axis=0, keepdims=True) - upper, upper


def range_tile(left, right, size, step, codes, store):
    turned = left.T
    for start in range(0, right.shape[1], step):
        cols = slice(start, start + step)
        grad = dot(turned, right[:, cols])
        for g in range(turned.shape[0] // size):
            cut = slice(g * size, (g + 1) * size)
            low, high = ends(grad[cut], codes(cut, cols))
            store(g, cols, low, high)


def ranges_down(place, hidden, grad, codes, groups, halves, found=None):
    _, height, quarter = codes.shape
    size = height // groups
    per, rows = hidden_rows(groups, size, halves)
    blocks = height // halves // rows
    earlier = [] if found is None else [found]

    def kernel(place_ref, *refs):
        hidden_refs = refs[:halves]
        grad_ref, code_ref, *found_refs, out_ref = refs[halves:]
        step = pl.program_id(0)
        base = moved(step, blocks, place_ref) * per

        def store(g, cols, low, high):
            for k, value in ((0, low), (1, high)):
                for ref in found_refs:
                    value += ref[k, pl.ds(base + g, 1), cols]
                out_ref[k, pl.ds(base + g, 1), cols] = value

        for d in range(halves):

            @pl.when(step // blocks == d)
            def _():
                range_tile(
                    hidden_refs[d][...],
                    grad_ref,
                    size,
                    256,
                    lambda cut, cols: code_ref[0, cut, cols],
                    store,
                )

    shape = (2, groups, quarter)
    return call(
        kernel,
        (height // rows,),
        [(part, (part.shape[0], rows), lambda i, p: (0, i % blocks)) for part in hidden]
        + [
            (grad, pltpu.VMEM, None),
            (codes, (1, rows, quarter), lambda i, p: (0, moved(i, blocks, p), 0)),
        ]
        + [(array, pltpu.VMEM, None) for array in earlier],
        [(shape, F32, shape, whole3)],
        place,
        mib=20,
        flops=2 * grad.shape[0] * height * quarter,
    )[0]


def ranges_in(place, x, grads, codes, groups, part, parts, found):
    _, _, width, hidden = codes.shape
    size = width // groups
    held = groups // parts
    per = next(p for p in (4, 2, 1) if held % p == 0)
    rows = per * size
    blocks = held // per
    flat = [piece for parts in x for piece in parts]
    chunks = len(grads)
    tokens, both = grads[0].shape
    wide = 256 if hidden % 256 == 0 else hidden

    def kernel(place_ref, *refs):
        x_refs = refs[: len(flat)]
        grad_refs = refs[len(flat) : len(flat) + chunks]
        code_ref, out_ref, right_ref = refs[len(flat) + chunks], refs[-2], refs[-1]
        base = pl.program_id(0) * per

        @pl.when(pl.program_id(0) == 0)
        def _():
            for c in range(chunks):
                right_ref[c * tokens : (c + 1) * tokens, :] = grad_refs[c][...]

        def split(cols):
            k = cols.start // hidden
            return k, slice(cols.start - k * hidden, cols.stop - k * hidden)

        def codes_at(cut, cols):
            k, cols = split(cols)
            return code_ref[0, k, cut, cols]

        def store(g, cols, low, high):
            k, cols = split(cols)
            out_ref[2 * k, pl.ds(base + g, 1), cols] = low
            out_ref[2 * k + 1, pl.ds(base + g, 1), cols] = high

        left = stacked_rows(x_refs, flat)
        range_tile(left, right_ref, size, wide, codes_at, store)

    shape = (4, groups, hidden)
    return call(
        kernel,
        (blocks,),
        [(a, (a.shape[0], rows), lambda i, p: (0, part * blocks + i)) for a, _, _ in flat]
        + [(grad, pltpu.VMEM, None) for grad in grads]
        + [(codes, (1, 2, rows, hidden), lambda i, p: (0, 0, part * blocks + i, 0))],
        [(shape, F32, (4, held, hidden), lambda i, p: (0, part, 0))],
        place,
        scratch=[pltpu.VMEM((chunks * tokens, both), BF16)],
        mib=20,
        flops=2 * sum(grad.size for grad in grads) * (width // parts),
        reuse=found,
    )[0]


def prepare(place, routes, route_scores, extra):
    experts = lax.axis_size("expert")
    rows, top_count = routes.shape

    def kernel(place_ref, route_ref, score_ref, out_ref):
        scores = score_ref[...]
        weights = scores / jnp.sum(scores, axis=1, keepdims=True)
        names = route_ref[...]
        lane = lax.broadcasted_iota(jnp.int32, (rows, extra), 1)
        third = jnp.where(lane < experts, 0, jnp.where(lane < 2 * experts, 1, 2))
        expert = lane - third * experts
        table = jnp.zeros((rows, extra), F32)
        for k in range(top_count):
            table += jnp.where(expert == names[:, k : k + 1], weights[:, k : k + 1], 0.0)
        top = table.astype(BF16).astype(F32)
        middle = (table - top).astype(BF16).astype(F32)
        bottom = table - top - middle
        terms = jnp.where(third == 0, top, jnp.where(third == 1, middle, bottom))
        out_ref[...] = terms.astype(BF16)

    return resident(kernel, [routes, route_scores], [((rows, extra), BF16)], place)[0]


def local(
    tokens, target, routes, route_scores, in_codes, in_low, in_high, down_codes, down_low, down_high
):
    experts = lax.axis_size("expert")
    halves = lax.axis_size("half")
    place = jnp.stack([lax.axis_index("expert"), lax.axis_index("half")]).astype(jnp.int32)
    quarter = target.shape[1]
    parts = range(halves)
    chunks = (0, 1)

    far = join(gather_far(tokens)[1:])
    near_own = swap(tokens, "expert", 4)
    across_own = swap(tokens, "expert", 2)
    extra = -(-3 * experts // 128) * 128
    terms = prepare(place, routes, route_scores, extra)
    w_in = dequant_wide(place, in_codes[0], tie(in_low, terms)[0], in_high[0], 30)
    near_own = tie(near_own, w_in)
    across_near = swap(near_own, "expert", 2)
    far = tie(far, w_in, across_own)
    near_far = swap(far, "expert", 4)
    terms = join(gather_far(terms))
    near_far = tie(near_far, across_near, terms)
    last = pack(place, [[far], [near_far]])
    across_last = swap(last, "expert", 2)
    first = pack(place, [[tokens], [tie(far, terms)], [near_own]])
    near_other = swap(near_far, "expert", 1)
    x = [[rows_of(part) for part in (first, near_far, swap(first, "expert", 1), near_other)]]

    hidden, slope, act = [], [], []
    for c in chunks:
        if c == 1:
            second = pack(place, [[across_own], [tie(across_near, near_other)]])
            second_other = swap(second, "expert", 1)
            across_last = tie(across_last, w_down, second_other, near_terms)
            last_other = swap(across_last, "expert", 1)
            size = tokens.shape[0]
            x.append([])
            for early, late in ((second, across_last), (second_other, last_other)):
                count = late.shape[0] // 2
                x[1] += [
                    rows_of(early, 0, size),
                    rows_of(late, 0, count),
                    rows_of(early, size),
                    rows_of(late, count),
                ]
        own, chunk_slope, chunk_act = forward_in(place, x[c], w_in)
        if c == 0:
            w_down = dequant(place, down_codes, tie(down_low, own), down_high, halves)
            near_terms = swap(tie(terms, w_down), "expert", 4)
        hidden.append([own] + [swap(own, "half", d) for d in parts if d])
        slope.append(chunk_slope)
        act.append(chunk_act)
    terms = jnp.concatenate([terms, tie(near_terms, hidden[1][0])], axis=0)
    terms = jnp.concatenate([terms, swap(terms, "expert", 2)], axis=0)
    terms = (terms, swap(terms, "expert", 1))

    sums = []
    for c in chunks:
        if c == 1:
            hidden[1][1:] = [tie(part, sums[0][0]) for part in hidden[1][1:]]
        out_own, out_other = forward_down(place, hidden[c], w_down, terms, c)
        sums.append([out_own, swap(out_other, "expert", 1)])
    middle = quarter // 2
    cuts = [slice(0, middle), slice(middle, quarter)]
    mixed = scatter_rows(sums[0], sums[1], cuts)
    error = [
        (mixed[f] - target[:, cuts[f]].astype(F32)).astype(BF16) for f in range(len(cuts))
    ]

    kept = pack(place, [list(line) for line in zip(*[gather_far(part) for part in error])])
    near = swap(kept, "expert", 4)
    across_kept = swap(kept, "expert", 2)
    kept_other = swap(kept, "expert", 1)
    near = tie(near, across_kept, kept_other)
    across_near = swap(near, "expert", 2)
    across_other = swap(across_kept, "expert", 1)
    errors = [([kept, near], [kept_other, swap(near, "expert", 1)])]
    grads, grad_own, arrived = [], [], []
    down_groups = down_low.shape[1]
    for c in chunks:
        if c == 1:
            across_near = tie(across_near, grads[0], across_other)
            down_grad = ranges_down(place, hidden[0], grads[0], down_codes, down_groups, halves)
            last_other = tie(swap(across_near, "expert", 1), down_grad, *arrived[0])
            errors.append(([across_kept, across_near], [across_other, last_other]))
        grad, own, *others = backward_down(place, *errors[c], w_down, terms, c, halves)
        grads.append(grad)
        grad_own.append(own)
        arrived.append([swap(other, "half", d + 1) for d, other in enumerate(others)])

    grad_in, kinds = [], []
    down_grad = ranges_down(
        place, hidden[1], grads[1], down_codes, down_groups, halves, down_grad
    )
    for c in chunks:
        if c == 1:
            arrived[1] = [tie(part, grad_in[0], down_grad) for part in arrived[1]]
        grad, found = backward_hidden(
            place, grad_own[c], arrived[c], slope[c], act[c], w_in, halves
        )
        grad_in.append(grad)
        kinds.append(found)
    kinds[0] = [tie(part, grad_in[1]) for part in kinds[0]]
    rows = height_of(errors[0][0])
    lower, upper = slice(0, rows // 2), slice(rows // 2, rows)
    keep, go = [
        [[found[2 * d], swap(found[2 * d + 1], "expert", 1)] for d in parts] for found in kinds
    ]
    stay, leave = keep[0], go[0]
    outer = [(d, keep[d]) for d in parts if d]
    crossed = [
        (
            swap(add([part[upper] for part in go[d]]).astype(BF16), "half", d),
            swap(add([part[lower] for part in go[d]]).astype(BF16), "expert", 2),
        )
        for d in parts
        if d
    ]

    def ranges(part, pieces, found, *after):
        held = [tie(grad, *after) for grad in grad_in] if after else grad_in
        return ranges_in(place, x, held, in_codes, in_low.shape[2], part, pieces, found)

    by_half = [pair[0] for pair in crossed]
    across_upper = swap(
        add([part[upper] for part in leave] + by_half).astype(BF16), "expert", 2
    )
    arrived_upper = [
        swap(tie(add([part[upper] for part in keep]).astype(BF16), *by_half), "half", d)
        for d, keep in outer
    ]
    in_grad = ranges(0, 2, None, *by_half)
    near = swap(
        tie(
            add([part[upper] for part in stay] + arrived_upper + [across_upper]).astype(BF16),
            in_grad,
        ),
        "expert",
        4,
    )
    across_lower = swap(
        tie(add([part[lower] for part in leave]).astype(BF16), across_upper), "expert", 2
    )
    arrived_lower = [
        swap(
            tie(
                add([part[lower] for part in keep] + [pair[1]]).astype(BF16), *arrived_upper
            ),
            "half",
            d,
        )
        for (d, keep), pair in zip(outer, crossed)
    ]
    in_grad = ranges(2, 4, in_grad)
    near = tie(near, in_grad)
    grad_tokens = scatter_far(
        [part[lower] for part in stay] + arrived_lower + [across_lower, near]
    )

    in_grad = ranges(3, 4, in_grad)
    return (grad_tokens.astype(BF16), in_grad[None], down_grad[None])


def solution(mesh):
    placed = (
        P("expert", None),
        P("expert", "half"),
        P("expert", None),
        P("expert", None),
        P("expert", None, None, "half"),
        P("expert", None, None, "half"),
        P("expert", None, None, "half"),
        P("expert", None, "half"),
        P("expert", None, "half"),
        P("expert", None, "half"),
    )
    return jax.shard_map(
        local,
        mesh=mesh,
        in_specs=placed,
        out_specs=(
            P("expert", "half"),
            P("expert", None, None, "half"),
            P("expert", None, None, "half"),
        ),
        check_vma=False,
    )
```

```python
import functools

import jax
import jax.numpy as jnp
from jax import lax
from jax.experimental import pallas as pl
from jax.experimental.pallas import tpu as pltpu
from jax.sharding import PartitionSpec as P

BF16 = jnp.bfloat16
F32 = jnp.float32
MIB = 1 << 20


def swap(array, axis, distance):
    size = lax.axis_size(axis)
    return lax.ppermute(array, axis, [(i, i ^ distance) for i in range(size)])


def tie(array, *others):
    return lax.optimization_barrier((array, *others))[0]


def far_distances():
    experts = lax.axis_size("expert")
    distances = []
    distance = experts // 2
    while distance > 4:
        distances.append(distance)
        distance //= 2
    return distances


def join(parts):
    return parts[0] if len(parts) == 1 else jnp.concatenate(parts, axis=0)


def gather_far(block):
    parts = [block]
    for distance in far_distances():
        parts.append(swap(join(parts), "expert", distance))
    return parts


def add(parts):
    total = parts[0].astype(F32)
    for part in parts[1:]:
        total = total + part.astype(F32)
    return total


def scatter_far(terms):
    for distance in reversed(far_distances()):
        half = terms[0].shape[0] // 2
        sent = swap(add([part[half:] for part in terms]).astype(BF16), "expert", distance)
        terms = [part[:half] for part in terms] + [sent]
    return add(terms)


def scatter_rows(near, across, cuts):
    rows = near[0].shape[0] // 2
    upper = [swap(add([part[rows:, cut] for part in across]).astype(BF16), "expert", 2) for cut in cuts]
    sent = [
        swap(add([part[rows:, cut] for part in near] + [part_of]).astype(BF16), "expert", 4)
        for cut, part_of in zip(cuts, upper)
    ]
    lower = swap(tie(add([part[:rows] for part in across]).astype(BF16), *upper), "expert", 2)
    return [
        scatter_far([part[:rows, cut] for part in near] + [lower[:, cut], part_of])
        for cut, part_of in zip(cuts, sent)
    ]


def dot(left, right):
    return jnp.dot(left, right, preferred_element_type=F32)


def dot_cols(left, right):
    return lax.dot_general(left, right, (((1,), (1,)), ((), ())), preferred_element_type=F32)


def dot_rows(left, right):
    return lax.dot_general(left, right, (((0,), (0,)), ((), ())), preferred_element_type=F32)


def cost(flops, bytes_accessed):
    return pl.CostEstimate(flops=int(flops), bytes_accessed=int(bytes_accessed), transcendentals=0)


def moved(step, blocks, place):
    return ((step // blocks) ^ place[1]) * blocks + step % blocks


def call(kernel, grid, ins, outs, place, scratch=(), mib=16, flops=0, reuse=None, weight=1e-6):
    total = sum(a.size * a.dtype.itemsize for a, _, _ in ins)
    for shape, kind, _, _ in outs:
        count = 1
        for extent in shape:
            count *= extent
        total += count * jnp.dtype(kind).itemsize

    def spec(block, index):
        if isinstance(block, tuple):
            return pl.BlockSpec(block, index)
        return pl.BlockSpec(memory_space=block)

    in_specs = [spec(block, index) for _, block, index in ins]
    arrays = [a for a, _, _ in ins]
    if reuse is not None:
        in_specs.append(pl.BlockSpec(memory_space=pl.ANY))
        arrays.append(reuse)
    return pl.pallas_call(
        kernel,
        grid_spec=pltpu.PrefetchScalarGridSpec(
            num_scalar_prefetch=1,
            grid=grid,
            in_specs=in_specs,
            out_specs=[spec(block, index) for _, _, block, index in outs],
            scratch_shapes=list(scratch),
        ),
        out_shape=[jax.ShapeDtypeStruct(shape, kind) for shape, kind, _, _ in outs],
        compiler_params=pltpu.CompilerParams(vmem_limit_bytes=mib * MIB),
        cost_estimate=cost(flops * weight, total * weight),
        input_output_aliases={} if reuse is None else {1 + len(ins): 0},
    )(place, *arrays)


def resident(kernel, ins, outs, place, mib=16, flops=0, scratch=()):
    return call(
        kernel,
        (),
        [(a, pltpu.VMEM, None) for a in ins],
        [(shape, kind, pltpu.VMEM, None) for shape, kind in outs],
        place,
        mib=mib,
        flops=flops,
        scratch=scratch,
    )


def step_of(extent):
    return next(size for size in (512, 256, 128) if extent % size == 0)


def tiles(extent, body):
    size = step_of(extent)
    for start in range(0, extent, size):
        body(start)


def whole2(*_):
    return (0, 0)


def whole3(*_):
    return (0, 0, 0)


def whole4(*_):
    return (0, 0, 0, 0)


def pack(place, parts):
    rows = sum(line[0].shape[0] for line in parts)
    cols = sum(part.shape[1] for part in parts[0])

    def kernel(place_ref, *refs):
        refs, out_ref = list(refs[:-1]), refs[-1]
        row = 0
        for line in parts:
            col = 0
            for part in line:
                height, width = part.shape
                out_ref[row : row + height, col : col + width] = refs.pop(0)[...]
                col += width
            row += line[0].shape[0]

    flat = [part for line in parts for part in line]
    return resident(kernel, flat, [((rows, cols), parts[0][0].dtype)], place)[0]


def dequant(place, codes, low, high, halves=1):
    count, height, cols = codes.shape
    groups = low.shape[1]
    size = height // groups
    held = groups // halves

    def kernel(place_ref, code_ref, low_ref, high_ref, out_ref):
        def block(i, carry):
            base = moved(i, held, place_ref) if halves > 1 else i
            source = pl.multiple_of(base * size, size)
            to = pl.multiple_of(i * size, size)
            for k in range(count):
                bottom = low_ref[k, pl.ds(base, 1), :]
                scale = (high_ref[k, pl.ds(base, 1), :] - bottom) * (1.0 / 255.0)
                vals = code_ref[k, pl.ds(source, size), :].astype(F32)
                out_ref[pl.ds(to, size), k * cols : (k + 1) * cols] = (
                    bottom + scale * vals
                ).astype(BF16)
            return carry

        lax.fori_loop(0, groups, block, 0)

    return resident(
        kernel, [codes, low, high], [((height, count * cols), BF16)], place
    )[0]


def dequant_wide(place, codes, low, high, mib):
    count, height, cols = codes.shape
    groups = low.shape[1]
    size = height // groups
    per = next(p for p in (4, 2, 1) if groups % p == 0)
    steps = groups // per
    rows = per * size

    def kernel(place_ref, code_hbm, low_hbm, high_hbm, out_ref, code_ref, low_ref, high_ref, sems):
        ends = [
            pltpu.make_async_copy(low_hbm, low_ref, sems.at[steps]),
            pltpu.make_async_copy(high_hbm, high_ref, sems.at[steps + 1]),
        ]
        blocks = []
        for i in range(steps):
            held = slice(i * rows, (i + 1) * rows)
            blocks.append(
                pltpu.make_async_copy(code_hbm.at[:, held, :], code_ref.at[:, held, :], sems.at[i])
            )
        for copy in ends + blocks:
            copy.start()
        for copy in ends:
            copy.wait()
        for i in range(steps):
            blocks[i].wait()

            def group(j, carry):
                at = i * per + j
                held = pl.ds(pl.multiple_of(at * size, size), size)
                for k in range(count):
                    bottom = low_ref[k, pl.ds(at, 1), :]
                    scale = (high_ref[k, pl.ds(at, 1), :] - bottom) * (1.0 / 255.0)
                    vals = code_ref[k, held, :].astype(F32)
                    out_ref[held, k * cols : (k + 1) * cols] = (bottom + scale * vals).astype(BF16)
                return carry

            lax.fori_loop(0, per, group, 0)

    return call(
        kernel,
        (),
        [(a, pltpu.HBM, None) for a in (codes, low, high)],
        [((height, count * cols), BF16, pltpu.VMEM, None)],
        place,
        scratch=[
            pltpu.VMEM(codes.shape, BF16),
            pltpu.VMEM(low.shape, F32),
            pltpu.VMEM(high.shape, F32),
            pltpu.SemaphoreType.DMA((steps + 2,)),
        ],
        mib=mib,
    )[0]


def hidden_rows(total_groups, size, halves):
    per = total_groups // halves
    while per > 3:
        per = next(f for f in range(2, per + 1) if per % f == 0) and per // next(
            f for f in range(2, per + 1) if per % f == 0
        )
    return per, per * size


def height_of(parts):
    return sum(part.shape[0] for part in parts)


def stacked(refs):
    return jnp.concatenate([ref[...] for ref in refs], axis=0)


def rows_of(array, start=0, stop=None):
    return (array, start, array.shape[0] if stop is None else stop)


def stacked_rows(refs, pieces):
    return jnp.concatenate(
        [ref[start:stop, :] for ref, (_, start, stop) in zip(refs, pieces)], axis=0
    )


def forward_in(place, x, w_in):
    rows = sum(stop - start for _, start, stop in x)
    width, both = w_in.shape
    hidden = both // 2
    size = step_of(hidden)

    def kernel(place_ref, *refs):
        w_ref, hidden_ref, slope_ref, act_ref = refs[len(x) :]
        left = stacked_rows(refs[: len(x)], x)

        def body(start):
            gate = dot(left, w_ref[:, pl.ds(start, size)])
            up = dot(left, w_ref[:, pl.ds(hidden + start, size)])
            sig = 1.0 / (1.0 + jnp.exp(-gate))
            act = gate * sig
            hidden_ref[:, pl.ds(start, size)] = (act * up).astype(BF16)
            slope_ref[:, pl.ds(start, size)] = up * sig * (1.0 + gate * (1.0 - sig))
            act_ref[:, pl.ds(start, size)] = act

        tiles(hidden, body)

    shape = (rows, hidden)
    return resident(
        kernel,
        [*[array for array, _, _ in x], w_in],
        [(shape, BF16), (shape, F32), (shape, F32)],
        place,
        flops=2 * rows * width * both,
    )


def route_weight(extra, place_ref, experts):
    lane = lax.broadcasted_iota(jnp.int32, extra.shape, 1)
    me = place_ref[0]
    named = (lane == me) | (lane == me + experts) | (lane == me + 2 * experts)
    return jnp.sum(jnp.where(named, extra.astype(F32), 0.0), axis=1, keepdims=True)


def forward_down(place, hidden, w_down, terms, c):
    experts = lax.axis_size("expert")
    rows = hidden[0].shape[0] // 2
    height, quarter = w_down.shape
    size = step_of(quarter)
    held = slice(c * rows, (c + 1) * rows)

    def kernel(place_ref, *refs):
        *hidden_refs, w_ref, own_ref, other_ref, out_own_ref, out_other_ref = refs
        left = jnp.concatenate([ref[...] for ref in hidden_refs], axis=1)
        own = route_weight(own_ref[held, :], place_ref, experts)
        other = route_weight(other_ref[held, :], place_ref, experts)

        def body(start):
            total = dot(left, w_ref[:, pl.ds(start, size)])
            out_own_ref[:, pl.ds(start, size)] = (own * total[:rows]).astype(BF16)
            out_other_ref[:, pl.ds(start, size)] = (other * total[rows:]).astype(BF16)

        tiles(quarter, body)

    return resident(
        kernel,
        [*hidden, w_down, *terms],
        [((rows, quarter), BF16)] * 2,
        place,
        flops=4 * rows * height * quarter,
    )


def backward_down(place, err_own, err_other, w_down, terms, c, halves):
    experts = lax.axis_size("expert")
    rows, quarter = height_of(err_own), err_own[0].shape[1]
    count = len(err_own)
    height = w_down.shape[0]
    own = height // halves
    size = step_of(own)
    held = slice(c * rows, (c + 1) * rows)

    def kernel(place_ref, *refs):
        own_ref, other_ref, w_ref, grad_ref, *outs = refs[2 * count :]
        weight = route_weight(own_ref[held, :], place_ref, experts)
        grad_ref[:rows, :] = (weight * stacked(refs[:count]).astype(F32)).astype(BF16)
        weight = route_weight(other_ref[held, :], place_ref, experts)
        grad_ref[rows:, :] = (weight * stacked(refs[count : 2 * count]).astype(F32)).astype(BF16)
        for d in reversed(range(halves)):

            def body(start):
                at = d * own + start
                part = dot_cols(grad_ref[...], w_ref[pl.ds(at, size), :])
                outs[d][:, pl.ds(start, size)] = part.astype(outs[d].dtype)

            tiles(own, body)

    shape = (2 * rows, own)
    return resident(
        kernel,
        [*err_own, *err_other, *terms, w_down],
        [((2 * rows, quarter), BF16), (shape, F32)] + [(shape, BF16)] * (halves - 1),
        place,
        flops=4 * rows * height * quarter,
    )


def backward_hidden(place, grad_own, arrived, slope, act, w_in, halves):
    both_rows, hidden = slope.shape
    rows = both_rows // 2
    quarter = w_in.shape[0] // halves
    size = step_of(quarter)
    count = len(arrived)

    def kernel(place_ref, grad_own_ref, *refs):
        arrived_refs = refs[:count]
        slope_ref, act_ref, w_ref, grad_ref, *outs = refs[count:]
        grad_hidden = grad_own_ref[...]
        for ref in arrived_refs:
            grad_hidden += ref[...].astype(F32)
        grad_ref[:, :hidden] = (grad_hidden * slope_ref[...]).astype(BF16)
        grad_ref[:, hidden:] = (grad_hidden * act_ref[...]).astype(BF16)
        for d in range(halves):

            def body(start):
                at = pl.multiple_of((place_ref[1] ^ d) * quarter + start, size)
                part = dot_cols(grad_ref[...], w_ref[pl.ds(at, size), :]).astype(BF16)
                outs[2 * d][:, pl.ds(start, size)] = part[:rows]
                outs[2 * d + 1][:, pl.ds(start, size)] = part[rows:]

            tiles(quarter, body)

    grad, *parts = resident(
        kernel,
        [grad_own, *arrived, slope, act, w_in],
        [((both_rows, 2 * hidden), BF16)] + [((rows, quarter), BF16)] * (2 * halves),
        place,
        flops=4 * both_rows * hidden * quarter * halves,
    )
    return grad, parts


def ends(grad, codes):
    upper = jnp.sum(grad * codes.astype(F32), axis=0, keepdims=True) * (1.0 / 255.0)
    return jnp.sum(grad, axis=0, keepdims=True) - upper, upper


def range_tile(left, right, size, step, codes, store):
    turned = left.T
    for start in range(0, right.shape[1], step):
        cols = slice(start, start + step)
        grad = dot(turned, right[:, cols])
        for g in range(turned.shape[0] // size):
            cut = slice(g * size, (g + 1) * size)
            low, high = ends(grad[cut], codes(cut, cols))
            store(g, cols, low, high)


def ranges_down(place, hidden, grad, codes, groups, halves, found=None):
    _, height, quarter = codes.shape
    size = height // groups
    per, rows = hidden_rows(groups, size, halves)
    blocks = height // halves // rows
    earlier = [] if found is None else [found]

    def kernel(place_ref, *refs):
        hidden_refs = refs[:halves]
        grad_ref, code_ref, *found_refs, out_ref = refs[halves:]
        step = pl.program_id(0)
        base = moved(step, blocks, place_ref) * per

        def store(g, cols, low, high):
            for k, value in ((0, low), (1, high)):
                for ref in found_refs:
                    value += ref[k, pl.ds(base + g, 1), cols]
                out_ref[k, pl.ds(base + g, 1), cols] = value

        for d in range(halves):

            @pl.when(step // blocks == d)
            def _():
                range_tile(
                    hidden_refs[d][...],
                    grad_ref,
                    size,
                    256,
                    lambda cut, cols: code_ref[0, cut, cols],
                    store,
                )

    shape = (2, groups, quarter)
    return call(
        kernel,
        (height // rows,),
        [(part, (part.shape[0], rows), lambda i, p: (0, i % blocks)) for part in hidden]
        + [
            (grad, pltpu.VMEM, None),
            (codes, (1, rows, quarter), lambda i, p: (0, moved(i, blocks, p), 0)),
        ]
        + [(array, pltpu.VMEM, None) for array in earlier],
        [(shape, F32, shape, whole3)],
        place,
        mib=20,
        flops=2 * grad.shape[0] * height * quarter,
    )[0]


def ranges_in(place, x, grads, codes, groups, part, parts, found):
    _, _, width, hidden = codes.shape
    size = width // groups
    held = groups // parts
    per = next(p for p in (4, 2, 1) if held % p == 0)
    rows = per * size
    blocks = held // per
    flat = [piece for parts in x for piece in parts]
    chunks = len(grads)
    tokens, both = grads[0].shape
    wide = 256 if hidden % 256 == 0 else hidden

    def kernel(place_ref, *refs):
        x_refs = refs[: len(flat)]
        grad_refs = refs[len(flat) : len(flat) + chunks]
        code_ref, out_ref, right_ref = refs[len(flat) + chunks], refs[-2], refs[-1]
        base = pl.program_id(0) * per

        @pl.when(pl.program_id(0) == 0)
        def _():
            for c in range(chunks):
                right_ref[c * tokens : (c + 1) * tokens, :] = grad_refs[c][...]

        def split(cols):
            k = cols.start // hidden
            return k, slice(cols.start - k * hidden, cols.stop - k * hidden)

        def codes_at(cut, cols):
            k, cols = split(cols)
            return code_ref[0, k, cut, cols]

        def store(g, cols, low, high):
            k, cols = split(cols)
            out_ref[2 * k, pl.ds(base + g, 1), cols] = low
            out_ref[2 * k + 1, pl.ds(base + g, 1), cols] = high

        left = stacked_rows(x_refs, flat)
        range_tile(left, right_ref, size, wide, codes_at, store)

    shape = (4, groups, hidden)
    return call(
        kernel,
        (blocks,),
        [(a, (a.shape[0], rows), lambda i, p: (0, part * blocks + i)) for a, _, _ in flat]
        + [(grad, pltpu.VMEM, None) for grad in grads]
        + [(codes, (1, 2, rows, hidden), lambda i, p: (0, 0, part * blocks + i, 0))],
        [(shape, F32, (4, held, hidden), lambda i, p: (0, part, 0))],
        place,
        scratch=[pltpu.VMEM((chunks * tokens, both), BF16)],
        mib=20,
        flops=2 * sum(grad.size for grad in grads) * (width // parts),
        reuse=found,
    )[0]


def prepare(place, routes, route_scores, extra):
    experts = lax.axis_size("expert")
    rows, top_count = routes.shape

    def kernel(place_ref, route_ref, score_ref, out_ref):
        scores = score_ref[...]
        weights = scores / jnp.sum(scores, axis=1, keepdims=True)
        names = route_ref[...]
        lane = lax.broadcasted_iota(jnp.int32, (rows, extra), 1)
        third = jnp.where(lane < experts, 0, jnp.where(lane < 2 * experts, 1, 2))
        expert = lane - third * experts
        table = jnp.zeros((rows, extra), F32)
        for k in range(top_count):
            table += jnp.where(expert == names[:, k : k + 1], weights[:, k : k + 1], 0.0)
        top = table.astype(BF16).astype(F32)
        middle = (table - top).astype(BF16).astype(F32)
        bottom = table - top - middle
        terms = jnp.where(third == 0, top, jnp.where(third == 1, middle, bottom))
        out_ref[...] = terms.astype(BF16)

    return resident(kernel, [routes, route_scores], [((rows, extra), BF16)], place)[0]


def local(
    tokens, target, routes, route_scores, in_codes, in_low, in_high, down_codes, down_low, down_high
):
    experts = lax.axis_size("expert")
    halves = lax.axis_size("half")
    place = jnp.stack([lax.axis_index("expert"), lax.axis_index("half")]).astype(jnp.int32)
    quarter = target.shape[1]
    parts = range(halves)
    chunks = (0, 1)

    far = join(gather_far(tokens)[1:])
    near_own = swap(tokens, "expert", 4)
    across_own = swap(tokens, "expert", 2)
    extra = -(-3 * experts // 128) * 128
    terms = prepare(place, routes, route_scores, extra)
    w_in = dequant_wide(place, in_codes[0], tie(in_low, terms)[0], in_high[0], 30)
    near_own = tie(near_own, w_in)
    across_near = swap(near_own, "expert", 2)
    far = tie(far, w_in, across_own)
    near_far = swap(far, "expert", 4)
    terms = join(gather_far(terms))
    near_far = tie(near_far, across_near, terms)
    last = pack(place, [[far], [near_far]])
    across_last = swap(last, "expert", 2)
    first = pack(place, [[tokens], [tie(far, terms)], [near_own]])
    near_other = swap(near_far, "expert", 1)
    x = [[rows_of(part) for part in (first, near_far, swap(first, "expert", 1), near_other)]]

    hidden, slope, act = [], [], []
    for c in chunks:
        if c == 1:
            second = pack(place, [[across_own], [tie(across_near, near_other)]])
            second_other = swap(second, "expert", 1)
            across_last = tie(across_last, w_down, second_other, near_terms)
            last_other = swap(across_last, "expert", 1)
            size = tokens.shape[0]
            x.append([])
            for early, late in ((second, across_last), (second_other, last_other)):
                count = late.shape[0] // 2
                x[1] += [
                    rows_of(early, 0, size),
                    rows_of(late, 0, count),
                    rows_of(early, size),
                    rows_of(late, count),
                ]
        own, chunk_slope, chunk_act = forward_in(place, x[c], w_in)
        if c == 0:
            w_down = dequant(place, down_codes, tie(down_low, own), down_high, halves)
            near_terms = swap(tie(terms, w_down), "expert", 4)
        hidden.append([own] + [swap(own, "half", d) for d in parts if d])
        slope.append(chunk_slope)
        act.append(chunk_act)
    terms = jnp.concatenate([terms, tie(near_terms, hidden[1][0])], axis=0)
    terms = jnp.concatenate([terms, swap(terms, "expert", 2)], axis=0)
    terms = (terms, swap(terms, "expert", 1))

    sums = []
    for c in chunks:
        if c == 1:
            hidden[1][1:] = [tie(part, sums[0][0]) for part in hidden[1][1:]]
        out_own, out_other = forward_down(place, hidden[c], w_down, terms, c)
        sums.append([out_own, swap(out_other, "expert", 1)])
    middle = quarter // 2
    cuts = [slice(0, middle), slice(middle, quarter)]
    mixed = scatter_rows(sums[0], sums[1], cuts)
    error = [
        (mixed[f] - target[:, cuts[f]].astype(F32)).astype(BF16) for f in range(len(cuts))
    ]

    kept = pack(place, [list(line) for line in zip(*[gather_far(part) for part in error])])
    near = swap(kept, "expert", 4)
    across_kept = swap(kept, "expert", 2)
    kept_other = swap(kept, "expert", 1)
    near = tie(near, across_kept, kept_other)
    across_near = swap(near, "expert", 2)
    across_other = swap(across_kept, "expert", 1)
    errors = [([kept, near], [kept_other, swap(near, "expert", 1)])]
    grads, grad_own, arrived = [], [], []
    down_groups = down_low.shape[1]
    for c in chunks:
        if c == 1:
            across_near = tie(across_near, grads[0], across_other)
            down_grad = ranges_down(place, hidden[0], grads[0], down_codes, down_groups, halves)
            last_other = tie(swap(across_near, "expert", 1), down_grad, *arrived[0])
            errors.append(([across_kept, across_near], [across_other, last_other]))
        grad, own, *others = backward_down(place, *errors[c], w_down, terms, c, halves)
        grads.append(grad)
        grad_own.append(own)
        arrived.append([swap(other, "half", d + 1) for d, other in enumerate(others)])

    grad_in, kinds = [], []
    down_grad = ranges_down(
        place, hidden[1], grads[1], down_codes, down_groups, halves, down_grad
    )
    for c in chunks:
        if c == 1:
            arrived[1] = [tie(part, grad_in[0], down_grad) for part in arrived[1]]
        grad, found = backward_hidden(
            place, grad_own[c], arrived[c], slope[c], act[c], w_in, halves
        )
        grad_in.append(grad)
        kinds.append(found)
    kinds[0] = [tie(part, grad_in[1]) for part in kinds[0]]
    rows = height_of(errors[0][0])
    lower, upper = slice(0, rows // 2), slice(rows // 2, rows)
    keep, go = [
        [[found[2 * d], swap(found[2 * d + 1], "expert", 1)] for d in parts] for found in kinds
    ]
    stay, leave = keep[0], go[0]
    outer = [(d, keep[d]) for d in parts if d]
    crossed = [
        (
            swap(add([part[upper] for part in go[d]]).astype(BF16), "half", d),
            swap(add([part[lower] for part in go[d]]).astype(BF16), "expert", 2),
        )
        for d in parts
        if d
    ]

    def ranges(part, pieces, found, *after):
        held = [tie(grad, *after) for grad in grad_in] if after else grad_in
        return ranges_in(place, x, held, in_codes, in_low.shape[2], part, pieces, found)

    by_half = [pair[0] for pair in crossed]
    across_upper = swap(
        tie(
            add([part[upper] for part in leave] + by_half).astype(BF16),
            *[pair[1] for pair in crossed],
        ),
        "expert",
        2,
    )
    arrived_upper = [
        swap(tie(add([part[upper] for part in keep]).astype(BF16), *by_half), "half", d)
        for d, keep in outer
    ]
    in_grad = ranges(0, 2, None, *by_half)
    near = swap(
        tie(
            add([part[upper] for part in stay] + arrived_upper + [across_upper]).astype(BF16),
            in_grad,
        ),
        "expert",
        4,
    )
    across_lower = swap(
        tie(add([part[lower] for part in leave]).astype(BF16), across_upper), "expert", 2
    )
    arrived_lower = [
        swap(
            add([part[lower] for part in keep] + [tie(pair[1], *arrived_upper)]).astype(BF16),
            "half",
            d,
        )
        for (d, keep), pair in zip(outer, crossed)
    ]
    in_grad = ranges(2, 4, in_grad)
    near = tie(near, in_grad)
    grad_tokens = scatter_far(
        [part[lower] for part in stay] + arrived_lower + [across_lower, near]
    )

    in_grad = ranges(3, 4, in_grad)
    return (grad_tokens.astype(BF16), in_grad[None], down_grad[None])


def solution(mesh):
    placed = (
        P("expert", None),
        P("expert", "half"),
        P("expert", None),
        P("expert", None),
        P("expert", None, None, "half"),
        P("expert", None, None, "half"),
        P("expert", None, None, "half"),
        P("expert", None, "half"),
        P("expert", None, "half"),
        P("expert", None, "half"),
    )
    return jax.shard_map(
        local,
        mesh=mesh,
        in_specs=placed,
        out_specs=(
            P("expert", "half"),
            P("expert", None, None, "half"),
            P("expert", None, None, "half"),
        ),
        check_vma=False,
    )
```

```python
import functools

import jax
import jax.numpy as jnp
from jax import lax
from jax.experimental import pallas as pl
from jax.experimental.pallas import tpu as pltpu
from jax.sharding import PartitionSpec as P

BF16 = jnp.bfloat16
F32 = jnp.float32
MIB = 1 << 20


def swap(array, axis, distance):
    size = lax.axis_size(axis)
    return lax.ppermute(array, axis, [(i, i ^ distance) for i in range(size)])


def tie(array, *others):
    return lax.optimization_barrier((array, *others))[0]


def far_distances():
    experts = lax.axis_size("expert")
    distances = []
    distance = experts // 2
    while distance > 4:
        distances.append(distance)
        distance //= 2
    return distances


def join(parts):
    return parts[0] if len(parts) == 1 else jnp.concatenate(parts, axis=0)


def gather_far(block):
    parts = [block]
    for distance in far_distances():
        parts.append(swap(join(parts), "expert", distance))
    return parts


def add(parts):
    total = parts[0].astype(F32)
    for part in parts[1:]:
        total = total + part.astype(F32)
    return total


def scatter_far(terms):
    for distance in reversed(far_distances()):
        half = terms[0].shape[0] // 2
        sent = swap(add([part[half:] for part in terms]).astype(BF16), "expert", distance)
        terms = [part[:half] for part in terms] + [sent]
    return add(terms)


def scatter_rows(near, across, cuts):
    rows = near[0].shape[0] // 2
    upper = [swap(add([part[rows:, cut] for part in across]).astype(BF16), "expert", 2) for cut in cuts]
    sent = [
        swap(add([part[rows:, cut] for part in near] + [part_of]).astype(BF16), "expert", 4)
        for cut, part_of in zip(cuts, upper)
    ]
    lower = swap(tie(add([part[:rows] for part in across]).astype(BF16), *upper), "expert", 2)
    return [
        scatter_far([part[:rows, cut] for part in near] + [lower[:, cut], part_of])
        for cut, part_of in zip(cuts, sent)
    ]


def dot(left, right):
    return jnp.dot(left, right, preferred_element_type=F32)


def dot_cols(left, right):
    return lax.dot_general(left, right, (((1,), (1,)), ((), ())), preferred_element_type=F32)


def dot_rows(left, right):
    return lax.dot_general(left, right, (((0,), (0,)), ((), ())), preferred_element_type=F32)


def cost(flops, bytes_accessed):
    return pl.CostEstimate(flops=int(flops), bytes_accessed=int(bytes_accessed), transcendentals=0)


def moved(step, blocks, place):
    return ((step // blocks) ^ place[1]) * blocks + step % blocks


def call(kernel, grid, ins, outs, place, scratch=(), mib=16, flops=0, reuse=None, weight=1e-6):
    total = sum(a.size * a.dtype.itemsize for a, _, _ in ins)
    for shape, kind, _, _ in outs:
        count = 1
        for extent in shape:
            count *= extent
        total += count * jnp.dtype(kind).itemsize

    def spec(block, index):
        if isinstance(block, tuple):
            return pl.BlockSpec(block, index)
        return pl.BlockSpec(memory_space=block)

    in_specs = [spec(block, index) for _, block, index in ins]
    arrays = [a for a, _, _ in ins]
    if reuse is not None:
        in_specs.append(pl.BlockSpec(memory_space=pl.ANY))
        arrays.append(reuse)
    return pl.pallas_call(
        kernel,
        grid_spec=pltpu.PrefetchScalarGridSpec(
            num_scalar_prefetch=1,
            grid=grid,
            in_specs=in_specs,
            out_specs=[spec(block, index) for _, _, block, index in outs],
            scratch_shapes=list(scratch),
        ),
        out_shape=[jax.ShapeDtypeStruct(shape, kind) for shape, kind, _, _ in outs],
        compiler_params=pltpu.CompilerParams(vmem_limit_bytes=mib * MIB),
        cost_estimate=cost(flops * weight, total * weight),
        input_output_aliases={} if reuse is None else {1 + len(ins): 0},
    )(place, *arrays)


def resident(kernel, ins, outs, place, mib=16, flops=0, scratch=()):
    return call(
        kernel,
        (),
        [(a, pltpu.VMEM, None) for a in ins],
        [(shape, kind, pltpu.VMEM, None) for shape, kind in outs],
        place,
        mib=mib,
        flops=flops,
        scratch=scratch,
    )


def step_of(extent):
    return next(size for size in (512, 256, 128) if extent % size == 0)


def tiles(extent, body):
    size = step_of(extent)
    for start in range(0, extent, size):
        body(start)


def whole2(*_):
    return (0, 0)


def whole3(*_):
    return (0, 0, 0)


def whole4(*_):
    return (0, 0, 0, 0)


def pack(place, parts):
    rows = sum(line[0].shape[0] for line in parts)
    cols = sum(part.shape[1] for part in parts[0])

    def kernel(place_ref, *refs):
        refs, out_ref = list(refs[:-1]), refs[-1]
        row = 0
        for line in parts:
            col = 0
            for part in line:
                height, width = part.shape
                out_ref[row : row + height, col : col + width] = refs.pop(0)[...]
                col += width
            row += line[0].shape[0]

    flat = [part for line in parts for part in line]
    return resident(kernel, flat, [((rows, cols), parts[0][0].dtype)], place)[0]


def dequant(place, codes, low, high, halves=1):
    count, height, cols = codes.shape
    groups = low.shape[1]
    size = height // groups
    held = groups // halves

    def kernel(place_ref, code_ref, low_ref, high_ref, out_ref):
        def block(i, carry):
            base = moved(i, held, place_ref) if halves > 1 else i
            source = pl.multiple_of(base * size, size)
            to = pl.multiple_of(i * size, size)
            for k in range(count):
                bottom = low_ref[k, pl.ds(base, 1), :]
                scale = (high_ref[k, pl.ds(base, 1), :] - bottom) * (1.0 / 255.0)
                vals = code_ref[k, pl.ds(source, size), :].astype(F32)
                out_ref[pl.ds(to, size), k * cols : (k + 1) * cols] = (
                    bottom + scale * vals
                ).astype(BF16)
            return carry

        lax.fori_loop(0, groups, block, 0)

    return resident(
        kernel, [codes, low, high], [((height, count * cols), BF16)], place
    )[0]


def dequant_wide(place, codes, low, high, mib):
    count, height, cols = codes.shape
    groups = low.shape[1]
    size = height // groups
    per = next(p for p in (4, 2, 1) if groups % p == 0)
    steps = groups // per
    rows = per * size

    def kernel(place_ref, code_hbm, low_hbm, high_hbm, out_ref, code_ref, low_ref, high_ref, sems):
        ends = [
            pltpu.make_async_copy(low_hbm, low_ref, sems.at[steps]),
            pltpu.make_async_copy(high_hbm, high_ref, sems.at[steps + 1]),
        ]
        blocks = []
        for i in range(steps):
            held = slice(i * rows, (i + 1) * rows)
            blocks.append(
                pltpu.make_async_copy(code_hbm.at[:, held, :], code_ref.at[:, held, :], sems.at[i])
            )
        for copy in ends + blocks:
            copy.start()
        for copy in ends:
            copy.wait()
        for i in range(steps):
            blocks[i].wait()

            def group(j, carry):
                at = i * per + j
                held = pl.ds(pl.multiple_of(at * size, size), size)
                for k in range(count):
                    bottom = low_ref[k, pl.ds(at, 1), :]
                    scale = (high_ref[k, pl.ds(at, 1), :] - bottom) * (1.0 / 255.0)
                    vals = code_ref[k, held, :].astype(F32)
                    out_ref[held, k * cols : (k + 1) * cols] = (bottom + scale * vals).astype(BF16)
                return carry

            lax.fori_loop(0, per, group, 0)

    return call(
        kernel,
        (),
        [(a, pltpu.HBM, None) for a in (codes, low, high)],
        [((height, count * cols), BF16, pltpu.VMEM, None)],
        place,
        scratch=[
            pltpu.VMEM(codes.shape, BF16),
            pltpu.VMEM(low.shape, F32),
            pltpu.VMEM(high.shape, F32),
            pltpu.SemaphoreType.DMA((steps + 2,)),
        ],
        mib=mib,
    )[0]


def hidden_rows(total_groups, size, halves):
    per = total_groups // halves
    while per > 3:
        per = next(f for f in range(2, per + 1) if per % f == 0) and per // next(
            f for f in range(2, per + 1) if per % f == 0
        )
    return per, per * size


def height_of(parts):
    return sum(part.shape[0] for part in parts)


def stacked(refs):
    return jnp.concatenate([ref[...] for ref in refs], axis=0)


def rows_of(array, start=0, stop=None):
    return (array, start, array.shape[0] if stop is None else stop)


def stacked_rows(refs, pieces):
    return jnp.concatenate(
        [ref[start:stop, :] for ref, (_, start, stop) in zip(refs, pieces)], axis=0
    )


def forward_in(place, x, w_in):
    rows = sum(stop - start for _, start, stop in x)
    width, both = w_in.shape
    hidden = both // 2
    size = step_of(hidden)

    def kernel(place_ref, *refs):
        w_ref, hidden_ref, slope_ref, act_ref = refs[len(x) :]
        left = stacked_rows(refs[: len(x)], x)

        def body(start):
            gate = dot(left, w_ref[:, pl.ds(start, size)])
            up = dot(left, w_ref[:, pl.ds(hidden + start, size)])
            sig = 1.0 / (1.0 + jnp.exp(-gate))
            act = gate * sig
            hidden_ref[:, pl.ds(start, size)] = (act * up).astype(BF16)
            slope_ref[:, pl.ds(start, size)] = up * sig * (1.0 + gate * (1.0 - sig))
            act_ref[:, pl.ds(start, size)] = act

        tiles(hidden, body)

    shape = (rows, hidden)
    return resident(
        kernel,
        [*[array for array, _, _ in x], w_in],
        [(shape, BF16), (shape, F32), (shape, F32)],
        place,
        flops=2 * rows * width * both,
    )


def route_weight(extra, place_ref, experts):
    lane = lax.broadcasted_iota(jnp.int32, extra.shape, 1)
    me = place_ref[0]
    named = (lane == me) | (lane == me + experts) | (lane == me + 2 * experts)
    return jnp.sum(jnp.where(named, extra.astype(F32), 0.0), axis=1, keepdims=True)


def forward_down(place, hidden, w_down, terms, c):
    experts = lax.axis_size("expert")
    rows = hidden[0].shape[0] // 2
    height, quarter = w_down.shape
    size = step_of(quarter)
    held = slice(c * rows, (c + 1) * rows)

    def kernel(place_ref, *refs):
        *hidden_refs, w_ref, own_ref, other_ref, out_own_ref, out_other_ref = refs
        left = jnp.concatenate([ref[...] for ref in hidden_refs], axis=1)
        own = route_weight(own_ref[held, :], place_ref, experts)
        other = route_weight(other_ref[held, :], place_ref, experts)

        def body(start):
            total = dot(left, w_ref[:, pl.ds(start, size)])
            out_own_ref[:, pl.ds(start, size)] = (own * total[:rows]).astype(BF16)
            out_other_ref[:, pl.ds(start, size)] = (other * total[rows:]).astype(BF16)

        tiles(quarter, body)

    return resident(
        kernel,
        [*hidden, w_down, *terms],
        [((rows, quarter), BF16)] * 2,
        place,
        flops=4 * rows * height * quarter,
    )


def backward_down(place, err_own, err_other, w_down, terms, c, halves):
    experts = lax.axis_size("expert")
    rows, quarter = height_of(err_own), err_own[0].shape[1]
    count = len(err_own)
    height = w_down.shape[0]
    own = height // halves
    size = step_of(own)
    held = slice(c * rows, (c + 1) * rows)

    def kernel(place_ref, *refs):
        own_ref, other_ref, w_ref, grad_ref, *outs = refs[2 * count :]
        weight = route_weight(own_ref[held, :], place_ref, experts)
        grad_ref[:rows, :] = (weight * stacked(refs[:count]).astype(F32)).astype(BF16)
        weight = route_weight(other_ref[held, :], place_ref, experts)
        grad_ref[rows:, :] = (weight * stacked(refs[count : 2 * count]).astype(F32)).astype(BF16)
        for d in reversed(range(halves)):

            def body(start):
                at = d * own + start
                part = dot_cols(grad_ref[...], w_ref[pl.ds(at, size), :])
                outs[d][:, pl.ds(start, size)] = part.astype(outs[d].dtype)

            tiles(own, body)

    shape = (2 * rows, own)
    return resident(
        kernel,
        [*err_own, *err_other, *terms, w_down],
        [((2 * rows, quarter), BF16), (shape, F32)] + [(shape, BF16)] * (halves - 1),
        place,
        flops=4 * rows * height * quarter,
    )


def backward_hidden(place, grad_own, arrived, slope, act, w_in, halves):
    both_rows, hidden = slope.shape
    rows = both_rows // 2
    quarter = w_in.shape[0] // halves
    size = step_of(quarter)
    count = len(arrived)

    def kernel(place_ref, grad_own_ref, *refs):
        arrived_refs = refs[:count]
        slope_ref, act_ref, w_ref, grad_ref, *outs = refs[count:]
        grad_hidden = grad_own_ref[...]
        for ref in arrived_refs:
            grad_hidden += ref[...].astype(F32)
        grad_ref[:, :hidden] = (grad_hidden * slope_ref[...]).astype(BF16)
        grad_ref[:, hidden:] = (grad_hidden * act_ref[...]).astype(BF16)
        for d in range(halves):

            def body(start):
                at = pl.multiple_of((place_ref[1] ^ d) * quarter + start, size)
                part = dot_cols(grad_ref[...], w_ref[pl.ds(at, size), :]).astype(BF16)
                outs[2 * d][:, pl.ds(start, size)] = part[:rows]
                outs[2 * d + 1][:, pl.ds(start, size)] = part[rows:]

            tiles(quarter, body)

    grad, *parts = resident(
        kernel,
        [grad_own, *arrived, slope, act, w_in],
        [((both_rows, 2 * hidden), BF16)] + [((rows, quarter), BF16)] * (2 * halves),
        place,
        flops=4 * both_rows * hidden * quarter * halves,
    )
    return grad, parts


def ends(grad, codes):
    upper = jnp.sum(grad * codes.astype(F32), axis=0, keepdims=True) * (1.0 / 255.0)
    return jnp.sum(grad, axis=0, keepdims=True) - upper, upper


def range_tile(left, right, size, step, codes, store):
    turned = left.T
    for start in range(0, right.shape[1], step):
        cols = slice(start, start + step)
        grad = dot(turned, right[:, cols])
        for g in range(turned.shape[0] // size):
            cut = slice(g * size, (g + 1) * size)
            low, high = ends(grad[cut], codes(cut, cols))
            store(g, cols, low, high)


def ranges_down(place, hidden, grad, codes, groups, halves, found=None):
    _, height, quarter = codes.shape
    size = height // groups
    per, rows = hidden_rows(groups, size, halves)
    blocks = height // halves // rows
    earlier = [] if found is None else [found]

    def kernel(place_ref, *refs):
        hidden_refs = refs[:halves]
        grad_ref, code_ref, *found_refs, out_ref = refs[halves:]
        step = pl.program_id(0)
        base = moved(step, blocks, place_ref) * per

        def store(g, cols, low, high):
            for k, value in ((0, low), (1, high)):
                for ref in found_refs:
                    value += ref[k, pl.ds(base + g, 1), cols]
                out_ref[k, pl.ds(base + g, 1), cols] = value

        for d in range(halves):

            @pl.when(step // blocks == d)
            def _():
                range_tile(
                    hidden_refs[d][...],
                    grad_ref,
                    size,
                    256,
                    lambda cut, cols: code_ref[0, cut, cols],
                    store,
                )

    shape = (2, groups, quarter)
    return call(
        kernel,
        (height // rows,),
        [(part, (part.shape[0], rows), lambda i, p: (0, i % blocks)) for part in hidden]
        + [
            (grad, pltpu.VMEM, None),
            (codes, (1, rows, quarter), lambda i, p: (0, moved(i, blocks, p), 0)),
        ]
        + [(array, pltpu.VMEM, None) for array in earlier],
        [(shape, F32, shape, whole3)],
        place,
        mib=20,
        flops=2 * grad.shape[0] * height * quarter,
    )[0]


def ranges_in(place, x, grads, codes, groups, part, parts, found):
    _, _, width, hidden = codes.shape
    size = width // groups
    held = groups // parts
    per = next(p for p in (4, 2, 1) if held % p == 0)
    rows = per * size
    blocks = held // per
    flat = [piece for parts in x for piece in parts]
    chunks = len(grads)
    tokens, both = grads[0].shape
    wide = 256 if hidden % 256 == 0 else hidden

    def kernel(place_ref, *refs):
        x_refs = refs[: len(flat)]
        grad_refs = refs[len(flat) : len(flat) + chunks]
        code_ref, out_ref, right_ref = refs[len(flat) + chunks], refs[-2], refs[-1]
        base = pl.program_id(0) * per

        @pl.when(pl.program_id(0) == 0)
        def _():
            for c in range(chunks):
                right_ref[c * tokens : (c + 1) * tokens, :] = grad_refs[c][...]

        def split(cols):
            k = cols.start // hidden
            return k, slice(cols.start - k * hidden, cols.stop - k * hidden)

        def codes_at(cut, cols):
            k, cols = split(cols)
            return code_ref[0, k, cut, cols]

        def store(g, cols, low, high):
            k, cols = split(cols)
            out_ref[2 * k, pl.ds(base + g, 1), cols] = low
            out_ref[2 * k + 1, pl.ds(base + g, 1), cols] = high

        left = stacked_rows(x_refs, flat)
        range_tile(left, right_ref, size, wide, codes_at, store)

    shape = (4, groups, hidden)
    return call(
        kernel,
        (blocks,),
        [(a, (a.shape[0], rows), lambda i, p: (0, part * blocks + i)) for a, _, _ in flat]
        + [(grad, pltpu.VMEM, None) for grad in grads]
        + [(codes, (1, 2, rows, hidden), lambda i, p: (0, 0, part * blocks + i, 0))],
        [(shape, F32, (4, held, hidden), lambda i, p: (0, part, 0))],
        place,
        scratch=[pltpu.VMEM((chunks * tokens, both), BF16)],
        mib=20,
        flops=2 * sum(grad.size for grad in grads) * (width // parts),
        reuse=found,
    )[0]


def prepare(place, routes, route_scores, extra):
    experts = lax.axis_size("expert")
    rows, top_count = routes.shape

    def kernel(place_ref, route_ref, score_ref, out_ref):
        scores = score_ref[...]
        weights = scores / jnp.sum(scores, axis=1, keepdims=True)
        names = route_ref[...]
        lane = lax.broadcasted_iota(jnp.int32, (rows, extra), 1)
        third = jnp.where(lane < experts, 0, jnp.where(lane < 2 * experts, 1, 2))
        expert = lane - third * experts
        table = jnp.zeros((rows, extra), F32)
        for k in range(top_count):
            table += jnp.where(expert == names[:, k : k + 1], weights[:, k : k + 1], 0.0)
        top = table.astype(BF16).astype(F32)
        middle = (table - top).astype(BF16).astype(F32)
        bottom = table - top - middle
        terms = jnp.where(third == 0, top, jnp.where(third == 1, middle, bottom))
        out_ref[...] = terms.astype(BF16)

    return resident(kernel, [routes, route_scores], [((rows, extra), BF16)], place)[0]


def local(
    tokens, target, routes, route_scores, in_codes, in_low, in_high, down_codes, down_low, down_high
):
    experts = lax.axis_size("expert")
    halves = lax.axis_size("half")
    place = jnp.stack([lax.axis_index("expert"), lax.axis_index("half")]).astype(jnp.int32)
    quarter = target.shape[1]
    parts = range(halves)
    chunks = (0, 1)

    far = join(gather_far(tokens)[1:])
    near_own = swap(tokens, "expert", 4)
    across_own = swap(tokens, "expert", 2)
    extra = -(-3 * experts // 128) * 128
    terms = prepare(place, routes, route_scores, extra)
    w_in = dequant_wide(place, in_codes[0], tie(in_low, terms)[0], in_high[0], 30)
    near_own = tie(near_own, w_in)
    across_near = swap(near_own, "expert", 2)
    far = tie(far, w_in, across_own)
    near_far = swap(far, "expert", 4)
    terms = join(gather_far(terms))
    near_far = tie(near_far, across_near, terms)
    last = pack(place, [[far], [near_far]])
    across_last = swap(last, "expert", 2)
    first = pack(place, [[tokens], [tie(far, terms)], [near_own]])
    near_other = swap(near_far, "expert", 1)
    x = [[rows_of(part) for part in (first, near_far, swap(first, "expert", 1), near_other)]]

    hidden, slope, act = [], [], []
    for c in chunks:
        if c == 1:
            second = pack(place, [[across_own], [tie(across_near, near_other)]])
            second_other = swap(second, "expert", 1)
            across_last = tie(across_last, w_down, second_other, near_terms)
            last_other = swap(across_last, "expert", 1)
            size = tokens.shape[0]
            x.append([])
            for early, late in ((second, across_last), (second_other, last_other)):
                count = late.shape[0] // 2
                x[1] += [
                    rows_of(early, 0, size),
                    rows_of(late, 0, count),
                    rows_of(early, size),
                    rows_of(late, count),
                ]
        own, chunk_slope, chunk_act = forward_in(place, x[c], w_in)
        if c == 0:
            w_down = dequant(place, down_codes, tie(down_low, own), down_high, halves)
            near_terms = swap(tie(terms, w_down), "expert", 4)
        hidden.append([own] + [swap(own, "half", d) for d in parts if d])
        slope.append(chunk_slope)
        act.append(chunk_act)
    terms = jnp.concatenate([terms, tie(near_terms, hidden[1][0])], axis=0)
    terms = jnp.concatenate([terms, swap(terms, "expert", 2)], axis=0)
    terms = (terms, swap(terms, "expert", 1))

    sums = []
    for c in chunks:
        if c == 1:
            hidden[1][1:] = [tie(part, sums[0][0]) for part in hidden[1][1:]]
        out_own, out_other = forward_down(place, hidden[c], w_down, terms, c)
        sums.append([out_own, swap(out_other, "expert", 1)])
    cuts = [slice(0, quarter)]
    mixed = scatter_rows(sums[0], sums[1], cuts)
    error = [
        (mixed[f] - target[:, cuts[f]].astype(F32)).astype(BF16) for f in range(len(cuts))
    ]

    kept = pack(place, [list(line) for line in zip(*[gather_far(part) for part in error])])
    near = swap(kept, "expert", 4)
    across_kept = swap(kept, "expert", 2)
    kept_other = swap(kept, "expert", 1)
    near = tie(near, across_kept, kept_other)
    across_near = swap(near, "expert", 2)
    across_other = swap(across_kept, "expert", 1)
    errors = [([kept, near], [kept_other, swap(near, "expert", 1)])]
    grads, grad_own, arrived = [], [], []
    down_groups = down_low.shape[1]
    for c in chunks:
        if c == 1:
            across_near = tie(across_near, grads[0], across_other)
            down_grad = ranges_down(place, hidden[0], grads[0], down_codes, down_groups, halves)
            last_other = tie(swap(across_near, "expert", 1), down_grad, *arrived[0])
            errors.append(([across_kept, across_near], [across_other, last_other]))
        grad, own, *others = backward_down(place, *errors[c], w_down, terms, c, halves)
        grads.append(grad)
        grad_own.append(own)
        arrived.append([swap(other, "half", d + 1) for d, other in enumerate(others)])

    grad_in, kinds = [], []
    down_grad = ranges_down(
        place, hidden[1], grads[1], down_codes, down_groups, halves, down_grad
    )
    for c in chunks:
        if c == 1:
            arrived[1] = [tie(part, grad_in[0], down_grad) for part in arrived[1]]
        grad, found = backward_hidden(
            place, grad_own[c], arrived[c], slope[c], act[c], w_in, halves
        )
        grad_in.append(grad)
        kinds.append(found)
    kinds[0] = [tie(part, grad_in[1]) for part in kinds[0]]
    rows = height_of(errors[0][0])
    lower, upper = slice(0, rows // 2), slice(rows // 2, rows)
    keep, go = [
        [[found[2 * d], swap(found[2 * d + 1], "expert", 1)] for d in parts] for found in kinds
    ]
    stay, leave = keep[0], go[0]
    outer = [(d, keep[d]) for d in parts if d]
    crossed = [
        (
            swap(add([part[upper] for part in go[d]]).astype(BF16), "half", d),
            swap(add([part[lower] for part in go[d]]).astype(BF16), "expert", 2),
        )
        for d in parts
        if d
    ]

    def ranges(part, pieces, found, *after):
        held = [tie(grad, *after) for grad in grad_in] if after else grad_in
        return ranges_in(place, x, held, in_codes, in_low.shape[2], part, pieces, found)

    by_half = [pair[0] for pair in crossed]
    across_upper = swap(
        tie(
            add([part[upper] for part in leave] + by_half).astype(BF16),
            *[pair[1] for pair in crossed],
        ),
        "expert",
        2,
    )
    arrived_upper = [
        swap(tie(add([part[upper] for part in keep]).astype(BF16), *by_half), "half", d)
        for d, keep in outer
    ]
    in_grad = ranges(0, 2, None, *by_half)
    near = swap(
        tie(
            add([part[upper] for part in stay] + arrived_upper + [across_upper]).astype(BF16),
            in_grad,
        ),
        "expert",
        4,
    )
    across_lower = swap(
        tie(add([part[lower] for part in leave]).astype(BF16), across_upper), "expert", 2
    )
    arrived_lower = [
        swap(
            add([part[lower] for part in keep] + [tie(pair[1], *arrived_upper)]).astype(BF16),
            "half",
            d,
        )
        for (d, keep), pair in zip(outer, crossed)
    ]
    in_grad = ranges(2, 4, in_grad)
    near = tie(near, in_grad)
    grad_tokens = scatter_far(
        [part[lower] for part in stay] + arrived_lower + [across_lower, near]
    )

    in_grad = ranges(3, 4, in_grad)
    return (grad_tokens.astype(BF16), in_grad[None], down_grad[None])


def solution(mesh):
    placed = (
        P("expert", None),
        P("expert", "half"),
        P("expert", None),
        P("expert", None),
        P("expert", None, None, "half"),
        P("expert", None, None, "half"),
        P("expert", None, None, "half"),
        P("expert", None, "half"),
        P("expert", None, "half"),
        P("expert", None, "half"),
    )
    return jax.shard_map(
        local,
        mesh=mesh,
        in_specs=placed,
        out_specs=(
            P("expert", "half"),
            P("expert", None, None, "half"),
            P("expert", None, None, "half"),
        ),
        check_vma=False,
    )
```
